512 devices in a mesh: band: 32 (over y, x, core), slab: 16 (over z).
Axes of the slice: x: 4, y: 4, z: 16, core: 2. Of those that a mesh axis runs over, the one named last changes fastest.
Arguments:
- response: float32 [32, 2048, 256], P('band', 'slab'), may hold values from -70 to 70, as said below
- previous: float32 [32, 2048, 256], P('band', 'slab'), may hold values from -18 to 18, as said below
- earlier_beta: float32 [1], replicated, may hold values from 0.3 to 1
- band_gap: float32 [32], P('band'), may hold values from 0.5 to 2
- occupied: bfloat16 [32, 2048, 256], P('band', 'slab'), may hold values from -1 to 1, as said below
- occupied_real: bfloat16 [32, 2, 128, 16384], P('band', None, 'slab'), may hold values from -13 to 13, as said below
- xc_kernel: float32 [128, 16384], P('slab'), may hold values from -1.5 to -0.3
- stick_map: int32 [2048], replicated, may hold values from 0 to 16383, as said below
Outputs:
- next_vector: float32 [32, 2048, 256], P('band', 'slab')
- margins: float32 [2, 32, 32], P(None, None, 'band')
- coefficients: float32 [2], replicated
The draws below stay inside these ranges and needn't reach their ends.
Inputs may be any that keep to these rules, and one draw needn't show every extreme that they name: response stays within the range. previous stays within the range. occupied stays within the range. occupied_real stays within the range. `stick_map`: distinct grid columns, those of the 2048 smallest in-plane frequencies (the sphere's cross-section, ties broken arbitrarily), in an arbitrary order.
All inputs are finite; a program needn't handle non-finite values.
Results may differ from the reference program's by a relative error of at most 0.00075.
Values may be sent and summed in bfloat16 or wider, within the bound.
No kernel may reach another device: no remote copies, remote signals or barrier semaphores. Data moves between devices by JAX's collectives and lax.ppermute only.
A program may use at most 64 MiB of HBM per device.

```python
import math
import jax
import jax.numpy as jnp
from jax import lax

NG = 128
STK_DEV = 128
STICKS = 2048
NBANDS = 32


def band_ramp(top):
    position = jnp.arange(NBANDS, dtype=jnp.float32) / max(NBANDS - 1, 1)
    return jnp.exp(position * math.log(top))


def occupied_unit(key):
    unit_key = jax.random.fold_in(key, 101)
    return jnp.clip(jax.random.normal(unit_key, (NBANDS, STICKS, 2 * NG)), -5.0, 5.0)


def block_levels(key):
    raw_levels = jnp.exp(jax.random.uniform(key, (NBANDS, STICKS // STK_DEV, 1), minval=-1.2, maxval=0.0))
    return jnp.repeat(raw_levels, STK_DEV, axis=1)


def draw_occupied(key, part):
    unit = occupied_unit(key)
    return (unit * (2.0 * STICKS * NG) ** (-0.5)).astype(jnp.bfloat16)


def draw_response(key, part):
    unit = occupied_unit(key)
    key = jax.random.fold_in(key, 11)
    first_key = jax.random.fold_in(key, 0)
    second_key = jax.random.fold_in(key, 1)
    fourth_key = jax.random.fold_in(key, 3)
    dims_all = (NBANDS, STICKS, 2 * NG)
    stick_scale = jnp.exp(jax.random.uniform(second_key, (1, STICKS, 1), minval=0.0, maxval=math.log(10.0)))
    scaling = 0.1 * band_ramp(10.0)[:, None, None] * stick_scale * block_levels(fourth_key)
    along = 0.2 * band_ramp(10.0)[:, None, None] * unit
    return scaling * jnp.clip(jax.random.normal(first_key, dims_all), -5.0, 5.0) + along


def draw_previous(key, part):
    key = jax.random.fold_in(key, 12)
    first_key = jax.random.fold_in(key, 0)
    second_key = jax.random.fold_in(key, 1)
    fourth_key = jax.random.fold_in(key, 3)
    dims_all = (NBANDS, STICKS, 2 * NG)
    stick_scale = jnp.exp(jax.random.uniform(second_key, (1, STICKS, 1), minval=0.0, maxval=math.log(10.0)))
    scaling = 0.1 * band_ramp(3.0)[:, None, None] * stick_scale * block_levels(fourth_key)
    return scaling * jnp.clip(jax.random.normal(first_key, dims_all), -5.0, 5.0)


def draw_occupied_real(key, part):
    key = jax.random.fold_in(key, 13)
    noise_key, sign_key, level_key = jax.random.split(key, 3)
    dims_all = (NBANDS, 2, NG, NG * NG)
    scaling = (2.0 * NBANDS) ** (-0.25) * band_ramp(3.0)[:, None, None, None]
    signs = jnp.where(jax.random.uniform(sign_key, (NBANDS, 2, 1, 1)) < 0.5, -1.0, 1.0)
    offset = signs * jax.random.uniform(level_key, (NBANDS, 2, 1, 1), minval=0.6, maxval=1.2)
    return (scaling * (jnp.clip(jax.random.normal(noise_key, dims_all), -5.0, 5.0) + offset)).astype(jnp.bfloat16)


def draw_stick_map(key, part):
    key = jax.random.fold_in(key, 14)
    first_key, second_key = jax.random.split(key)
    columns = jnp.arange(NG * NG, dtype=jnp.int32)
    x_freq = columns // NG
    y_freq = columns % NG
    x_freq = jnp.where(x_freq < NG // 2, x_freq, x_freq - NG)
    y_freq = jnp.where(y_freq < NG // 2, y_freq, y_freq - NG)
    distance = x_freq * x_freq + y_freq * y_freq
    ranking = jax.random.permutation(first_key, NG * NG).astype(jnp.int32)
    scores = distance * (NG * NG) + ranking
    chosen = jnp.argsort(scores, stable=True)[:STICKS].astype(jnp.int32)
    return jax.random.permutation(second_key, chosen).astype(jnp.int32)


def shard_levels(rng, shape, cuts, smallest, top_value):
    def one(dim, parts):
        heights = jax.random.uniform(jax.random.fold_in(jax.random.fold_in(rng, 6), dim), (parts,), jnp.float32, smallest / len(cuts), top_value / len(cuts))
        return jnp.repeat(jnp.exp(heights), shape[dim] // parts).reshape((-1,) + (1,) * (len(shape) - dim - 1))

    level = one(*cuts[0])
    for cut in cuts[1:]:
        level = level * one(*cut)
    return level


def setup_inputs(seed: int = 0) -> dict:
    key_of = jax.random.split(jax.random.key(seed), 9)
    return {
        "response": draw_response(jax.random.fold_in(key_of[8], 71), 0),
        "previous": draw_previous(jax.random.fold_in(key_of[8], 71), 0),
        "earlier_beta": jnp.clip(jax.random.uniform(key_of[2], (1,), jnp.float32, 0.3, 1.0), 0.3, 1.0),
        "band_gap": jnp.clip(jnp.exp(math.log(2.0) - 1.3862944 * jax.random.uniform(key_of[3], (NBANDS,), jnp.float32) ** shard_levels(key_of[3], (NBANDS,), ((0, 32),), -0.2, 0.2)), 0.5, 2.0),
        "occupied": draw_occupied(jax.random.fold_in(key_of[8], 71), 0),
        "occupied_real": draw_occupied_real(jax.random.fold_in(key_of[8], 71), 0),
        "xc_kernel": jnp.clip(-1.5 + 1.2 * jax.random.uniform(key_of[6], (NG, NG * NG), jnp.float32) ** shard_levels(key_of[6], (NG, NG * NG), ((0, 16),), -0.2, 0.2), -1.5, -0.3),
        "stick_map": draw_stick_map(jax.random.fold_in(key_of[8], 71), 0),
    }


PRECISE = lax.Precision.HIGHEST

def signed_freq(points):
    indices = jnp.arange(points)
    return jnp.where(indices < points // 2, indices, indices - points).astype(jnp.float32)

def reference(response, previous, earlier_beta, band_gap, occupied, occupied_real, xc_kernel, stick_map):
    norm_root = float(NG) ** 1.5
    zeros_grid = jnp.zeros((NG, NG * NG), jnp.float32)

    def to_field(coefficient):
        real_grid = zeros_grid.at[:, stick_map].set(coefficient[:, :NG].T)
        imag_grid = zeros_grid.at[:, stick_map].set(coefficient[:, NG:].T)
        full_grid = (real_grid + 1j * imag_grid).reshape(NG, NG, NG)
        return jnp.fft.ifftn(full_grid).reshape(NG, NG * NG) * norm_root

    def add_band(running, pieces):
        coefficient, orbital = pieces
        field_values = to_field(coefficient)
        orbital32 = orbital.astype(jnp.float32)
        term = orbital32[0] * jnp.real(field_values) + orbital32[1] * jnp.imag(field_values)
        return (running + 2.0 * term, None)
    density = lax.scan(add_band, zeros_grid, (response, occupied_real))[0]
    frequency = signed_freq(NG)
    wave_sq = frequency[:, None, None] ** 2 + frequency[None, :, None] ** 2 + frequency[None, None, :] ** 2
    kernel = jnp.where(wave_sq > 0.0, (0.2 * NG) ** 2 / (math.pi * jnp.maximum(wave_sq, 1.0)), 0.0)
    spectrum = jnp.fft.fftn(density.reshape(NG, NG, NG))
    hartree = jnp.real(jnp.fft.ifftn(kernel * spectrum)).reshape(NG, NG * NG)
    potential = hartree + xc_kernel * density

    def apply_band(orbital):
        orbital32 = orbital.astype(jnp.float32)
        product = (potential * orbital32[0] + 1j * (potential * orbital32[1])).reshape(NG, NG, NG)
        transformed = jnp.fft.fftn(product).reshape(NG, NG * NG) / norm_root
        columns = transformed[:, stick_map]
        return jnp.concatenate([jnp.real(columns).T, jnp.imag(columns).T], axis=1)
    applied = lax.map(apply_band, occupied_real)
    rounded = lax.optimization_barrier(applied.astype(jnp.bfloat16)).astype(jnp.float32)
    rounded = rounded.reshape(NBANDS, STICKS, 2, NG)
    occ32 = occupied.astype(jnp.float32).reshape(NBANDS, STICKS, 2, NG)
    over_real = jnp.einsum('wscg,vscg->wv', occ32, rounded, precision=PRECISE)
    over_imag = jnp.einsum('wsg,vsg->wv', occ32[:, :, 0], rounded[:, :, 1], precision=PRECISE) - jnp.einsum('wsg,vsg->wv', occ32[:, :, 1], rounded[:, :, 0], precision=PRECISE)
    margins = jnp.stack([over_real, over_imag])
    weights = lax.optimization_barrier(margins.astype(jnp.bfloat16)).astype(jnp.float32)
    removed_real = jnp.einsum('wv,wsg->vsg', weights[0], occ32[:, :, 0], precision=PRECISE) - jnp.einsum('wv,wsg->vsg', weights[1], occ32[:, :, 1], precision=PRECISE)
    removed_imag = jnp.einsum('wv,wsg->vsg', weights[1], occ32[:, :, 0], precision=PRECISE) + jnp.einsum('wv,wsg->vsg', weights[0], occ32[:, :, 1], precision=PRECISE)
    removed = jnp.concatenate([removed_real, removed_imag], axis=2)
    pushed = band_gap[:, None, None] * response + applied - removed
    alpha_coef = jnp.sum(response * pushed) / jnp.sum(response * response)
    residual = pushed - alpha_coef * response - earlier_beta[0] * previous
    entries = 2.0 * NBANDS * STICKS * NG
    beta_coef = jnp.sqrt(jnp.sum(residual * residual) / entries + 1e-06)
    next_vector = residual / beta_coef
    return (next_vector, margins, jnp.stack([alpha_coef, beta_coef]))
```

```python
import math

import jax
import jax.numpy as jnp
import ml_dtypes
import numpy as np
from jax import lax
from jax.experimental import pallas as pl
from jax.experimental.pallas import tpu as pltpu
from jax.sharding import PartitionSpec as P

F32 = jnp.float32
BF16 = jnp.bfloat16
VMEM_LIMIT = 48 * 1024 * 1024

N = 128
SLABS = 16
PL = N // SLABS
BANDS = 32
AX = N // BANDS
STK = 128
STICKS = SLABS * STK
HALF = 64
NORM = float(N) ** -1.5


def pieces(table):
    high = table.astype(np.float32).astype(ml_dtypes.bfloat16)
    low = (table - high.astype(np.float64)).astype(np.float32).astype(ml_dtypes.bfloat16)
    return np.stack([high, low])


def angle(a, b):
    return 2.0 * np.pi * ((np.asarray(a)[:, None] * np.asarray(b)[None, :]) % N) / N


def tables():
    every = np.arange(N)
    short = np.arange(HALF)
    signed = np.where(short < HALF // 2, short, short - HALF)
    signed_x = signed.reshape(16, 4).T.reshape(-1)

    c, s = np.cos(angle(every, every)), np.sin(angle(every, every))
    by_slab = lambda m: m.reshape(SLABS, 1, PL, -1)
    z_inverse = np.concatenate(
        [
            np.concatenate([by_slab(c), by_slab(-s)], axis=3),
            np.concatenate([by_slab(s), by_slab(c)], axis=3),
        ],
        axis=1,
    ).reshape(2 * N, 2 * N)
    z_forward = np.concatenate(
        [
            np.concatenate([by_slab(c), by_slab(-s)], axis=3),
            np.concatenate([by_slab(s), by_slab(c)], axis=3),
        ],
        axis=1,
    ).reshape(2 * N, 2 * N)

    cy, sy = np.cos(angle(signed, every)), np.sin(angle(signed, every))
    y_inverse = np.zeros((4, HALF, 4, 2, N))
    for j in range(4):
        y_inverse[j, :, j, 0] = cy
        y_inverse[j, :, j, 1] = sy
    y_inverse = y_inverse.reshape(4 * HALF, 4 * 2 * N)
    y_forward = np.zeros((4, 2, N, 2, 4, HALF))
    for j in range(4):
        y_forward[j, 0, :, 0, j] = cy.T
        y_forward[j, 1, :, 0, j] = sy.T
        y_forward[j, 1, :, 1, j] = cy.T
        y_forward[j, 0, :, 1, j] = -sy.T
    y_forward = y_forward.reshape(4 * 2 * N, 2 * 4 * HALF)

    cx, sx = np.cos(angle(every, signed_x)), np.sin(angle(every, signed_x))
    x_inverse = 2.0 * NORM * np.block([[cx, -sx], [sx, cx]])
    x_forward = NORM * np.concatenate([cx.T, sx.T], axis=0)

    modes = np.zeros((N, N))
    modes[0] = 1.0 / math.sqrt(N)
    modes[1:64] = math.sqrt(2.0 / N) * np.cos(angle(np.arange(1, 64), every))
    modes[64] = np.cos(np.pi * every) / math.sqrt(N)
    modes[65:] = math.sqrt(2.0 / N) * np.sin(angle(np.arange(1, 64), every))
    return {
        "z_inverse": pieces(z_inverse),
        "z_forward": pieces(z_forward),
        "y_inverse": pieces(y_inverse),
        "y_forward": pieces(y_forward),
        "x_inverse": pieces(x_inverse),
        "x_forward": pieces(x_forward),
        "modes": pieces(modes),
        "modes_t": pieces(modes.T),
        "modes_t32": modes.T.astype(np.float32),
    }


TABLES = tables()


def split(value):
    high = value.astype(BF16)
    return high, (value - high.astype(F32)).astype(BF16)


def dot(a, b, contract=((1,), (0,))):
    return lax.dot_general(a, b, (contract, ((), ())), preferred_element_type=F32)


def dot3(a, b, contract=((1,), (0,))):
    return dot(a[0], b[0], contract) + (dot(a[1], b[0], contract) + dot(a[0], b[1], contract))


def call(body, out, *args, scratch=(), in_smem=()):
    specs = [
        pl.BlockSpec(memory_space=pltpu.SMEM if i in in_smem else pltpu.VMEM)
        for i in range(len(args))
    ]
    many = isinstance(out, (list, tuple))
    out_specs = [pl.BlockSpec(memory_space=pltpu.VMEM)] * len(out) if many else pl.BlockSpec(memory_space=pltpu.VMEM)
    return pl.pallas_call(
        body,
        out_shape=out,
        in_specs=specs,
        out_specs=out_specs,
        scratch_shapes=list(scratch),
        compiler_params=pltpu.CompilerParams(vmem_limit_bytes=VMEM_LIMIT),
    )(*args)


def shape(*dims, dtype=F32):
    return jax.ShapeDtypeStruct(dims, dtype)


def sticks_to_z(resp, table, out):
    out[...] = dot3((table[0], table[1]), split(resp[...]), ((1,), (1,))).reshape(SLABS, 2 * PL, STK)


def planes_to_modes(
    recv, q_mask, place, y_table, x_table, occ, modes, modes_t, out, r_high, r_low, d_high, d_low
):
    grid = jnp.zeros((256, 256), F32)
    for src in range(SLABS):
        lanes = slice(src * STK, (src + 1) * STK)
        high, low = split(recv[src])
        mask = q_mask[:, lanes]
        rows = [
            (part.astype(F32)[:, None, :] * mask[None]).reshape(256, STK).astype(BF16)
            for part in (high, low)
        ]
        chosen = place[lanes, :]
        grid += dot(jnp.concatenate(rows, axis=1), jnp.concatenate([chosen, chosen], axis=0))
    grid = split(grid)
    for j in range(4):
        cols = slice(j * 2 * N, (j + 1) * 2 * N)
        mixed = dot3(grid, (y_table[0, :, cols], y_table[1, :, cols]))
        real = mixed[:N, :N] - mixed[N:, N:]
        imag = mixed[:N, N:] + mixed[N:, :N]
        for c, part in enumerate((real, imag)):
            high, low = split(part)
            at = slice(c * HALF + j * 16, c * HALF + (j + 1) * 16)
            for p in range(PL):
                r_high[at, p * N : (p + 1) * N] = high[p * 16 : (p + 1) * 16]
                r_low[at, p * N : (p + 1) * N] = low[p * 16 : (p + 1) * 16]
    for p in range(PL):
        lanes = slice(p * N, (p + 1) * N)
        field = dot3((x_table[0], x_table[1]), (r_high[:, lanes], r_low[:, lanes]))
        density = occ[0, p].astype(F32) * field[:N] + occ[1, p].astype(F32) * field[N:]
        half = dot3(split(density), (modes_t[0], modes_t[1]))
        d_high[:, lanes], d_low[:, lanes] = split(half)
    for p in range(PL):
        lanes = slice(p * N, (p + 1) * N)
        out[pl.ds(p, N, stride=PL), :] = dot3(
            (modes[0], modes[1]), (d_high[:, lanes], d_low[:, lanes])
        )


def sum_bands(recv, to_slabs, to_bands):
    total = recv[0]
    for b in range(1, BANDS):
        total = total + recv[b]
    for i in range(SLABS):
        to_slabs[i] = total
    for i in range(BANDS):
        to_bands[i] = total


def solve_z(where, recv, modes, modes_t32, out):
    columns = [
        jnp.concatenate([recv[i, a * PL : (a + 1) * PL, :] for i in range(SLABS)], axis=0)
        for a in range(AX)
    ]
    spectrum = dot3((modes[0], modes[1]), split(jnp.concatenate(columns, axis=1)))
    freq = lambda i: jnp.where(i <= N // 2, i, i - N // 2)
    fz = freq(lax.broadcasted_iota(jnp.int32, (N, N), 0))
    fy = freq(lax.broadcasted_iota(jnp.int32, (N, N), 1))
    plane_sq = fz * fz + fy * fy
    weighted = []
    for a in range(AX):
        fx = freq(where[0] * AX + a)
        square = (plane_sq + fx * fx).astype(F32)
        kernel = jnp.where(
            square > 0.0, (0.2 * N) ** 2 / (math.pi * jnp.maximum(square, 1.0)), 0.0
        )
        weighted.append(spectrum[:, a * N : (a + 1) * N] * kernel)
    own = modes_t32[pl.ds(pl.multiple_of(where[1] * PL, PL), PL), :]
    result = dot3(split(own), split(jnp.concatenate(weighted, axis=1)))
    tile = jnp.concatenate([result[:, a * N : (a + 1) * N] for a in range(AX)], axis=0)
    for i in range(BANDS):
        out[i] = tile


def from_modes(recv, modes, modes_t, p):
    spectrum = recv[pl.ds(p, N, stride=PL), :]
    half = dot3((modes_t[0], modes_t[1]), split(spectrum))
    return dot3(split(half), (modes[0], modes[1]))


def density_part(recv, modes, modes_t, xc, out):
    for p in range(PL):
        out[p] = xc[p] * from_modes(recv, modes, modes_t, p)


def planes_to_sticks(
    recv, xc_part, occ, q_mask, pick, modes, modes_t, x_table, y_table, out, l_high, l_low, grid
):
    for p in range(PL):
        potential = from_modes(recv, modes, modes_t, p) + xc_part[p]
        product = jnp.concatenate(
            [potential * occ[0, p].astype(F32), potential * occ[1, p].astype(F32)], axis=1
        )
        mixed = dot3((x_table[0], x_table[1]), split(product))
        real = mixed[:HALF, :N] + mixed[HALF:, N:]
        imag = mixed[:HALF, N:] - mixed[HALF:, :N]
        for c, part in enumerate((real, imag)):
            high, low = split(part)
            for j in range(4):
                at = slice(j * 2 * N + c * N, j * 2 * N + (c + 1) * N)
                l_high[p * 16 : (p + 1) * 16, at] = high[j * 16 : (j + 1) * 16]
                l_low[p * 16 : (p + 1) * 16, at] = low[j * 16 : (j + 1) * 16]
    spectrum = dot3((l_high[...], l_low[...]), (y_table[0], y_table[1]))
    for part in range(2):
        for h in range(2):
            lanes = slice(part * 2 * N + h * N, part * 2 * N + (h + 1) * N)
            grid[h, part * N : (part + 1) * N, :] = spectrum[:, lanes]
    high, low = split(
        jnp.concatenate(
            [
                jnp.concatenate([grid[h, pl.ds(q, 16, stride=16), :] for h in range(2)], axis=1)
                for q in range(16)
            ],
            axis=0,
        )
    )
    for dst in range(SLABS):
        lanes = slice(dst * STK, (dst + 1) * STK)
        chosen = dot(high, pick[:, lanes]) + dot(low, pick[:, lanes])
        total = chosen[:16] * q_mask[0:1, lanes]
        for q in range(1, 16):
            total = total + chosen[q * 16 : (q + 1) * 16] * q_mask[q : q + 1, lanes]
        out[dst] = total


def apply_and_overlap(recv, table, occ_all, applied_out, part_out, sums):
    values = recv[...].reshape(2 * N, STK).T
    applied = dot3(split(values), (table[0], table[1]))
    applied_out[...] = applied
    rounded = applied.astype(BF16).astype(F32)
    turned = jnp.concatenate([rounded[:, N:], -rounded[:, :N]], axis=1)
    for w in range(BANDS):
        orbital = occ_all[w].astype(F32)
        for c, probe in enumerate((rounded, turned)):
            line = jnp.sum(orbital * probe, axis=0, keepdims=True)
            sums[c * BANDS + w : c * BANDS + w + 1, :] = line[:, :N] + line[:, N:]
    sums[2 * BANDS :, :] = jnp.zeros((N - 2 * BANDS, N), F32)
    row = jnp.sum(sums[...].T, axis=0, keepdims=True)
    for i in range(SLABS):
        part_out[i] = row


def total_sum(value):
    return jnp.sum(jnp.sum(value, axis=0, keepdims=True), axis=1, keepdims=True)


def lanes_of(values):
    lane = lax.broadcasted_iota(jnp.int32, (1, N), 1)
    row = jnp.zeros((1, N), F32)
    for i, value in enumerate(values):
        row = jnp.where(lane == i, value, row)
    return row


def push(recv, scalars, resp, prev, applied, occ_all, rest_out, margin_out, part_out):
    margin = recv[0]
    for i in range(1, SLABS):
        margin = margin + recv[i]
    margin_out[...] = margin
    weights = margin.astype(BF16).astype(F32)
    plain = jnp.zeros((STK, 2 * N), F32)
    turned = jnp.zeros((STK, 2 * N), F32)
    for w in range(BANDS):
        orbital = occ_all[w].astype(F32)
        plain = plain + weights[:, w : w + 1] * orbital
        turned = turned + weights[:, BANDS + w : BANDS + w + 1] * orbital
    removed = plain + jnp.concatenate([-turned[:, N:], turned[:, :N]], axis=1)
    response = resp[...]
    pushed = scalars[0] * response + applied[...] - removed
    rest = pushed - scalars[1] * prev[...]
    rest_out[...] = rest
    norm = total_sum(response * response)
    along = total_sum(response * pushed)
    slope = total_sum(response * rest) / jnp.where(norm > 0.0, norm, 1.0)
    left = rest - slope * response
    row = lanes_of([norm, along, slope, total_sum(left * left)])
    for i in range(SLABS):
        part_out[i] = row


def merge(recv, count):
    rows = jnp.concatenate([recv[i] for i in range(count)], axis=0)
    norms, alongs, slopes, least = (rows[:, i : i + 1] for i in range(4))
    add = lambda v: jnp.sum(v, axis=0, keepdims=True)
    norm = add(norms)
    slope = add(norms * slopes) / jnp.where(norm > 0.0, norm, 1.0)
    spread = slopes - slope
    return norm, add(alongs), slope, add(least + norms * spread * spread)


def merge_slabs(recv, part_out):
    row = lanes_of(merge(recv, SLABS))
    for i in range(BANDS):
        part_out[i] = row


def finish(recv, resp, rest, next_out, coef_out):
    norm, along, slope, least = merge(recv, BANDS)
    alpha = along / norm
    gap = slope - alpha
    resid_sq = least + norm * gap * gap
    beta = jnp.sqrt(resid_sq / float(2 * BANDS * STICKS * N) + 1e-06)
    next_out[...] = (rest[...] - alpha * resp[...]) / beta
    coef_out[...] = lanes_of([alpha, beta])


def swap(value, axis):
    return lax.all_to_all(value, axis, 0, 0, tiled=True)


def per_device(
    response, previous, earlier_beta, band_gap, occupied, occupied_real, xc_kernel, stick_map
):
    t = {name: jnp.asarray(value) for name, value in TABLES.items()}
    where = jnp.stack([lax.axis_index("band"), lax.axis_index("slab")]).astype(jnp.int32)
    resp = response.reshape(STK, 2 * N)
    prev = previous.reshape(STK, 2 * N)
    occ_all = lax.all_gather(occupied.reshape(1, STK, 2 * N), "band", axis=0, tiled=True)

    occ_planes = occupied_real.reshape(2, PL, N, N)
    xc_planes = xc_kernel.reshape(PL, N, N)
    gx = stick_map // N % HALF
    gy = stick_map % HALF
    q_mask = (gx[None, :] // 4 == jnp.arange(16, dtype=jnp.int32)[:, None]).astype(F32)
    column = gx % 4 * HALF + gy
    cells = jnp.arange(256, dtype=jnp.int32)
    pick = (column[None, :] == cells[:, None]).astype(BF16)
    place = (column[:, None] == cells[None, :]).astype(BF16)

    field = call(sticks_to_z, shape(SLABS, 2 * PL, STK), resp, t["z_inverse"])
    field = swap(field, "slab")
    bf_scratch = lambda *dims: pltpu.VMEM(dims, BF16)
    partial = call(
        planes_to_modes,
        shape(N * PL, N),
        field, q_mask, place, t["y_inverse"], t["x_inverse"], occ_planes, t["modes"], t["modes_t"],
        scratch=[bf_scratch(N, PL * N) for _ in range(4)],
    )
    partial = swap(partial.reshape(BANDS, AX * PL, N), "band")
    to_slabs, to_bands = call(
        sum_bands, [shape(SLABS, AX * PL, N), shape(BANDS, AX * PL, N)], partial
    )
    columns = swap(to_slabs, "slab")
    density = swap(to_bands, "band")
    xc_part = call(
        density_part, shape(PL, N, N), density.reshape(N * PL, N), t["modes"], t["modes_t"], xc_planes
    )
    hartree = call(
        solve_z, shape(BANDS, AX * PL, N), where, columns, t["modes"], t["modes_t32"], in_smem=(0,)
    )
    hartree = swap(hartree, "band")
    chosen = call(
        planes_to_sticks,
        shape(SLABS, 2 * PL, STK),
        hartree.reshape(N * PL, N), xc_part, occ_planes, q_mask, pick,
        t["modes"], t["modes_t"], t["x_forward"], t["y_forward"],
        scratch=[bf_scratch(N, 8 * N), bf_scratch(N, 8 * N), pltpu.VMEM((2, 2 * N, N), F32)],
    )
    gathered = swap(chosen, "slab")
    applied, overlaps = call(
        apply_and_overlap,
        [shape(STK, 2 * N), shape(SLABS, 1, N)],
        gathered, t["z_forward"], occ_all,
        scratch=[pltpu.VMEM((N, N), F32)],
    )
    overlaps = swap(overlaps, "slab")
    scalars = jnp.stack([band_gap[0], earlier_beta[0]])
    rest, margin, sums = call(
        push,
        [shape(STK, 2 * N), shape(1, N), shape(SLABS, 1, N)],
        overlaps, scalars, resp, prev, applied, occ_all,
        in_smem=(1,),
    )
    sums = swap(sums, "slab")
    sums = swap(call(merge_slabs, shape(BANDS, 1, N), sums), "band")
    next_vector, coefficients = call(
        finish, [shape(STK, 2 * N), shape(1, N)], sums, resp, rest
    )
    return (
        next_vector.reshape(1, STK, 2 * N),
        margin[0, : 2 * BANDS].reshape(2, BANDS, 1),
        coefficients[0, :2],
    )


def solution(mesh):
    placed = (
        P("band", "slab", None),
        P("band", "slab", None),
        P(),
        P("band"),
        P("band", "slab", None),
        P("band", None, "slab", None),
        P("slab", None),
        P(),
    )
    return jax.shard_map(
        per_device,
        mesh=mesh,
        in_specs=placed,
        out_specs=(P("band", "slab", None), P(None, None, "band"), P()),
        check_vma=False,
    )
```

```python
import math

import jax
import jax.numpy as jnp
import ml_dtypes
import numpy as np
from jax import lax
from jax.experimental import pallas as pl
from jax.experimental.pallas import tpu as pltpu
from jax.sharding import PartitionSpec as P

F32 = jnp.float32
BF16 = jnp.bfloat16
MIB = 1024 * 1024

N = 128
SLABS = 16
PL = N // SLABS
BANDS = 32
AX = N // BANDS
STK = 128
STICKS = SLABS * STK
HALF = 64
NORM = float(N) ** -1.5


def pieces(table):
    high = table.astype(np.float32).astype(ml_dtypes.bfloat16)
    low = (table - high.astype(np.float64)).astype(np.float32).astype(ml_dtypes.bfloat16)
    return np.stack([high, low])


def angle(a, b):
    return 2.0 * np.pi * ((np.asarray(a)[:, None] * np.asarray(b)[None, :]) % N) / N


def tables():
    every = np.arange(N)
    short = np.arange(HALF)
    signed = np.where(short < HALF // 2, short, short - HALF)
    signed_x = signed.reshape(16, 4).T.reshape(-1)

    c, s = np.cos(angle(every, every)), np.sin(angle(every, every))
    by_slab = lambda m: m.reshape(SLABS, 1, PL, -1)
    z_inverse = np.concatenate(
        [
            np.concatenate([by_slab(c), by_slab(-s)], axis=3),
            np.concatenate([by_slab(s), by_slab(c)], axis=3),
        ],
        axis=1,
    ).reshape(2 * N, 2 * N)
    z_forward = np.concatenate(
        [
            np.concatenate([by_slab(c), by_slab(-s)], axis=3),
            np.concatenate([by_slab(s), by_slab(c)], axis=3),
        ],
        axis=1,
    ).reshape(2 * N, 2 * N)

    cy, sy = np.cos(angle(signed, every)), np.sin(angle(signed, every))
    y_inverse = np.tile(np.concatenate([cy, sy], axis=1), (4, 1))
    y_forward = np.block(
        [[np.tile(cy.T, (1, 4)), np.tile(-sy.T, (1, 4))], [np.tile(sy.T, (1, 4)), np.tile(cy.T, (1, 4))]]
    )

    cx, sx = np.cos(angle(every, signed_x)), np.sin(angle(every, signed_x))
    x_inverse = 2.0 * NORM * np.block([[cx, -sx], [sx, cx]])
    x_forward = NORM * np.concatenate([cx.T, sx.T], axis=0)

    modes = np.zeros((N, N))
    modes[0] = 1.0 / math.sqrt(N)
    modes[1:64] = math.sqrt(2.0 / N) * np.cos(angle(np.arange(1, 64), every))
    modes[64] = np.cos(np.pi * every) / math.sqrt(N)
    modes[65:] = math.sqrt(2.0 / N) * np.sin(angle(np.arange(1, 64), every))
    return {
        "z_inverse": pieces(z_inverse),
        "z_forward": pieces(z_forward),
        "y_inverse": pieces(y_inverse),
        "y_forward": pieces(y_forward),
        "x_inverse": pieces(x_inverse),
        "x_forward": pieces(x_forward),
        "modes": pieces(modes),
        "modes_t": pieces(modes.T),
        "modes_t32": modes.T.astype(np.float32),
    }


TABLES = tables()


def split(value):
    high = value.astype(BF16)
    return high, (value - high.astype(F32)).astype(BF16)


def dot(a, b, contract=((1,), (0,))):
    return lax.dot_general(a, b, (contract, ((), ())), preferred_element_type=F32)


def dot3(a, b, contract=((1,), (0,))):
    return dot(a[0], b[0], contract) + (dot(a[1], b[0], contract) + dot(a[0], b[1], contract))


def call(body, out, *args, scratch=(), in_smem=(), in_hbm=(), vmem=16):
    space = lambda i: pltpu.SMEM if i in in_smem else pltpu.HBM if i in in_hbm else pltpu.VMEM
    in_vmem = pl.BlockSpec(memory_space=pltpu.VMEM)
    many = isinstance(out, (list, tuple))
    return pl.pallas_call(
        body,
        out_shape=out,
        in_specs=[pl.BlockSpec(memory_space=space(i)) for i in range(len(args))],
        out_specs=[in_vmem] * len(out) if many else in_vmem,
        scratch_shapes=[
            *(pltpu.VMEM(args[i].shape, args[i].dtype) for i in in_hbm),
            *([pltpu.SemaphoreType.DMA((max(len(in_hbm), BANDS // CHUNK),))] if in_hbm else []),
            *scratch,
        ],
        compiler_params=pltpu.CompilerParams(vmem_limit_bytes=vmem * MIB),
    )(*args)


def fetch(sources, targets, sems):
    copies = [pltpu.make_async_copy(s, t, sems.at[i]) for i, (s, t) in enumerate(zip(sources, targets))]
    for copy in copies:
        copy.start()
    return copies


def shape(*dims, dtype=F32):
    return jax.ShapeDtypeStruct(dims, dtype)


def sticks_to_z(resp_hbm, table_hbm, out, resp, table, sems):
    for copy in fetch((resp_hbm, table_hbm), (resp, table), sems):
        copy.wait()
    out[...] = dot3((table[0], table[1]), split(resp[...]), ((1,), (1,))).reshape(SLABS, 2 * PL, STK)


def q_mask_of(cells, lanes):
    q = lax.broadcasted_iota(jnp.int32, (16, 1), 0)
    return (cells[:, lanes] // 256 == q).astype(F32)


def pick_of(cells, lanes):
    column = lax.broadcasted_iota(jnp.int32, (256, 1), 0)
    return jnp.where(cells[:, lanes] % 256 == column, 1.0, 0.0).astype(BF16)


def planes_to_modes(
    recv, cells, y_hbm, x_hbm, occ_hbm, modes_hbm, modes_t_hbm,
    out, y_table, x_table, occ, modes, modes_t, sems, r_high, r_low, d_high, d_low
):
    copies = fetch(
        (y_hbm, x_hbm, occ_hbm, modes_hbm, modes_t_hbm), (y_table, x_table, occ, modes, modes_t), sems
    )
    grid = jnp.zeros((256, 256), F32)
    for src in range(SLABS):
        lanes = slice(src * STK, (src + 1) * STK)
        high, low = split(recv[src])
        mask = q_mask_of(cells, lanes)
        rows = [
            (part.astype(F32)[:, None, :] * mask[None]).reshape(256, STK).astype(BF16)
            for part in (high, low)
        ]
        chosen = pick_of(cells, lanes)
        grid += dot(
            jnp.concatenate(rows, axis=1), jnp.concatenate([chosen, chosen], axis=1), ((1,), (1,))
        )
    grid = split(grid)
    for copy in copies:
        copy.wait()
    lane_j = lax.broadcasted_iota(jnp.int32, (1, 256), 1) // HALF
    for j in range(4):
        own = (lane_j == j).astype(BF16)
        mixed = dot3((grid[0] * own, grid[1] * own), (y_table[0], y_table[1]))
        real = mixed[:N, :N] - mixed[N:, N:]
        imag = mixed[:N, N:] + mixed[N:, :N]
        for c, part in enumerate((real, imag)):
            high, low = split(part)
            at = slice(c * HALF + j * 16, c * HALF + (j + 1) * 16)
            for p in range(PL):
                r_high[at, p * N : (p + 1) * N] = high[p * 16 : (p + 1) * 16]
                r_low[at, p * N : (p + 1) * N] = low[p * 16 : (p + 1) * 16]
    for p in range(PL):
        lanes = slice(p * N, (p + 1) * N)
        field = dot3((x_table[0], x_table[1]), (r_high[:, lanes], r_low[:, lanes]))
        density = occ[0, p].astype(F32) * field[:N] + occ[1, p].astype(F32) * field[N:]
        half = dot3(split(density), (modes_t[0], modes_t[1]))
        d_high[:, lanes], d_low[:, lanes] = split(half)
    for p in range(PL):
        lanes = slice(p * N, (p + 1) * N)
        out[pl.ds(p, N, stride=PL), :] = dot3(
            (modes[0], modes[1]), (d_high[:, lanes], d_low[:, lanes])
        )


def sum_bands(recv, to_slabs):
    total = recv[0]
    for b in range(1, BANDS):
        total = total + recv[b]
    for i in range(SLABS):
        to_slabs[i] = total


def solve_z(where, recv, modes, modes_t32, out):
    columns = [
        jnp.concatenate([recv[i, a * PL : (a + 1) * PL, :] for i in range(SLABS)], axis=0)
        for a in range(AX)
    ]
    spectrum = dot3((modes[0], modes[1]), split(jnp.concatenate(columns, axis=1)))
    freq = lambda i: jnp.where(i <= N // 2, i, i - N // 2)
    fz = freq(lax.broadcasted_iota(jnp.int32, (N, N), 0))
    fy = freq(lax.broadcasted_iota(jnp.int32, (N, N), 1))
    plane_sq = fz * fz + fy * fy
    weighted = []
    for a in range(AX):
        fx = freq(where[0] * AX + a)
        square = (plane_sq + fx * fx).astype(F32)
        kernel = jnp.where(
            square > 0.0, (0.2 * N) ** 2 / (math.pi * jnp.maximum(square, 1.0)), 0.0
        )
        weighted.append(spectrum[:, a * N : (a + 1) * N] * kernel)
    own = modes_t32[pl.ds(pl.multiple_of(where[1] * PL, PL), PL), :]
    result = dot3(split(own), split(jnp.concatenate(weighted, axis=1)))
    density = recv[where[1]]
    tile = []
    for a in range(AX):
        tile += [result[:, a * N : (a + 1) * N], density[a * PL : (a + 1) * PL]]
    tile = jnp.concatenate(tile, axis=0)
    for i in range(BANDS):
        out[i] = tile


def planes_from_modes(recv, modes, modes_t, p):
    spectrum = jnp.concatenate(
        [recv[pl.ds(i * PL + p, N, stride=2 * PL), :] for i in range(2)], axis=1
    )
    half = dot3((modes_t[0], modes_t[1]), split(spectrum))
    half = jnp.concatenate([half[:, :N], half[:, N:]], axis=0)
    plane = dot3(split(half), (modes[0], modes[1]))
    return plane[:N], plane[N:]


def planes_to_sticks(
    recv, cells, modes_hbm, modes_t_hbm, xc_hbm, occ_hbm, x_hbm, y_hbm,
    out, modes, modes_t, xc, occ, x_table, y_table, sems, l_high, l_low, grid
):
    copies = fetch(
        (modes_hbm, modes_t_hbm, xc_hbm, occ_hbm, x_hbm, y_hbm),
        (modes, modes_t, xc, occ, x_table, y_table),
        sems,
    )
    for copy in copies:
        copy.wait()
    for p in range(PL):
        hartree, density = planes_from_modes(recv, modes, modes_t, p)
        potential = hartree + xc[p] * density
        product = jnp.concatenate(
            [potential * occ[0, p].astype(F32), potential * occ[1, p].astype(F32)], axis=1
        )
        mixed = dot3((x_table[0], x_table[1]), split(product))
        real = mixed[:HALF, :N] + mixed[HALF:, N:]
        imag = mixed[:HALF, N:] - mixed[HALF:, :N]
        for c, part in enumerate((real, imag)):
            high, low = split(part)
            for j in range(4):
                at = slice(j * 2 * N + c * N, j * 2 * N + (c + 1) * N)
                l_high[p * 16 : (p + 1) * 16, at] = high[j * 16 : (j + 1) * 16]
                l_low[p * 16 : (p + 1) * 16, at] = low[j * 16 : (j + 1) * 16]
    lane_j = lax.broadcasted_iota(jnp.int32, (1, 512), 1) // HALF % 4
    spectrum = jnp.zeros((N, 512), F32)
    for j in range(4):
        at = slice(j * 2 * N, (j + 1) * 2 * N)
        mixed = dot3((l_high[:, at], l_low[:, at]), (y_table[0], y_table[1]))
        spectrum = jnp.where(lane_j == j, mixed, spectrum)
    for part in range(2):
        for h in range(2):
            lanes = slice(part * 2 * N + h * N, part * 2 * N + (h + 1) * N)
            grid[h, part * N : (part + 1) * N, :] = spectrum[:, lanes]
    high, low = split(
        jnp.concatenate(
            [
                jnp.concatenate([grid[h, pl.ds(q, 16, stride=16), :] for h in range(2)], axis=1)
                for q in range(16)
            ],
            axis=0,
        )
    )
    for dst in range(SLABS):
        lanes = slice(dst * STK, (dst + 1) * STK)
        pick = pick_of(cells, lanes)
        mask = q_mask_of(cells, lanes)
        chosen = dot(high, pick) + dot(low, pick)
        total = chosen[:16] * mask[:1]
        for q in range(1, 16):
            total = total + chosen[q * 16 : (q + 1) * 16] * mask[q : q + 1]
        out[dst] = total


CHUNK = 8


def orbitals(hbm, held, sems):
    copies = [
        pltpu.make_async_copy(
            hbm.at[pl.ds(i * CHUNK, CHUNK)], held.at[pl.ds(i * CHUNK, CHUNK)], sems.at[i]
        )
        for i in range(BANDS // CHUNK)
    ]
    for copy in copies:
        copy.start()

    def at(w):
        if w % CHUNK == 0:
            copies[w // CHUNK].wait()
        return held[w].astype(F32)

    return at


def overlap_rows(at, probes, sums):
    pairs = [
        (x, jnp.concatenate([x[:, N:], -x[:, :N]], axis=1)) for x in probes
    ]
    for w in range(BANDS):
        orbital = at(w)
        for i, pair in enumerate(pairs):
            for c, probe in enumerate(pair):
                line = jnp.sum(orbital * probe, axis=0, keepdims=True)
                k = c * BANDS + w
                sums[i, k : k + 1, :] = line[:, :N] + line[:, N:]
    rows = []
    for i in range(len(probes)):
        sums[i, 2 * BANDS :, :] = jnp.zeros((N - 2 * BANDS, N), F32)
        rows.append(jnp.sum(sums[i].T, axis=0, keepdims=True))
    return rows


def total_sum(value):
    return jnp.sum(jnp.sum(value, axis=0, keepdims=True), axis=1, keepdims=True)


def lane():
    return lax.broadcasted_iota(jnp.int32, (1, N), 1)


def with_lanes(row, first, values):
    for i, value in enumerate(values):
        row = jnp.where(lane() == first + i, value, row)
    return row


def lower(row):
    return jnp.where(lane() < 2 * BANDS, row, 0.0)


def fixed_overlaps(occ_all, resp, prev, occ, out, held, sems, sums):
    at = orbitals(occ_all, held, sems)
    rows = overlap_rows(at, [resp[...], prev[...], occ[...].astype(F32)], sums)
    for i, row in enumerate(rows):
        out[i : i + 1, :] = row
    out[3:, :] = jnp.zeros((5, N), F32)


def apply_and_overlap(
    recv, table, scalars, resp, prev, fixed, occ_all, applied_out, part_out, held, sems, sums
):
    at = orbitals(occ_all, held, sems)
    values = recv[...].reshape(2 * N, STK).T
    applied = dot3(split(values), (table[0], table[1]))
    applied_out[...] = applied
    margin, along = overlap_rows(at, [applied.astype(BF16).astype(F32), applied], sums)
    response = resp[...]
    first = scalars[0] * response + applied
    rest = first - scalars[1] * prev[...]
    norm = total_sum(response * response)
    slope = total_sum(response * rest) / jnp.where(norm > 0.0, norm, 1.0)
    left = rest - slope * response
    with_resp, with_prev, with_occ = fixed[0:1, :], fixed[1:2, :], fixed[2:3, :]
    along = along + (scalars[0] - slope) * with_resp - scalars[1] * with_prev
    row = jnp.concatenate(
        [
            margin + pltpu.roll(with_occ, 2 * BANDS, 1),
            along,
            with_lanes(
                with_resp,
                2 * BANDS,
                [norm, total_sum(response * first), slope, total_sum(left * left)],
            ),
        ],
        axis=1,
    )
    for i in range(SLABS):
        part_out[i] = row


def join_slabs(recv, margin_out, part_out):
    rows = [jnp.concatenate([recv[i][:, j * N : (j + 1) * N] for i in range(SLABS)], axis=0) for j in range(3)]
    add = lambda v: jnp.sum(v, axis=0, keepdims=True)
    norms, firsts, slopes, lefts = (rows[2][:, 2 * BANDS + i : 2 * BANDS + i + 1] for i in range(4))
    norm = add(norms)
    slope = add(norms * slopes) / jnp.where(norm > 0.0, norm, 1.0)
    spread_ = slopes - slope
    left = add(lefts + norms * spread_ * spread_)
    head = add(rows[0])
    weights = lower(head.astype(BF16).astype(F32))
    with_left = add(rows[1] + spread_ * rows[2])
    with_resp = add(rows[2])
    inner = lambda x: jnp.sum(weights * lower(x), axis=1, keepdims=True)
    removed_resp = inner(with_resp)
    margin_out[...] = head
    row = jnp.concatenate(
        [
            jnp.where(lane() < 2 * BANDS, weights, head),
            with_lanes(
                jnp.zeros((1, N), F32),
                0,
                [norm, add(firsts) - removed_resp, slope, removed_resp, left - 2.0 * inner(with_left)],
            ),
        ],
        axis=1,
    )
    for i in range(BANDS):
        part_out[i] = row


def remove(margin, scalars, resp, prev, applied, occ_all, rest_out, held, sems):
    at = orbitals(occ_all, held, sems)
    weights = margin[...].astype(BF16).astype(F32)
    plain = jnp.zeros((STK, 2 * N), F32)
    turned = jnp.zeros((STK, 2 * N), F32)
    for w in range(BANDS):
        orbital = at(w)
        plain = plain + weights[:, w : w + 1] * orbital
        turned = turned + weights[:, BANDS + w : BANDS + w + 1] * orbital
    removed = plain + jnp.concatenate([-turned[:, N:], turned[:, :N]], axis=1)
    rest_out[...] = scalars[0] * resp[...] + applied[...] - removed - scalars[1] * prev[...]


def finish(recv, resp, rest, next_out, coef_out):
    rows = [jnp.concatenate([recv[i][:, j * N : (j + 1) * N] for i in range(BANDS)], axis=0) for j in range(2)]
    norms, alongs, slopes, removed_resp, lefts = (rows[1][:, i : i + 1] for i in range(5))
    add = lambda v: jnp.sum(v, axis=0, keepdims=True)
    real, imag, same, cross = (rows[0][:, i * BANDS : (i + 1) * BANDS] for i in range(4))
    times = lambda a, b: lax.dot_general(
        a, b, (((1,), (1,)), ((), ())), precision=lax.Precision.HIGHEST, preferred_element_type=F32
    )
    square = total_sum(real * (times(real, same) + 2.0 * times(imag, cross)) + imag * times(imag, same))
    alpha = add(alongs) / add(norms)
    gap = slopes - alpha
    resid_sq = add(lefts + gap * (gap * norms - 2.0 * removed_resp)) + square
    beta = jnp.sqrt(jnp.maximum(resid_sq, 0.0) / float(2 * BANDS * STICKS * N) + 1e-06)
    next_out[...] = (rest[...] - alpha * resp[...]) / beta
    coef_out[...] = with_lanes(jnp.zeros((1, N), F32), 0, [alpha, beta])


def swap(value, axis):
    return lax.all_to_all(value, axis, 0, 0, tiled=True)


def after(value, other):
    return lax.optimization_barrier((value, other))


def per_device(
    response, previous, earlier_beta, band_gap, occupied, occupied_real, xc_kernel, stick_map
):
    t = {name: jnp.asarray(value) for name, value in TABLES.items()}
    where = jnp.stack([lax.axis_index("band"), lax.axis_index("slab")]).astype(jnp.int32)
    resp = response.reshape(STK, 2 * N)
    prev = previous.reshape(STK, 2 * N)

    occ_planes = occupied_real.reshape(2, PL, N, N)
    field = call(sticks_to_z, shape(SLABS, 2 * PL, STK), resp, t["z_inverse"], in_hbm=(0, 1), vmem=60)
    stick_map, _ = after(stick_map, field)
    gx = stick_map // N % HALF
    cells = (gx // 4 * 256 + gx % 4 * HALF + stick_map % HALF).reshape(1, STICKS)
    occ_all = lax.all_gather(occupied.reshape(1, STK, 2 * N), "band", axis=0, tiled=True)
    field = swap(field, "slab")
    bf_scratch = lambda *dims: pltpu.VMEM(dims, BF16)
    partial = call(
        planes_to_modes,
        shape(N * PL, N),
        field, cells, t["y_inverse"], t["x_inverse"], occ_planes, t["modes"], t["modes_t"],
        in_hbm=(2, 3, 4, 5, 6),
        scratch=[bf_scratch(N, PL * N) for _ in range(4)],
    )
    partial = swap(partial.reshape(BANDS, AX * PL, N), "band")
    total = call(sum_bands, shape(SLABS, AX * PL, N), partial)
    columns = swap(total, "slab")
    hartree = call(
        solve_z, shape(BANDS, 2 * AX * PL, N), where, columns, t["modes"], t["modes_t32"], in_smem=(0,)
    )
    xc_planes, _ = after(xc_kernel, hartree)
    xc_planes = xc_planes.reshape(PL, N, N)
    hartree = swap(hartree, "band")
    chosen = call(
        planes_to_sticks,
        shape(SLABS, 2 * PL, STK),
        hartree.reshape(2 * N * PL, N), cells,
        t["modes"], t["modes_t"], xc_planes, occ_planes, t["x_forward"], t["y_forward"],
        in_hbm=(2, 3, 4, 5, 6, 7),
        scratch=[bf_scratch(N, 8 * N), bf_scratch(N, 8 * N), pltpu.VMEM((2, 2 * N, N), F32)],
    )
    gathered = swap(chosen, "slab")
    fixed = call(
        fixed_overlaps,
        shape(8, N),
        occ_all, resp, prev, occupied.reshape(STK, 2 * N),
        in_hbm=(0,),
        scratch=[pltpu.VMEM((3, N, N), F32)],
    )
    scalars = jnp.stack([band_gap[0], earlier_beta[0]])
    applied, parts = call(
        apply_and_overlap,
        [shape(STK, 2 * N), shape(SLABS, 1, 3 * N)],
        gathered, t["z_forward"], scalars, resp, prev, fixed, occ_all,
        in_smem=(2,),
        in_hbm=(6,),
        scratch=[pltpu.VMEM((2, N, N), F32)],
    )
    margin, parts = call(
        join_slabs, [shape(1, N), shape(BANDS, 1, 2 * N)], swap(parts, "slab")
    )
    rest = call(
        remove,
        shape(STK, 2 * N),
        margin, scalars, resp, prev, applied, occ_all,
        in_smem=(1,),
        in_hbm=(5,),
    )
    next_vector, coefficients = call(
        finish, [shape(STK, 2 * N), shape(1, N)], swap(parts, "band"), resp, rest
    )
    return (
        next_vector.reshape(1, STK, 2 * N),
        margin[0, : 2 * BANDS].reshape(2, BANDS, 1),
        coefficients[0, :2],
    )


def solution(mesh):
    placed = (
        P("band", "slab", None),
        P("band", "slab", None),
        P(),
        P("band"),
        P("band", "slab", None),
        P("band", None, "slab", None),
        P("slab", None),
        P(),
    )
    return jax.shard_map(
        per_device,
        mesh=mesh,
        in_specs=placed,
        out_specs=(P("band", "slab", None), P(None, None, "band"), P()),
        check_vma=False,
    )
```

```python
import math

import jax
import jax.numpy as jnp
import ml_dtypes
import numpy as np
from jax import lax
from jax.experimental import pallas as pl
from jax.experimental.pallas import tpu as pltpu
from jax.sharding import PartitionSpec as P

F32 = jnp.float32
BF16 = jnp.bfloat16
MIB = 1024 * 1024

N = 128
SLABS = 16
PL = N // SLABS
BANDS = 32
AX = N // BANDS
STK = 128
STICKS = SLABS * STK
HALF = 64
NORM = float(N) ** -1.5


def pieces(table):
    high = table.astype(np.float32).astype(ml_dtypes.bfloat16)
    low = (table - high.astype(np.float64)).astype(np.float32).astype(ml_dtypes.bfloat16)
    return np.stack([high, low])


def left(table):
    high, low = pieces(table)
    return np.concatenate([np.concatenate([high, high], 1), np.concatenate([low, np.zeros_like(low)], 1)], 0)


def right(table):
    return left(table.T).T.copy()


def angle(a, b):
    return 2.0 * np.pi * ((np.asarray(a)[:, None] * np.asarray(b)[None, :]) % N) / N


def tables():
    every = np.arange(N)
    short = np.arange(HALF)
    signed = np.where(short < HALF // 2, short, short - HALF)
    signed_x = signed.reshape(16, 4).T.reshape(-1)

    c, s = np.cos(angle(every, every)), np.sin(angle(every, every))
    by_slab = lambda m: m.reshape(SLABS, 1, PL, -1)
    z_inverse = np.concatenate(
        [
            np.concatenate([by_slab(c), by_slab(-s)], axis=3),
            np.concatenate([by_slab(s), by_slab(c)], axis=3),
        ],
        axis=1,
    ).reshape(2 * N, 2 * N)
    z_forward = np.concatenate(
        [
            np.concatenate([by_slab(c), by_slab(-s)], axis=3),
            np.concatenate([by_slab(s), by_slab(c)], axis=3),
        ],
        axis=1,
    ).reshape(2 * N, 2 * N)

    cy, sy = np.cos(angle(signed, every)), np.sin(angle(signed, every))
    high, low = pieces(np.concatenate([cy, sy], axis=1))
    y_inverse = np.concatenate([high, high, low, np.zeros_like(low)], axis=0)
    y_forward = np.concatenate(pieces(np.block([[cy.T, -sy.T], [sy.T, cy.T]])), axis=1)

    cx, sx = np.cos(angle(every, signed_x)), np.sin(angle(every, signed_x))
    x_inverse = 2.0 * NORM * np.block([[cx, -sx], [sx, cx]])
    x_forward = NORM * np.concatenate([cx.T, sx.T], axis=0)

    modes = np.zeros((N, N))
    modes[0] = 1.0 / math.sqrt(N)
    modes[1:64] = math.sqrt(2.0 / N) * np.cos(angle(np.arange(1, 64), every))
    modes[64] = np.cos(np.pi * every) / math.sqrt(N)
    modes[65:] = math.sqrt(2.0 / N) * np.sin(angle(np.arange(1, 64), every))
    return {
        "z_inverse": pieces(z_inverse),
        "z_forward": pieces(z_forward),
        "y_inverse": y_inverse,
        "y_forward": y_forward,
        "x_inverse": left(x_inverse),
        "x_forward": left(x_forward),
        "modes_left": left(modes),
        "modes_right": right(modes),
        "modes_t_left": left(modes.T),
        "modes_t_right": right(modes.T),
        "modes_t32": modes.T.astype(np.float32),
    }


TABLES = tables()


def split(value):
    high = value.astype(BF16)
    return high, (value - high.astype(F32)).astype(BF16)


def dot(a, b, contract=((1,), (0,))):
    return lax.dot_general(a, b, (contract, ((), ())), preferred_element_type=F32)


def dot3(a, b, contract=((1,), (0,))):
    return dot(a[0], b[0], contract) + (dot(a[1], b[0], contract) + dot(a[0], b[1], contract))


def both(value, axis):
    return jnp.concatenate(split(value), axis=axis)


def times_left(table, value):
    out = dot(table[...], both(value, 0) if value.dtype == F32 else value)
    half = out.shape[0] // 2
    return out[:half] + out[half:]


def times_right(value, table):
    out = dot(both(value, 1), table[...])
    return out[:, :N] + out[:, N:]


def call(body, out, *args, scratch=(), in_smem=(), in_hbm=(), vmem=16, late=()):
    space = lambda i: pltpu.SMEM if i in in_smem else pltpu.HBM if i in in_hbm else pltpu.VMEM
    in_vmem = pl.BlockSpec(memory_space=pltpu.VMEM)
    many = isinstance(out, (list, tuple))
    n = len(args)
    inner = (lambda *refs: body(*refs[:n], *refs[n + len(late) :])) if late else body
    return pl.pallas_call(
        inner,
        out_shape=out,
        in_specs=[
            *(pl.BlockSpec(memory_space=space(i)) for i in range(len(args))),
            *(pl.BlockSpec(memory_space=pltpu.HBM) for _ in late),
        ],
        out_specs=[in_vmem] * len(out) if many else in_vmem,
        scratch_shapes=[
            *(pltpu.VMEM(args[i].shape, args[i].dtype) for i in in_hbm),
            *([pltpu.SemaphoreType.DMA((max(len(in_hbm), BANDS // CHUNK),))] if in_hbm else []),
            *scratch,
        ],
        compiler_params=pltpu.CompilerParams(vmem_limit_bytes=vmem * MIB),
    )(*args, *late)


def fetch(sources, targets, sems):
    copies = [pltpu.make_async_copy(s, t, sems.at[i]) for i, (s, t) in enumerate(zip(sources, targets))]
    for copy in copies:
        copy.start()
    return copies


def shape(*dims, dtype=F32):
    return jax.ShapeDtypeStruct(dims, dtype)


def sticks_to_z(resp_hbm, table_hbm, out, resp, table, sems):
    for copy in fetch((resp_hbm, table_hbm), (resp, table), sems):
        copy.wait()
    out[...] = dot3((table[0], table[1]), split(resp[...]), ((1,), (1,))).reshape(SLABS, 2 * PL, STK)


def q_mask_of(cells, lanes):
    q = lax.broadcasted_iota(jnp.int32, (16, 1), 0)
    return (cells[:, lanes] // 256 == q).astype(F32)


def pick_of(cells, lanes):
    column = lax.broadcasted_iota(jnp.int32, (256, 1), 0)
    return jnp.where(cells[:, lanes] % 256 == column, 1.0, 0.0).astype(BF16)


def planes_to_modes(
    recv, cells, y_hbm, x_hbm, occ_hbm, modes_hbm, modes_t_hbm,
    out, y_table, x_table, occ, modes, modes_t, sems, field, spectrum
):
    copies = fetch(
        (y_hbm, x_hbm, occ_hbm, modes_hbm, modes_t_hbm), (y_table, x_table, occ, modes, modes_t), sems
    )
    grid = jnp.zeros((512, 256), F32)
    for pair in range(SLABS // 2):
        rows = []
        for src in (2 * pair, 2 * pair + 1):
            mask = q_mask_of(cells, slice(src * STK, (src + 1) * STK))
            rows.append(
                jnp.concatenate(
                    [
                        (part.astype(F32)[:, None, :] * mask[None]).reshape(256, STK).astype(BF16)
                        for part in split(recv[src])
                    ],
                    axis=0,
                )
            )
        chosen = pick_of(cells, slice(2 * pair * STK, 2 * (pair + 1) * STK))
        grid += dot(jnp.concatenate(rows, axis=1), chosen, ((1,), (1,)))
    high, low = split(grid[:256] + grid[256:])
    first = lax.broadcasted_iota(jnp.int32, (1, N), 1) < HALF
    swap_halves = lambda v: jnp.concatenate([v[:, HALF:], v[:, :HALF]], axis=1)
    rows = []
    for j in range(4):
        h, l = (v[:, j // 2 * N : (j // 2 + 1) * N] for v in (high, low))
        if j % 2 == 0:
            l = swap_halves(l)
        else:
            h = swap_halves(h)
        rows.append(jnp.concatenate([jnp.where(first, h, l), h], axis=1))
    for copy in copies:
        copy.wait()
    mixed = dot(jnp.concatenate(rows, axis=0), y_table[...])
    for j in range(4):
        block = mixed[j * 256 : (j + 1) * 256]
        real = block[:N, :N] - block[N:, N:]
        imag = block[:N, N:] + block[N:, :N]
        for c, part in enumerate((real, imag)):
            for k, piece in enumerate(split(part)):
                at = slice(k * N + c * HALF + j * 16, k * N + c * HALF + (j + 1) * 16)
                for p in range(PL):
                    field[at, p * N : (p + 1) * N] = piece[p * 16 : (p + 1) * 16]
    for pair in range(PL // 2):
        lanes = slice(pair * 2 * N, (pair + 1) * 2 * N)
        values = times_left(x_table, field[:, lanes])
        for i in range(2):
            p = 2 * pair + i
            at = slice(i * N, (i + 1) * N)
            density = occ[0, p].astype(F32) * values[:N, at] + occ[1, p].astype(F32) * values[N:, at]
            spectrum[:, p * N : (p + 1) * N] = both(times_right(density, modes_t), 0)
    for pair in range(PL // 2):
        values = times_left(modes, spectrum[:, pair * 2 * N : (pair + 1) * 2 * N])
        for i in range(2):
            out[pl.ds(2 * pair + i, N, stride=PL), :] = values[:, i * N : (i + 1) * N]


def sum_bands(recv, to_slabs):
    total = recv[0]
    for b in range(1, BANDS):
        total = total + recv[b]
    for i in range(SLABS):
        to_slabs[i] = total


def solve_z(where, recv, modes, modes_t32, out):
    columns = [
        jnp.concatenate([recv[i, a * PL : (a + 1) * PL, :] for i in range(SLABS)], axis=0)
        for a in range(AX)
    ]
    spectrum = times_left(modes, jnp.concatenate(columns, axis=1))
    freq = lambda i: jnp.where(i <= N // 2, i, i - N // 2)
    fz = freq(lax.broadcasted_iota(jnp.int32, (N, N), 0))
    fy = freq(lax.broadcasted_iota(jnp.int32, (N, N), 1))
    plane_sq = fz * fz + fy * fy
    weighted = []
    for a in range(AX):
        fx = freq(where[0] * AX + a)
        square = (plane_sq + fx * fx).astype(F32)
        kernel = jnp.where(
            square > 0.0, (0.2 * N) ** 2 / (math.pi * jnp.maximum(square, 1.0)), 0.0
        )
        weighted.append(spectrum[:, a * N : (a + 1) * N] * kernel)
    own = modes_t32[pl.ds(pl.multiple_of(where[1] * PL, PL), PL), :]
    result = dot3(split(own), split(jnp.concatenate(weighted, axis=1)))
    density = recv[where[1]]
    tile = []
    for a in range(AX):
        tile += [result[:, a * N : (a + 1) * N], density[a * PL : (a + 1) * PL]]
    tile = jnp.concatenate(tile, axis=0)
    for i in range(BANDS):
        out[i] = tile


def planes_to_sticks(
    recv_hbm, modes_hbm, modes_t_hbm, xc_hbm, occ_hbm, x_hbm, y_hbm, cells,
    out, recv, modes, modes_t, xc, occ, x_table, y_table, sems, half, rows, grid
):
    copies = fetch(
        (recv_hbm, modes_hbm, modes_t_hbm, xc_hbm, occ_hbm, x_hbm, y_hbm),
        (recv, modes, modes_t, xc, occ, x_table, y_table),
        sems,
    )
    for copy in copies[:3]:
        copy.wait()
    for i in range(8):
        at = slice(i * 256, (i + 1) * 256)
        half[at, :] = times_right(recv[at, :], modes)
    for copy in copies[3:]:
        copy.wait()
    for p in range(PL):
        value = jnp.concatenate(
            [half[pl.ds(i * PL + p, N, stride=2 * PL), :] for i in range(2)], axis=1
        )
        value = times_left(modes_t, value)
        potential = value[:, :N] + xc[p] * value[:, N:]
        product = jnp.concatenate(
            [potential * occ[0, p].astype(F32), potential * occ[1, p].astype(F32)], axis=1
        )
        mixed = times_left(x_table, product)
        real = mixed[:HALF, :N] + mixed[HALF:, N:]
        imag = mixed[:HALF, N:] - mixed[HALF:, :N]
        for c, part in enumerate((real, imag)):
            for k, piece in enumerate(split(part)):
                for j in range(4):
                    at = slice(k * 512 + j * N + p * 16, k * 512 + j * N + (p + 1) * 16)
                    rows[at, c * N : (c + 1) * N] = piece[j * 16 : (j + 1) * 16]
    mixed = dot(rows[:512], y_table[...])
    mixed = mixed[:, :N] + mixed[:, N:] + dot(rows[512:], y_table[:, :N])
    by_j = [mixed[j * N : (j + 1) * N] for j in range(4)]
    first = lax.broadcasted_iota(jnp.int32, (1, N), 1) < HALF
    for h in range(2):
        even, odd = by_j[2 * h], by_j[2 * h + 1]
        grid[h, :N, :] = jnp.where(first, even, pltpu.roll(odd, HALF, 1))
        grid[h, N:, :] = jnp.where(first, pltpu.roll(even, HALF, 1), odd)
    values = both(
        jnp.concatenate(
            [
                jnp.concatenate([grid[h, pl.ds(q, 16, stride=16), :] for h in range(2)], axis=1)
                for q in range(16)
            ],
            axis=0,
        ),
        0,
    )
    for pair in range(SLABS // 2):
        lanes = slice(2 * pair * STK, 2 * (pair + 1) * STK)
        mask = q_mask_of(cells, lanes)
        chosen = dot(values, pick_of(cells, lanes))
        total = jnp.zeros((2 * PL, 2 * STK), F32)
        for q in range(16):
            at = slice(q * 16, (q + 1) * 16)
            total = total + (chosen[:256][at] + chosen[256:][at]) * mask[q : q + 1]
        out[2 * pair] = total[:, :STK]
        out[2 * pair + 1] = total[:, STK:]


CHUNK = 8


def orbitals(hbm, held, sems):
    parts = BANDS // 2 // CHUNK
    copies = [
        pltpu.make_async_copy(
            ref.at[pl.ds(i * CHUNK, CHUNK)], to.at[pl.ds(i * CHUNK, CHUNK)], sems.at[h * parts + i]
        )
        for h, (ref, to) in enumerate(zip(hbm, held))
        for i in range(parts)
    ]
    for copy in copies:
        copy.start()

    def at(k):
        if k % CHUNK == 0:
            copies[k // CHUNK].wait()
        return held[k * 2 // BANDS][k % (BANDS // 2)].astype(F32)

    return at


def overlap_rows(at, probes, sums):
    pairs = [
        (x, jnp.concatenate([x[:, N:], -x[:, :N]], axis=1)) for x in probes
    ]
    for w in range(BANDS):
        orbital = at(w)
        for i, pair in enumerate(pairs):
            for c, probe in enumerate(pair):
                line = jnp.sum(orbital * probe, axis=0, keepdims=True)
                k = c * BANDS + w
                sums[i, k : k + 1, :] = line[:, :N] + line[:, N:]
    rows = []
    for i in range(len(probes)):
        sums[i, 2 * BANDS :, :] = jnp.zeros((N - 2 * BANDS, N), F32)
        rows.append(jnp.sum(sums[i].T, axis=0, keepdims=True))
    return rows


def total_sum(value):
    return jnp.sum(jnp.sum(value, axis=0, keepdims=True), axis=1, keepdims=True)


def lane():
    return lax.broadcasted_iota(jnp.int32, (1, N), 1)


def with_lanes(row, first, values):
    for i, value in enumerate(values):
        row = jnp.where(lane() == first + i, value, row)
    return row


def lower(row):
    return jnp.where(lane() < 2 * BANDS, row, 0.0)


def fixed_overlaps(low, high, resp, prev, occ, out, low_held, high_held, sems, sums):
    at = orbitals((low, high), (low_held, high_held), sems)
    rows = overlap_rows(at, [resp[...], prev[...], occ[...].astype(F32)], sums)
    for i, row in enumerate(rows):
        out[i : i + 1, :] = row
    out[3:, :] = jnp.zeros((5, N), F32)


def apply_and_overlap(
    recv, table, scalars, resp, prev, fixed, low, high,
    applied_out, part_out, low_held, high_held, sems, sums
):
    at = orbitals((low, high), (low_held, high_held), sems)
    values = recv[...].reshape(2 * N, STK).T
    applied = dot3(split(values), (table[0], table[1]))
    applied_out[...] = applied
    margin, along = overlap_rows(at, [applied.astype(BF16).astype(F32), applied], sums)
    response = resp[...]
    first = scalars[0] * response + applied
    rest = first - scalars[1] * prev[...]
    norm = total_sum(response * response)
    slope = total_sum(response * rest) / jnp.where(norm > 0.0, norm, 1.0)
    left = rest - slope * response
    with_resp, with_prev, with_occ = fixed[0:1, :], fixed[1:2, :], fixed[2:3, :]
    along = along + (scalars[0] - slope) * with_resp - scalars[1] * with_prev
    row = jnp.concatenate(
        [
            margin + pltpu.roll(with_occ, 2 * BANDS, 1),
            along,
            with_lanes(
                with_resp,
                2 * BANDS,
                [norm, total_sum(response * first), slope, total_sum(left * left)],
            ),
        ],
        axis=1,
    )
    for i in range(SLABS):
        part_out[i] = row


def join_slabs(where, recv, margin_out, place_out, part_out):
    rows = [jnp.concatenate([recv[i][:, j * N : (j + 1) * N] for i in range(SLABS)], axis=0) for j in range(3)]
    add = lambda v: jnp.sum(v, axis=0, keepdims=True)
    norms, firsts, slopes, lefts = (rows[2][:, 2 * BANDS + i : 2 * BANDS + i + 1] for i in range(4))
    norm = add(norms)
    slope = add(norms * slopes) / jnp.where(norm > 0.0, norm, 1.0)
    spread_ = slopes - slope
    left = add(lefts + norms * spread_ * spread_)
    head = add(rows[0])
    weights = lower(head.astype(BF16).astype(F32))
    with_left = add(rows[1] + spread_ * rows[2])
    with_resp = add(rows[2])
    inner = lambda x: jnp.sum(weights * lower(x), axis=1, keepdims=True)
    removed_resp = inner(with_resp)
    place_out[...] = head
    i = lax.broadcasted_iota(jnp.int32, (N, 1), 0)
    k = i % BANDS
    band = (k % 4 * 2 + k // 4 % 4 * 8 + k // 16) ^ where[0]
    to_band = (i // BANDS * BANDS + band == lane()).astype(F32)
    heads = jnp.concatenate([head, jnp.where(lane() < 2 * BANDS, weights, head)], axis=0)
    heads = jnp.dot(heads, to_band, precision=lax.Precision.HIGHEST, preferred_element_type=F32)
    margin_out[...] = heads[:1]
    row = jnp.concatenate(
        [
            heads[1:],
            with_lanes(
                jnp.zeros((1, N), F32),
                0,
                [norm, add(firsts) - removed_resp, slope, removed_resp, left - 2.0 * inner(with_left)],
            ),
        ],
        axis=1,
    )
    for i in range(BANDS):
        part_out[i] = row


def remove(margin, scalars, resp, prev, applied, low, high, rest_out, low_held, high_held, sems):
    at = orbitals((low, high), (low_held, high_held), sems)
    weights = margin[...].astype(BF16).astype(F32)
    plain = jnp.zeros((STK, 2 * N), F32)
    turned = jnp.zeros((STK, 2 * N), F32)
    for w in range(BANDS):
        orbital = at(w)
        plain = plain + weights[:, w : w + 1] * orbital
        turned = turned + weights[:, BANDS + w : BANDS + w + 1] * orbital
    removed = plain + jnp.concatenate([-turned[:, N:], turned[:, :N]], axis=1)
    rest_out[...] = scalars[0] * resp[...] + applied[...] - removed - scalars[1] * prev[...]


def finish(recv, resp, rest, next_out, coef_out):
    rows = [jnp.concatenate([recv[i][:, j * N : (j + 1) * N] for i in range(BANDS)], axis=0) for j in range(2)]
    norms, alongs, slopes, removed_resp, lefts = (rows[1][:, i : i + 1] for i in range(5))
    add = lambda v: jnp.sum(v, axis=0, keepdims=True)
    real, imag, same, cross = (rows[0][:, i * BANDS : (i + 1) * BANDS] for i in range(4))
    times = lambda a, b: lax.dot_general(
        a, b, (((1,), (1,)), ((), ())), precision=lax.Precision.HIGHEST, preferred_element_type=F32
    )
    square = total_sum(real * (times(real, same) + 2.0 * times(imag, cross)) + imag * times(imag, same))
    alpha = add(alongs) / add(norms)
    gap = slopes - alpha
    resid_sq = add(lefts + gap * (gap * norms - 2.0 * removed_resp)) + square
    beta = jnp.sqrt(jnp.maximum(resid_sq, 0.0) / float(2 * BANDS * STICKS * N) + 1e-06)
    next_out[...] = (rest[...] - alpha * resp[...]) / beta
    coef_out[...] = with_lanes(jnp.zeros((1, N), F32), 0, [alpha, beta])


def swap(value, axis):
    return lax.all_to_all(value, axis, 0, 0, tiled=True)


def across(blocks, bit):
    return lax.ppermute(blocks, "band", [(i, i ^ bit) for i in range(BANDS)])


def after(value, other):
    return lax.optimization_barrier((value, other))


def per_device(
    response, previous, earlier_beta, band_gap, occupied, occupied_real, xc_kernel, stick_map
):
    t = {name: jnp.asarray(value) for name, value in TABLES.items()}
    where = jnp.stack([lax.axis_index("band"), lax.axis_index("slab")]).astype(jnp.int32)
    resp = response.reshape(STK, 2 * N)
    prev = previous.reshape(STK, 2 * N)

    occ_planes = occupied_real.reshape(2, PL, N, N)
    field = call(sticks_to_z, shape(SLABS, 2 * PL, STK), resp, t["z_inverse"], in_hbm=(0, 1), vmem=60)
    stick_map, _ = after(stick_map, field)
    gx = stick_map // N % HALF
    cells = (gx // 4 * 256 + gx % 4 * HALF + stick_map % HALF).reshape(1, STICKS)
    own, cells = after(occupied.reshape(1, STK, 2 * N), cells)
    x1, x3 = across(own, 2), across(own, 6)
    field = swap(field, "slab")
    bf_scratch = lambda *dims: pltpu.VMEM(dims, BF16)
    partial = call(
        planes_to_modes,
        shape(N * PL, N),
        field, cells, t["y_inverse"], t["x_inverse"], occ_planes, t["modes_left"], t["modes_t_right"],
        in_hbm=(2, 3, 4, 5, 6),
        late=(x1, x3),
        scratch=[bf_scratch(2 * N, PL * N), bf_scratch(2 * N, PL * N)],
    )
    partial = swap(partial.reshape(BANDS, AX * PL, N), "band")
    x2 = across(own, 4)
    total = call(sum_bands, shape(SLABS, AX * PL, N), partial, late=(x2,))
    row = jnp.concatenate([own, x1, x2, x3], axis=0)
    y1, y3 = across(row, 8), across(row, 24)
    columns = swap(total, "slab")
    hartree = call(
        solve_z, shape(BANDS, 2 * AX * PL, N), where, columns, t["modes_left"], t["modes_t32"],
        in_smem=(0,),
        late=(y1, y3),
    )
    y2 = across(row, 16)
    xc_planes, _ = after(xc_kernel, hartree)
    xc_planes = xc_planes.reshape(PL, N, N)
    hartree = swap(hartree, "band")
    chosen = call(
        planes_to_sticks,
        shape(SLABS, 2 * PL, STK),
        hartree.reshape(2 * N * PL, N), t["modes_right"], t["modes_t_left"],
        xc_planes, occ_planes, t["x_forward"], t["y_forward"], cells,
        in_hbm=(0, 1, 2, 3, 4, 5, 6),
        vmem=60,
        late=(y2,),
        scratch=[pltpu.VMEM((2 * N * PL, N), F32), bf_scratch(8 * N, 2 * N), pltpu.VMEM((2, 2 * N, N), F32)],
    )
    low = jnp.concatenate([row, y1, y2, y3], axis=0)
    high = across(low, 1)
    gathered = swap(chosen, "slab")
    fixed = call(
        fixed_overlaps,
        shape(8, N),
        low, high, resp, prev, occupied.reshape(STK, 2 * N),
        in_hbm=(0, 1),
        scratch=[pltpu.VMEM((3, N, N), F32)],
    )
    scalars = jnp.stack([band_gap[0], earlier_beta[0]])
    applied, parts = call(
        apply_and_overlap,
        [shape(STK, 2 * N), shape(SLABS, 1, 3 * N)],
        gathered, t["z_forward"], scalars, resp, prev, fixed, low, high,
        in_smem=(2,),
        in_hbm=(6, 7),
        scratch=[pltpu.VMEM((2, N, N), F32)],
    )
    margin, placed_margin, parts = call(
        join_slabs,
        [shape(1, N), shape(1, N), shape(BANDS, 1, 2 * N)],
        where, swap(parts, "slab"),
        in_smem=(0,),
    )
    rest = call(
        remove,
        shape(STK, 2 * N),
        placed_margin, scalars, resp, prev, applied, low, high,
        in_smem=(1,),
        in_hbm=(5, 6),
    )
    next_vector, coefficients = call(
        finish, [shape(STK, 2 * N), shape(1, N)], swap(parts, "band"), resp, rest
    )
    return (
        next_vector.reshape(1, STK, 2 * N),
        margin[0, : 2 * BANDS].reshape(2, BANDS, 1),
        coefficients[0, :2],
    )


def solution(mesh):
    placed = (
        P("band", "slab", None),
        P("band", "slab", None),
        P(),
        P("band"),
        P("band", "slab", None),
        P("band", None, "slab", None),
        P("slab", None),
        P(),
    )
    return jax.shard_map(
        per_device,
        mesh=mesh,
        in_specs=placed,
        out_specs=(P("band", "slab", None), P(None, None, "band"), P()),
        check_vma=False,
    )
```

```python
import math

import jax
import jax.numpy as jnp
import ml_dtypes
import numpy as np
from jax import lax
from jax.experimental import pallas as pl
from jax.experimental.pallas import tpu as pltpu
from jax.sharding import PartitionSpec as P

F32 = jnp.float32
BF16 = jnp.bfloat16
MIB = 1024 * 1024

N = 128
SLABS = 16
PL = N // SLABS
BANDS = 32
AX = N // BANDS
STK = 128
STICKS = SLABS * STK
HALF = 64
NORM = float(N) ** -1.5


def pieces(table):
    high = table.astype(np.float32).astype(ml_dtypes.bfloat16)
    low = (table - high.astype(np.float64)).astype(np.float32).astype(ml_dtypes.bfloat16)
    return np.stack([high, low])


def left(table):
    high, low = pieces(table)
    return np.concatenate([np.concatenate([high, high], 1), np.concatenate([low, np.zeros_like(low)], 1)], 0)


def right(table):
    return left(table.T).T.copy()


def angle(a, b):
    return 2.0 * np.pi * ((np.asarray(a)[:, None] * np.asarray(b)[None, :]) % N) / N


def tables():
    every = np.arange(N)
    short = np.arange(HALF)
    signed = np.where(short < HALF // 2, short, short - HALF)
    signed_x = signed.reshape(16, 4).T.reshape(-1)

    c, s = np.cos(angle(every, every)), np.sin(angle(every, every))
    by_slab = lambda m: m.reshape(SLABS, 1, PL, -1)
    z_inverse = np.concatenate(
        [
            np.concatenate([by_slab(c), by_slab(-s)], axis=3),
            np.concatenate([by_slab(s), by_slab(c)], axis=3),
        ],
        axis=1,
    ).reshape(2 * N, 2 * N)
    z_forward = np.concatenate(
        [
            np.concatenate([by_slab(c), by_slab(-s)], axis=3),
            np.concatenate([by_slab(s), by_slab(c)], axis=3),
        ],
        axis=1,
    ).reshape(2 * N, 2 * N)

    cy, sy = np.cos(angle(signed, every)), np.sin(angle(signed, every))
    high, low = pieces(np.concatenate([cy, sy], axis=1))
    y_inverse = np.concatenate([high, high, low, np.zeros_like(low)], axis=0)
    y_forward = np.concatenate(pieces(np.block([[cy.T, -sy.T], [sy.T, cy.T]])), axis=1)

    cx, sx = np.cos(angle(every, signed_x)), np.sin(angle(every, signed_x))
    x_inverse = 2.0 * NORM * np.block([[cx, -sx], [sx, cx]])
    x_forward = NORM * np.concatenate([cx.T, sx.T], axis=0)

    modes = np.zeros((N, N))
    modes[0] = 1.0 / math.sqrt(N)
    modes[1:64] = math.sqrt(2.0 / N) * np.cos(angle(np.arange(1, 64), every))
    modes[64] = np.cos(np.pi * every) / math.sqrt(N)
    modes[65:] = math.sqrt(2.0 / N) * np.sin(angle(np.arange(1, 64), every))
    return {
        "z_inverse": pieces(z_inverse),
        "z_forward": pieces(z_forward),
        "y_inverse": y_inverse,
        "y_forward": y_forward,
        "x_inverse": left(x_inverse),
        "x_forward": left(x_forward),
        "modes_left": left(modes),
        "modes_right": right(modes),
        "modes_t_left": left(modes.T),
        "modes_t_right": right(modes.T),
        "modes_t32": modes.T.astype(np.float32),
    }


TABLES = tables()


def split(value):
    high = value.astype(BF16)
    return high, (value - high.astype(F32)).astype(BF16)


def dot(a, b, contract=((1,), (0,))):
    return lax.dot_general(a, b, (contract, ((), ())), preferred_element_type=F32)


def dot3(a, b, contract=((1,), (0,))):
    return dot(a[0], b[0], contract) + (dot(a[1], b[0], contract) + dot(a[0], b[1], contract))


def both(value, axis):
    return jnp.concatenate(split(value), axis=axis)


def times_left(table, value):
    out = dot(table[...], both(value, 0) if value.dtype == F32 else value)
    half = out.shape[0] // 2
    return out[:half] + out[half:]


def times_right(value, table):
    out = dot(both(value, 1), table[...])
    return out[:, :N] + out[:, N:]


def call(body, out, *args, scratch=(), in_smem=(), in_hbm=(), out_smem=(), vmem=16, late=()):
    space = lambda i: pltpu.SMEM if i in in_smem else pltpu.HBM if i in in_hbm else pltpu.VMEM
    many = isinstance(out, (list, tuple))
    n = len(args)
    inner = (lambda *refs: body(*refs[:n], *refs[n + len(late) :])) if late else body
    return pl.pallas_call(
        inner,
        out_shape=out,
        in_specs=[
            *(pl.BlockSpec(memory_space=space(i)) for i in range(len(args))),
            *(pl.BlockSpec(memory_space=pltpu.HBM) for _ in late),
        ],
        out_specs=[
            pl.BlockSpec(memory_space=pltpu.SMEM if i in out_smem else pltpu.VMEM) for i in range(len(out))
        ]
        if many
        else pl.BlockSpec(memory_space=pltpu.VMEM),
        scratch_shapes=[
            *(pltpu.VMEM(args[i].shape, args[i].dtype) for i in in_hbm),
            *([pltpu.SemaphoreType.DMA((16,))] if in_hbm else []),
            *scratch,
        ],
        compiler_params=pltpu.CompilerParams(vmem_limit_bytes=int(vmem * MIB)),
    )(*args, *late)


def fetch(sources, targets, sems):
    copies = [pltpu.make_async_copy(s, t, sems.at[i]) for i, (s, t) in enumerate(zip(sources, targets))]
    for copy in copies:
        copy.start()
    return copies


def shape(*dims, dtype=F32):
    return jax.ShapeDtypeStruct(dims, dtype)


def sticks_to_z(resp_hbm, table_hbm, out, resp, table, sems):
    for copy in fetch((resp_hbm, table_hbm), (resp, table), sems):
        copy.wait()
    out[...] = dot3((table[0], table[1]), split(resp[...]), ((1,), (1,))).reshape(SLABS, 2 * PL, STK)


def q_mask_of(cells, lanes):
    q = lax.broadcasted_iota(jnp.int32, (16, 1), 0)
    return (cells[:, lanes] // 256 == q).astype(F32)


def pick_of(cells, lanes):
    column = lax.broadcasted_iota(jnp.int32, (256, 1), 0)
    return jnp.where(cells[:, lanes] % 256 == column, 1.0, 0.0).astype(BF16)


def planes_to_modes(
    recv, cells, y_hbm, x_hbm, occ_hbm, modes_hbm, modes_t_hbm,
    out, y_table, x_table, occ, modes, modes_t, sems, field, spectrum
):
    copies = fetch(
        (y_hbm, x_hbm, occ_hbm, modes_hbm, modes_t_hbm), (y_table, x_table, occ, modes, modes_t), sems
    )
    grid = jnp.zeros((512, 256), F32)
    for pair in range(SLABS // 2):
        rows = []
        for src in (2 * pair, 2 * pair + 1):
            mask = q_mask_of(cells, slice(src * STK, (src + 1) * STK))
            rows.append(
                jnp.concatenate(
                    [
                        (part.astype(F32)[:, None, :] * mask[None]).reshape(256, STK).astype(BF16)
                        for part in split(recv[src])
                    ],
                    axis=0,
                )
            )
        chosen = pick_of(cells, slice(2 * pair * STK, 2 * (pair + 1) * STK))
        grid += dot(jnp.concatenate(rows, axis=1), chosen, ((1,), (1,)))
    high, low = split(grid[:256] + grid[256:])
    first = lax.broadcasted_iota(jnp.int32, (1, N), 1) < HALF
    swap_halves = lambda v: jnp.concatenate([v[:, HALF:], v[:, :HALF]], axis=1)
    rows = []
    for j in range(4):
        h, l = (v[:, j // 2 * N : (j // 2 + 1) * N] for v in (high, low))
        if j % 2 == 0:
            l = swap_halves(l)
        else:
            h = swap_halves(h)
        rows.append(jnp.concatenate([jnp.where(first, h, l), h], axis=1))
    for copy in copies:
        copy.wait()
    mixed = dot(jnp.concatenate(rows, axis=0), y_table[...])
    for j in range(4):
        block = mixed[j * 256 : (j + 1) * 256]
        real = block[:N, :N] - block[N:, N:]
        imag = block[:N, N:] + block[N:, :N]
        for c, part in enumerate((real, imag)):
            for k, piece in enumerate(split(part)):
                at = slice(k * N + c * HALF + j * 16, k * N + c * HALF + (j + 1) * 16)
                for p in range(PL):
                    field[at, p * N : (p + 1) * N] = piece[p * 16 : (p + 1) * 16]
    for pair in range(PL // 2):
        lanes = slice(pair * 2 * N, (pair + 1) * 2 * N)
        values = times_left(x_table, field[:, lanes])
        for i in range(2):
            p = 2 * pair + i
            at = slice(i * N, (i + 1) * N)
            density = occ[0, p].astype(F32) * values[:N, at] + occ[1, p].astype(F32) * values[N:, at]
            spectrum[:, p * N : (p + 1) * N] = both(times_right(density, modes_t), 0)
    for pair in range(PL // 2):
        values = times_left(modes, spectrum[:, pair * 2 * N : (pair + 1) * 2 * N])
        for i in range(2):
            out[pl.ds(2 * pair + i, N, stride=PL), :] = values[:, i * N : (i + 1) * N]


TOP = 32767.0


def code(value):
    top = jnp.maximum(jnp.max(jnp.abs(value), axis=0, keepdims=True), 1e-30)
    log = jnp.ceil(jnp.log(top) * (4.0 / math.log(2.0)) + 0.01)
    codes = jnp.round(value * (TOP / jnp.exp2(log * 0.25)))
    return jnp.clip(codes, -TOP, TOP), log


def scale_of(log):
    return jnp.exp2(log * 0.25) * (1.0 / TOP)


def narrow(value):
    return value.astype(jnp.int32).astype(jnp.int16)


def widen(value):
    return value.astype(jnp.int32).astype(F32)


def sum_bands(recv, total_out, to_slabs):
    total = recv[0]
    for b in range(1, BANDS):
        total = total + recv[b]
    total_out[...] = total
    codes, log = code(total)
    tile = narrow(jnp.concatenate([codes, jnp.broadcast_to(log, (8, N))], axis=0))
    for i in range(SLABS):
        to_slabs[i] = tile


def solve_z(where, recv, density, modes, modes_t32, out):
    slabs = []
    for i in range(SLABS):
        tile = widen(recv[i])
        slabs.append(tile[: AX * PL] * scale_of(tile[AX * PL : AX * PL + 1]))
    columns = [
        jnp.concatenate([tile[a * PL : (a + 1) * PL] for tile in slabs], axis=0) for a in range(AX)
    ]
    spectrum = times_left(modes, jnp.concatenate(columns, axis=1))
    freq = lambda i: jnp.where(i <= N // 2, i, i - N // 2)
    fz = freq(lax.broadcasted_iota(jnp.int32, (N, N), 0))
    fy = freq(lax.broadcasted_iota(jnp.int32, (N, N), 1))
    plane_sq = fz * fz + fy * fy
    weighted = []
    for a in range(AX):
        fx = freq(where[0] * AX + a)
        square = (plane_sq + fx * fx).astype(F32)
        kernel = jnp.where(
            square > 0.0, (0.2 * N) ** 2 / (math.pi * jnp.maximum(square, 1.0)), 0.0
        )
        weighted.append(spectrum[:, a * N : (a + 1) * N] * kernel)
    own = modes_t32[pl.ds(pl.multiple_of(where[1] * PL, PL), PL), :]
    result = dot3(split(own), split(jnp.concatenate(weighted, axis=1)))
    result = jnp.concatenate([result[:, a * N : (a + 1) * N] for a in range(AX)], axis=0)
    values, logs = zip(code(result), code(density[...]))
    tile = []
    for a in range(AX):
        tile += [value[a * PL : (a + 1) * PL] for value in values]
    tile += [jnp.broadcast_to(log, (4, N)) for log in logs]
    tile = narrow(jnp.concatenate(tile, axis=0))
    for i in range(BANDS):
        out[i] = tile


def planes_to_sticks(
    recv, cells, modes_hbm, modes_t_hbm, xc_hbm, occ_hbm, x_hbm, y_hbm,
    out, modes, modes_t, xc, occ, x_table, y_table, sems, half, rows, grid
):
    copies = fetch(
        (modes_hbm, modes_t_hbm, xc_hbm, occ_hbm, x_hbm, y_hbm),
        (modes, modes_t, xc, occ, x_table, y_table),
        sems,
    )
    copies[0].wait()
    size = 2 * AX * PL
    for i in range(0, BANDS, 4):
        tiles = []
        for b in range(i, i + 4):
            tile = widen(recv[b])
            scales = [
                jnp.broadcast_to(scale_of(tile[size + 4 * k : size + 4 * k + 1]), (PL, N)) for k in range(2)
            ]
            tiles.append(tile[:size] * jnp.concatenate(scales * AX, axis=0))
        half[i * size : (i + 4) * size, :] = times_right(jnp.concatenate(tiles, axis=0), modes)
    for copy in copies[1:]:
        copy.wait()
    for p in range(PL):
        value = jnp.concatenate(
            [half[pl.ds(i * PL + p, N, stride=2 * PL), :] for i in range(2)], axis=1
        )
        value = times_left(modes_t, value)
        potential = value[:, :N] + xc[p] * value[:, N:]
        product = jnp.concatenate(
            [potential * occ[0, p].astype(F32), potential * occ[1, p].astype(F32)], axis=1
        )
        mixed = times_left(x_table, product)
        real = mixed[:HALF, :N] + mixed[HALF:, N:]
        imag = mixed[:HALF, N:] - mixed[HALF:, :N]
        for c, part in enumerate((real, imag)):
            for k, piece in enumerate(split(part)):
                for j in range(4):
                    at = slice(k * 512 + j * N + p * 16, k * 512 + j * N + (p + 1) * 16)
                    rows[at, c * N : (c + 1) * N] = piece[j * 16 : (j + 1) * 16]
    mixed = dot(rows[:512], y_table[...])
    mixed = mixed[:, :N] + mixed[:, N:] + dot(rows[512:], y_table[:, :N])
    by_j = [mixed[j * N : (j + 1) * N] for j in range(4)]
    first = lax.broadcasted_iota(jnp.int32, (1, N), 1) < HALF
    for h in range(2):
        even, odd = by_j[2 * h], by_j[2 * h + 1]
        grid[h, :N, :] = jnp.where(first, even, pltpu.roll(odd, HALF, 1))
        grid[h, N:, :] = jnp.where(first, pltpu.roll(even, HALF, 1), odd)
    values = both(
        jnp.concatenate(
            [
                jnp.concatenate([grid[h, pl.ds(q, 16, stride=16), :] for h in range(2)], axis=1)
                for q in range(16)
            ],
            axis=0,
        ),
        0,
    )
    for pair in range(SLABS // 2):
        lanes = slice(2 * pair * STK, 2 * (pair + 1) * STK)
        mask = q_mask_of(cells, lanes)
        chosen = dot(values, pick_of(cells, lanes))
        total = jnp.zeros((2 * PL, 2 * STK), F32)
        for q in range(16):
            at = slice(q * 16, (q + 1) * 16)
            total = total + (chosen[:256][at] + chosen[256:][at]) * mask[q : q + 1]
        out[2 * pair] = total[:, :STK]
        out[2 * pair + 1] = total[:, STK:]


CHUNK = 8


def orbitals(hbm, held, sems):
    parts = BANDS // 2 // CHUNK
    copies = [
        pltpu.make_async_copy(
            ref.at[pl.ds(i * CHUNK, CHUNK)], to.at[pl.ds(i * CHUNK, CHUNK)], sems.at[h * parts + i]
        )
        for h, (ref, to) in enumerate(zip(hbm, held))
        for i in range(parts)
    ]
    for copy in copies:
        copy.start()

    def at(k):
        if k % CHUNK == 0:
            copies[k // CHUNK].wait()
        return held[k * 2 // BANDS][k % (BANDS // 2)].astype(F32)

    return at


def band_of(place, me):
    return (place % 4 * 2 + place // 4 % 4 * 8 + place // 16) ^ me


def overlap_rows(at, where, probes, sums):
    pairs = [
        (x, jnp.concatenate([x[:, N:], -x[:, :N]], axis=1)) for x in probes
    ]
    for place in range(BANDS):
        orbital = at(place)
        w = band_of(place, where[0])
        for i, pair in enumerate(pairs):
            for c, probe in enumerate(pair):
                line = jnp.sum(orbital * probe, axis=0, keepdims=True)
                sums[i, pl.ds(c * BANDS + w, 1), :] = line[:, :N] + line[:, N:]
    rows = []
    for i in range(len(probes)):
        sums[i, 2 * BANDS :, :] = jnp.zeros((N - 2 * BANDS, N), F32)
        rows.append(jnp.sum(sums[i].T, axis=0, keepdims=True))
    return rows


def total_sum(value):
    return jnp.sum(jnp.sum(value, axis=0, keepdims=True), axis=1, keepdims=True)


def lane():
    return lax.broadcasted_iota(jnp.int32, (1, N), 1)


def with_lanes(row, first, values):
    for i, value in enumerate(values):
        row = jnp.where(lane() == first + i, value, row)
    return row


def lower(row):
    return jnp.where(lane() < 2 * BANDS, row, 0.0)


def fixed_overlaps(where, low, high, resp, prev, occ, out, low_held, high_held, sems, sums):
    at = orbitals((low, high), (low_held, high_held), sems)
    rows = overlap_rows(at, where, [resp[...], prev[...], occ[...].astype(F32)], sums)
    for i, row in enumerate(rows):
        out[i : i + 1, :] = row
    out[3:, :] = jnp.zeros((5, N), F32)


def apply_and_overlap(
    recv, table, where, scalars, resp, prev, fixed, low, high,
    applied_out, part_out, low_held, high_held, sems, sums
):
    at = orbitals((low, high), (low_held, high_held), sems)
    values = recv[...].reshape(2 * N, STK).T
    applied = dot3(split(values), (table[0], table[1]))
    applied_out[...] = applied
    margin, along = overlap_rows(at, where, [applied.astype(BF16).astype(F32), applied], sums)
    response = resp[...]
    first = scalars[0] * response + applied
    rest = first - scalars[1] * prev[...]
    norm = total_sum(response * response)
    slope = total_sum(response * rest) / jnp.where(norm > 0.0, norm, 1.0)
    left = rest - slope * response
    with_resp, with_prev, with_occ = fixed[0:1, :], fixed[1:2, :], fixed[2:3, :]
    along = along + (scalars[0] - slope) * with_resp - scalars[1] * with_prev
    row = jnp.concatenate(
        [
            margin + pltpu.roll(with_occ, 2 * BANDS, 1),
            along,
            with_lanes(
                with_resp,
                2 * BANDS,
                [norm, total_sum(response * first), slope, total_sum(left * left)],
            ),
        ],
        axis=1,
    )
    for i in range(SLABS):
        part_out[i] = row


def join_slabs(recv, margin_out, part_out):
    rows = [jnp.concatenate([recv[i][:, j * N : (j + 1) * N] for i in range(SLABS)], axis=0) for j in range(3)]
    add = lambda v: jnp.sum(v, axis=0, keepdims=True)
    norms, firsts, slopes, lefts = (rows[2][:, 2 * BANDS + i : 2 * BANDS + i + 1] for i in range(4))
    norm = add(norms)
    slope = add(norms * slopes) / jnp.where(norm > 0.0, norm, 1.0)
    spread_ = slopes - slope
    left = add(lefts + norms * spread_ * spread_)
    head = add(rows[0])
    weights = lower(head.astype(BF16).astype(F32))
    with_left = add(rows[1] + spread_ * rows[2])
    with_resp = add(rows[2])
    inner = lambda x: jnp.sum(weights * lower(x), axis=1, keepdims=True)
    removed_resp = inner(with_resp)
    margin_out[...] = head
    row = jnp.concatenate(
        [
            jnp.where(lane() < 2 * BANDS, weights, head),
            with_lanes(
                jnp.zeros((1, N), F32),
                0,
                [norm, add(firsts) - removed_resp, slope, removed_resp, left - 2.0 * inner(with_left)],
            ),
        ],
        axis=1,
    )
    for i in range(BANDS):
        part_out[i] = row


def remove(margin, where, scalars, resp, prev, applied, low, high, rest_out, low_held, high_held, sems):
    at = orbitals((low, high), (low_held, high_held), sems)
    weights = margin[...].astype(BF16)
    i = lax.broadcasted_iota(jnp.int32, (1, N), 1)
    band = i // BANDS * BANDS + band_of(i % BANDS, where[0])
    to_place = lax.broadcasted_iota(jnp.int32, (N, 1), 0) == band
    weights = dot(weights, jnp.where(to_place, 1.0, 0.0).astype(BF16))
    plain = jnp.zeros((STK, 2 * N), F32)
    turned = jnp.zeros((STK, 2 * N), F32)
    for w in range(BANDS):
        orbital = at(w)
        plain = plain + weights[:, w : w + 1] * orbital
        turned = turned + weights[:, BANDS + w : BANDS + w + 1] * orbital
    removed = plain + jnp.concatenate([-turned[:, N:], turned[:, :N]], axis=1)
    rest_out[...] = scalars[0] * resp[...] + applied[...] - removed - scalars[1] * prev[...]


def finish(recv, resp, rest, next_out, coef_out):
    rows = [jnp.concatenate([recv[i][:, j * N : (j + 1) * N] for i in range(BANDS)], axis=0) for j in range(2)]
    norms, alongs, slopes, removed_resp, lefts = (rows[1][:, i : i + 1] for i in range(5))
    add = lambda v: jnp.sum(v, axis=0, keepdims=True)
    real, imag, same, cross = (rows[0][:, i * BANDS : (i + 1) * BANDS] for i in range(4))
    times = lambda a, b: lax.dot_general(
        a, b, (((1,), (1,)), ((), ())), precision=lax.Precision.HIGHEST, preferred_element_type=F32
    )
    square = total_sum(real * (times(real, same) + 2.0 * times(imag, cross)) + imag * times(imag, same))
    alpha = add(alongs) / add(norms)
    gap = slopes - alpha
    resid_sq = add(lefts + gap * (gap * norms - 2.0 * removed_resp)) + square
    beta = jnp.sqrt(jnp.maximum(resid_sq, 0.0) / float(2 * BANDS * STICKS * N) + 1e-06)
    next_out[...] = (rest[...] - alpha * resp[...]) / beta
    coef_out[0] = alpha[0, 0]
    coef_out[1] = beta[0, 0]


def swap(value, axis):
    return lax.all_to_all(value, axis, 0, 0, tiled=True)


def across(blocks, bit):
    return lax.ppermute(blocks, "band", [(i, i ^ bit) for i in range(BANDS)])


def after(value, other):
    return lax.optimization_barrier((value, other))


def per_device(
    response, previous, earlier_beta, band_gap, occupied, occupied_real, xc_kernel, stick_map
):
    t = {name: jnp.asarray(value) for name, value in TABLES.items()}
    where = jnp.stack([lax.axis_index("band"), lax.axis_index("slab")]).astype(jnp.int32)
    resp = response.reshape(STK, 2 * N)
    prev = previous.reshape(STK, 2 * N)

    occ_planes = occupied_real.reshape(2, PL, N, N)
    field = call(sticks_to_z, shape(SLABS, 2 * PL, STK), resp, t["z_inverse"], in_hbm=(0, 1), vmem=60)
    stick_map, _ = after(stick_map, field)
    gx = stick_map // N % HALF
    cells = (gx // 4 * 256 + gx % 4 * HALF + stick_map % HALF).reshape(1, STICKS)
    own, cells = after(occupied.reshape(1, STK, 2 * N), cells)
    x1, x3 = across(own, 2), across(own, 6)
    field = swap(field, "slab")
    bf_scratch = lambda *dims: pltpu.VMEM(dims, BF16)
    partial = call(
        planes_to_modes,
        shape(N * PL, N),
        field, cells, t["y_inverse"], t["x_inverse"], occ_planes, t["modes_left"], t["modes_t_right"],
        in_hbm=(2, 3, 4, 5, 6),
        late=(x1, x3),
        scratch=[bf_scratch(2 * N, PL * N), bf_scratch(2 * N, PL * N)],
    )
    partial = swap(partial.reshape(BANDS, AX * PL, N), "band")
    x2 = across(own, 4)
    own_modes, total = call(
        sum_bands,
        [shape(AX * PL, N), shape(SLABS, AX * PL + 8, N, dtype=jnp.int16)],
        partial,
        late=(x2,),
    )
    row = jnp.concatenate([own, x1, x2, x3], axis=0)
    y1, y3 = across(row, 8), across(row, 24)
    columns = swap(total, "slab")
    hartree = call(
        solve_z, shape(BANDS, 2 * AX * PL + 8, N, dtype=jnp.int16), where, columns, own_modes, t["modes_left"], t["modes_t32"],
        in_smem=(0,),
        late=(y1, y3),
    )
    near, hartree = after(y1, hartree)
    y2 = across(near, 24)
    xc_planes, _ = after(xc_kernel, hartree)
    xc_planes = xc_planes.reshape(PL, N, N)
    hartree = swap(hartree, "band")
    chosen = call(
        planes_to_sticks,
        shape(SLABS, 2 * PL, STK),
        hartree, cells, t["modes_right"], t["modes_t_left"],
        xc_planes, occ_planes, t["x_forward"], t["y_forward"],
        in_hbm=(2, 3, 4, 5, 6, 7),
        vmem=59.8,
        late=(y2,),
        scratch=[pltpu.VMEM((2 * N * PL, N), F32), bf_scratch(8 * N, 2 * N), pltpu.VMEM((2, 2 * N, N), F32)],
    )
    low = jnp.concatenate([row, y1, y2, y3], axis=0)
    high = across(low, 1)
    gathered = swap(chosen, "slab")
    fixed = call(
        fixed_overlaps,
        shape(8, N),
        where, low, high, resp, prev, occupied.reshape(STK, 2 * N),
        in_smem=(0,),
        in_hbm=(1, 2),
        scratch=[pltpu.VMEM((3, N, N), F32)],
    )
    scalars = jnp.stack([band_gap[0], earlier_beta[0]])
    applied, parts = call(
        apply_and_overlap,
        [shape(STK, 2 * N), shape(SLABS, 1, 3 * N)],
        gathered, t["z_forward"], where, scalars, resp, prev, fixed, low, high,
        in_smem=(2, 3),
        in_hbm=(7, 8),
        scratch=[pltpu.VMEM((2, N, N), F32)],
    )
    margin, parts = call(
        join_slabs, [shape(1, N), shape(BANDS, 1, 2 * N)], swap(parts, "slab")
    )
    rest = call(
        remove,
        shape(STK, 2 * N),
        margin, where, scalars, resp, prev, applied, low, high,
        in_smem=(1, 2),
        in_hbm=(6, 7),
    )
    next_vector, coefficients = call(
        finish,
        [shape(STK, 2 * N), shape(2)],
        swap(parts, "band"), resp, rest,
        out_smem=(1,),
    )
    return (
        next_vector.reshape(1, STK, 2 * N),
        margin[0, : 2 * BANDS].reshape(2, BANDS, 1),
        coefficients,
    )


def solution(mesh):
    placed = (
        P("band", "slab", None),
        P("band", "slab", None),
        P(),
        P("band"),
        P("band", "slab", None),
        P("band", None, "slab", None),
        P("slab", None),
        P(),
    )
    return jax.shard_map(
        per_device,
        mesh=mesh,
        in_specs=placed,
        out_specs=(P("band", "slab", None), P(None, None, "band"), P()),
        check_vma=False,
    )
```

```python
import math

import jax
import jax.numpy as jnp
import ml_dtypes
import numpy as np
from jax import lax
from jax.experimental import pallas as pl
from jax.experimental.pallas import tpu as pltpu
from jax.sharding import PartitionSpec as P

F32 = jnp.float32
BF16 = jnp.bfloat16
MIB = 1024 * 1024

N = 128
SLABS = 16
PL = N // SLABS
BANDS = 32
AX = N // BANDS
STK = 128
STICKS = SLABS * STK
HALF = 64
NORM = float(N) ** -1.5


def pieces(table):
    high = table.astype(np.float32).astype(ml_dtypes.bfloat16)
    low = (table - high.astype(np.float64)).astype(np.float32).astype(ml_dtypes.bfloat16)
    return np.stack([high, low])


def left(table):
    high, low = pieces(table)
    return np.concatenate([np.concatenate([high, high], 1), np.concatenate([low, np.zeros_like(low)], 1)], 0)


def right(table):
    return left(table.T).T.copy()


def angle(a, b):
    return 2.0 * np.pi * ((np.asarray(a)[:, None] * np.asarray(b)[None, :]) % N) / N


def tables():
    every = np.arange(N)
    short = np.arange(HALF)
    signed = np.where(short < HALF // 2, short, short - HALF)
    signed_x = signed.reshape(16, 4).T.reshape(-1)

    c, s = np.cos(angle(every, every)), np.sin(angle(every, every))
    by_slab = lambda m: m.reshape(SLABS, 1, PL, -1)
    z_inverse = np.concatenate(
        [
            np.concatenate([by_slab(c), by_slab(-s)], axis=3),
            np.concatenate([by_slab(s), by_slab(c)], axis=3),
        ],
        axis=1,
    ).reshape(2 * N, 2 * N)
    z_forward = np.concatenate(
        [
            np.concatenate([by_slab(c), by_slab(-s)], axis=3),
            np.concatenate([by_slab(s), by_slab(c)], axis=3),
        ],
        axis=1,
    ).reshape(2 * N, 2 * N)

    cy, sy = np.cos(angle(signed, every)), np.sin(angle(signed, every))
    high, low = pieces(np.concatenate([cy, sy], axis=1))
    y_inverse = np.concatenate([high, high, low, np.zeros_like(low)], axis=0)
    y_forward = np.concatenate(pieces(np.block([[cy.T, -sy.T], [sy.T, cy.T]])), axis=1)

    cx, sx = np.cos(angle(every, signed_x)), np.sin(angle(every, signed_x))
    x_inverse = 2.0 * NORM * np.block([[cx, -sx], [sx, cx]])
    x_forward = NORM * np.concatenate([cx.T, sx.T], axis=0)

    modes = np.zeros((N, N))
    modes[0] = 1.0 / math.sqrt(N)
    modes[1:64] = math.sqrt(2.0 / N) * np.cos(angle(np.arange(1, 64), every))
    modes[64] = np.cos(np.pi * every) / math.sqrt(N)
    modes[65:] = math.sqrt(2.0 / N) * np.sin(angle(np.arange(1, 64), every))
    return {
        "z_inverse": pieces(z_inverse),
        "z_forward": pieces(z_forward),
        "y_inverse": y_inverse,
        "y_forward": y_forward,
        "x_inverse": left(x_inverse),
        "x_forward": left(x_forward),
        "modes_left": left(modes),
        "modes_right": right(modes),
        "modes_t_left": left(modes.T),
        "modes_t_right": right(modes.T),
        "modes_t32": modes.T.astype(np.float32),
    }


TABLES = tables()


def split(value):
    high = value.astype(BF16)
    return high, (value - high.astype(F32)).astype(BF16)


def dot(a, b, contract=((1,), (0,))):
    return lax.dot_general(a, b, (contract, ((), ())), preferred_element_type=F32)


def dot3(a, b, contract=((1,), (0,))):
    return dot(a[0], b[0], contract) + (dot(a[1], b[0], contract) + dot(a[0], b[1], contract))


def both(value, axis):
    return jnp.concatenate(split(value), axis=axis)


def times_left(table, value):
    out = dot(table[...], both(value, 0) if value.dtype == F32 else value)
    half = out.shape[0] // 2
    return out[:half] + out[half:]


def times_right(value, table):
    out = dot(both(value, 1), table[...])
    return out[:, :N] + out[:, N:]


def call(body, out, *args, scratch=(), in_smem=(), in_hbm=(), out_smem=(), vmem=16, late=()):
    space = lambda i: pltpu.SMEM if i in in_smem else pltpu.HBM if i in in_hbm else pltpu.VMEM
    many = isinstance(out, (list, tuple))
    n = len(args)
    inner = (lambda *refs: body(*refs[:n], *refs[n + len(late) :])) if late else body
    return pl.pallas_call(
        inner,
        out_shape=out,
        in_specs=[
            *(pl.BlockSpec(memory_space=space(i)) for i in range(len(args))),
            *(pl.BlockSpec(memory_space=pltpu.HBM) for _ in late),
        ],
        out_specs=[
            pl.BlockSpec(memory_space=pltpu.SMEM if i in out_smem else pltpu.VMEM) for i in range(len(out))
        ]
        if many
        else pl.BlockSpec(memory_space=pltpu.VMEM),
        scratch_shapes=[
            *(pltpu.VMEM(args[i].shape, args[i].dtype) for i in in_hbm),
            *([pltpu.SemaphoreType.DMA((16,))] if in_hbm else []),
            *scratch,
        ],
        compiler_params=pltpu.CompilerParams(vmem_limit_bytes=int(vmem * MIB)),
    )(*args, *late)


def fetch(sources, targets, sems):
    copies = [pltpu.make_async_copy(s, t, sems.at[i]) for i, (s, t) in enumerate(zip(sources, targets))]
    for copy in copies:
        copy.start()
    return copies


def shape(*dims, dtype=F32):
    return jax.ShapeDtypeStruct(dims, dtype)


def sticks_to_z(resp_hbm, table_hbm, out, resp, table, sems):
    for copy in fetch((resp_hbm, table_hbm), (resp, table), sems):
        copy.wait()
    out[...] = dot3((table[0], table[1]), split(resp[...]), ((1,), (1,))).reshape(SLABS, 2 * PL, STK)


def q_mask_of(cells, lanes):
    q = lax.broadcasted_iota(jnp.int32, (16, 1), 0)
    return (cells[:, lanes] // 256 == q).astype(F32)


def pick_of(cells, lanes):
    column = lax.broadcasted_iota(jnp.int32, (256, 1), 0)
    return jnp.where(cells[:, lanes] % 256 == column, 1.0, 0.0).astype(BF16)


def planes_to_modes(
    recv, cells, y_hbm, x_hbm, occ_hbm, modes_hbm, modes_t_hbm,
    out, y_table, x_table, occ, modes, modes_t, sems, field, spectrum
):
    copies = fetch(
        (y_hbm, x_hbm, occ_hbm, modes_hbm, modes_t_hbm), (y_table, x_table, occ, modes, modes_t), sems
    )
    grid = jnp.zeros((512, 256), F32)
    for pair in range(SLABS // 2):
        rows = []
        for src in (2 * pair, 2 * pair + 1):
            mask = q_mask_of(cells, slice(src * STK, (src + 1) * STK))
            rows.append(
                jnp.concatenate(
                    [
                        (part.astype(F32)[:, None, :] * mask[None]).reshape(256, STK).astype(BF16)
                        for part in split(recv[src])
                    ],
                    axis=0,
                )
            )
        chosen = pick_of(cells, slice(2 * pair * STK, 2 * (pair + 1) * STK))
        grid += dot(jnp.concatenate(rows, axis=1), chosen, ((1,), (1,)))
    high, low = split(grid[:256] + grid[256:])
    first = lax.broadcasted_iota(jnp.int32, (1, N), 1) < HALF
    swap_halves = lambda v: jnp.concatenate([v[:, HALF:], v[:, :HALF]], axis=1)
    rows = []
    for j in range(4):
        h, l = (v[:, j // 2 * N : (j // 2 + 1) * N] for v in (high, low))
        if j % 2 == 0:
            l = swap_halves(l)
        else:
            h = swap_halves(h)
        rows.append(jnp.concatenate([jnp.where(first, h, l), h], axis=1))
    for copy in copies:
        copy.wait()
    mixed = dot(jnp.concatenate(rows, axis=0), y_table[...])
    for j in range(4):
        block = mixed[j * 256 : (j + 1) * 256]
        real = block[:N, :N] - block[N:, N:]
        imag = block[:N, N:] + block[N:, :N]
        for c, part in enumerate((real, imag)):
            for k, piece in enumerate(split(part)):
                at = slice(k * N + c * HALF + j * 16, k * N + c * HALF + (j + 1) * 16)
                for p in range(PL):
                    field[at, p * N : (p + 1) * N] = piece[p * 16 : (p + 1) * 16]
    for pair in range(PL // 2):
        lanes = slice(pair * 2 * N, (pair + 1) * 2 * N)
        values = times_left(x_table, field[:, lanes])
        for i in range(2):
            p = 2 * pair + i
            at = slice(i * N, (i + 1) * N)
            density = occ[0, p].astype(F32) * values[:N, at] + occ[1, p].astype(F32) * values[N:, at]
            spectrum[:, p * N : (p + 1) * N] = both(times_right(density, modes_t), 0)
    for pair in range(PL // 2):
        values = times_left(modes, spectrum[:, pair * 2 * N : (pair + 1) * 2 * N])
        for i in range(2):
            out[pl.ds(2 * pair + i, N, stride=PL), :] = values[:, i * N : (i + 1) * N]


TOP = 32767.0


def code(value):
    top = jnp.maximum(jnp.max(jnp.abs(value), axis=0, keepdims=True), 1e-30)
    log = jnp.ceil(jnp.log(top) * (4.0 / math.log(2.0)) + 0.01)
    codes = jnp.round(value * (TOP / jnp.exp2(log * 0.25)))
    return jnp.clip(codes, -TOP, TOP), log


def scale_of(log):
    return jnp.exp2(log * 0.25) * (1.0 / TOP)


def narrow(value):
    return value.astype(jnp.int32).astype(jnp.int16)


def widen(value):
    return value.astype(jnp.int32).astype(F32)


def sum_bands(recv, total_out, to_slabs):
    total = recv[0]
    for b in range(1, BANDS):
        total = total + recv[b]
    total_out[...] = total
    codes, log = code(total)
    tile = narrow(jnp.concatenate([codes, jnp.broadcast_to(log, (8, N))], axis=0))
    for i in range(SLABS):
        to_slabs[i] = tile


def solve_z(where, recv, density, modes, modes_t32, out):
    slabs = []
    for i in range(SLABS):
        tile = widen(recv[i])
        slabs.append(tile[: AX * PL] * scale_of(tile[AX * PL : AX * PL + 1]))
    columns = [
        jnp.concatenate([tile[a * PL : (a + 1) * PL] for tile in slabs], axis=0) for a in range(AX)
    ]
    spectrum = times_left(modes, jnp.concatenate(columns, axis=1))
    freq = lambda i: jnp.where(i <= N // 2, i, i - N // 2)
    fz = freq(lax.broadcasted_iota(jnp.int32, (N, N), 0))
    fy = freq(lax.broadcasted_iota(jnp.int32, (N, N), 1))
    plane_sq = fz * fz + fy * fy
    weighted = []
    for a in range(AX):
        fx = freq(where[0] * AX + a)
        square = (plane_sq + fx * fx).astype(F32)
        kernel = jnp.where(
            square > 0.0, (0.2 * N) ** 2 / (math.pi * jnp.maximum(square, 1.0)), 0.0
        )
        weighted.append(spectrum[:, a * N : (a + 1) * N] * kernel)
    own = modes_t32[pl.ds(pl.multiple_of(where[1] * PL, PL), PL), :]
    result = dot3(split(own), split(jnp.concatenate(weighted, axis=1)))
    result = jnp.concatenate([result[:, a * N : (a + 1) * N] for a in range(AX)], axis=0)
    values, logs = zip(code(result), code(density[...]))
    tile = []
    for a in range(AX):
        tile += [value[a * PL : (a + 1) * PL] for value in values]
    tile += [jnp.broadcast_to(log, (4, N)) for log in logs]
    tile = narrow(jnp.concatenate(tile, axis=0))
    for i in range(BANDS):
        out[i] = tile


def planes_to_sticks(
    recv, cells, modes_hbm, modes_t_hbm, xc_hbm, occ_hbm, x_hbm, y_hbm,
    out, modes, modes_t, xc, occ, x_table, y_table, sems, half, rows, grid
):
    copies = fetch(
        (modes_hbm, modes_t_hbm, xc_hbm, occ_hbm, x_hbm, y_hbm),
        (modes, modes_t, xc, occ, x_table, y_table),
        sems,
    )
    copies[0].wait()
    size = 2 * AX * PL
    for i in range(0, BANDS, 4):
        tiles = []
        for b in range(i, i + 4):
            tile = widen(recv[b])
            scales = [
                jnp.broadcast_to(scale_of(tile[size + 4 * k : size + 4 * k + 1]), (PL, N)) for k in range(2)
            ]
            tiles.append(tile[:size] * jnp.concatenate(scales * AX, axis=0))
        half[i * size : (i + 4) * size, :] = times_right(jnp.concatenate(tiles, axis=0), modes)
    for copy in copies[1:]:
        copy.wait()
    for p in range(PL):
        value = jnp.concatenate(
            [half[pl.ds(i * PL + p, N, stride=2 * PL), :] for i in range(2)], axis=1
        )
        value = times_left(modes_t, value)
        potential = value[:, :N] + xc[p] * value[:, N:]
        product = jnp.concatenate(
            [potential * occ[0, p].astype(F32), potential * occ[1, p].astype(F32)], axis=1
        )
        mixed = times_left(x_table, product)
        real = mixed[:HALF, :N] + mixed[HALF:, N:]
        imag = mixed[:HALF, N:] - mixed[HALF:, :N]
        for c, part in enumerate((real, imag)):
            for k, piece in enumerate(split(part)):
                for j in range(4):
                    at = slice(k * 512 + j * N + p * 16, k * 512 + j * N + (p + 1) * 16)
                    rows[at, c * N : (c + 1) * N] = piece[j * 16 : (j + 1) * 16]
    mixed = dot(rows[:512], y_table[...])
    mixed = mixed[:, :N] + mixed[:, N:] + dot(rows[512:], y_table[:, :N])
    by_j = [mixed[j * N : (j + 1) * N] for j in range(4)]
    first = lax.broadcasted_iota(jnp.int32, (1, N), 1) < HALF
    for h in range(2):
        even, odd = by_j[2 * h], by_j[2 * h + 1]
        grid[h, :N, :] = jnp.where(first, even, pltpu.roll(odd, HALF, 1))
        grid[h, N:, :] = jnp.where(first, pltpu.roll(even, HALF, 1), odd)
    values = both(
        jnp.concatenate(
            [
                jnp.concatenate([grid[h, pl.ds(q, 16, stride=16), :] for h in range(2)], axis=1)
                for q in range(16)
            ],
            axis=0,
        ),
        0,
    )
    for pair in range(SLABS // 2):
        lanes = slice(2 * pair * STK, 2 * (pair + 1) * STK)
        mask = q_mask_of(cells, lanes)
        chosen = dot(values, pick_of(cells, lanes))
        total = jnp.zeros((2 * PL, 2 * STK), F32)
        for q in range(16):
            at = slice(q * 16, (q + 1) * 16)
            total = total + (chosen[:256][at] + chosen[256:][at]) * mask[q : q + 1]
        out[2 * pair] = total[:, :STK]
        out[2 * pair + 1] = total[:, STK:]


CHUNK = 8


def orbitals(hbm, held, sems):
    parts = BANDS // 2 // CHUNK
    copies = [
        pltpu.make_async_copy(
            ref.at[pl.ds(i * CHUNK, CHUNK)], to.at[pl.ds(i * CHUNK, CHUNK)], sems.at[h * parts + i]
        )
        for h, (ref, to) in enumerate(zip(hbm, held))
        for i in range(parts)
    ]
    for copy in copies:
        copy.start()

    def at(k):
        if k % CHUNK == 0:
            copies[k // CHUNK].wait()
        return held[k * 2 // BANDS][k % (BANDS // 2)].astype(F32)

    return at


def band_of(place, me):
    return (place % 4 * 2 + place // 4 % 4 * 8 + place // 16) ^ me


def overlap_rows(at, where, probes, sums):
    pairs = [
        (x, jnp.concatenate([x[:, N:], -x[:, :N]], axis=1)) for x in probes
    ]
    for place in range(BANDS):
        orbital = at(place)
        w = band_of(place, where[0])
        for i, pair in enumerate(pairs):
            for c, probe in enumerate(pair):
                line = jnp.sum(orbital * probe, axis=0, keepdims=True)
                sums[i, pl.ds(c * BANDS + w, 1), :] = line[:, :N] + line[:, N:]
    rows = []
    for i in range(len(probes)):
        sums[i, 2 * BANDS :, :] = jnp.zeros((N - 2 * BANDS, N), F32)
        rows.append(jnp.sum(sums[i].T, axis=0, keepdims=True))
    return rows


def total_sum(value):
    return jnp.sum(jnp.sum(value, axis=0, keepdims=True), axis=1, keepdims=True)


def lane():
    return lax.broadcasted_iota(jnp.int32, (1, N), 1)


def with_lanes(row, first, values):
    for i, value in enumerate(values):
        row = jnp.where(lane() == first + i, value, row)
    return row


def lower(row):
    return jnp.where(lane() < 2 * BANDS, row, 0.0)


def fixed_overlaps(where, low, high, resp, prev, occ, out, low_held, high_held, sems, sums):
    at = orbitals((low, high), (low_held, high_held), sems)
    rows = overlap_rows(at, where, [resp[...], prev[...], occ[...].astype(F32)], sums)
    for i, row in enumerate(rows):
        out[i : i + 1, :] = row
    out[3:, :] = jnp.zeros((5, N), F32)


def apply_and_overlap(
    recv, table, where, scalars, resp, prev, fixed, low, high,
    applied_out, part_out, low_held, high_held, sems, sums
):
    at = orbitals((low, high), (low_held, high_held), sems)
    values = recv[...].reshape(2 * N, STK).T
    applied = dot3(split(values), (table[0], table[1]))
    applied_out[...] = applied
    margin, along = overlap_rows(at, where, [applied.astype(BF16).astype(F32), applied], sums)
    response = resp[...]
    first = scalars[0] * response + applied
    rest = first - scalars[1] * prev[...]
    norm = total_sum(response * response)
    slope = total_sum(response * rest) / jnp.where(norm > 0.0, norm, 1.0)
    left = rest - slope * response
    with_resp, with_prev, with_occ = fixed[0:1, :], fixed[1:2, :], fixed[2:3, :]
    along = along + (scalars[0] - slope) * with_resp - scalars[1] * with_prev
    row = jnp.concatenate(
        [
            margin + pltpu.roll(with_occ, 2 * BANDS, 1),
            along,
            with_lanes(
                with_resp,
                2 * BANDS,
                [norm, total_sum(response * first), slope, total_sum(left * left)],
            ),
        ],
        axis=1,
    )
    for i in range(SLABS):
        part_out[i] = row


def join_slabs(recv, margin_out, part_out):
    rows = [jnp.concatenate([recv[i][:, j * N : (j + 1) * N] for i in range(SLABS)], axis=0) for j in range(3)]
    add = lambda v: jnp.sum(v, axis=0, keepdims=True)
    norms, firsts, slopes, lefts = (rows[2][:, 2 * BANDS + i : 2 * BANDS + i + 1] for i in range(4))
    norm = add(norms)
    slope = add(norms * slopes) / jnp.where(norm > 0.0, norm, 1.0)
    spread_ = slopes - slope
    left = add(lefts + norms * spread_ * spread_)
    head = add(rows[0])
    weights = lower(head.astype(BF16).astype(F32))
    with_left = add(rows[1] + spread_ * rows[2])
    with_resp = add(rows[2])
    inner = lambda x: jnp.sum(weights * lower(x), axis=1, keepdims=True)
    removed_resp = inner(with_resp)
    margin_out[...] = head
    row = jnp.concatenate(
        [
            jnp.where(lane() < 2 * BANDS, weights, head),
            with_lanes(
                jnp.zeros((1, N), F32),
                0,
                [norm, add(firsts) - removed_resp, slope, removed_resp, left - 2.0 * inner(with_left)],
            ),
        ],
        axis=1,
    )
    for i in range(BANDS):
        part_out[i] = row


def remove(margin, where, scalars, resp, prev, applied, low, high, rest_out, low_held, high_held, sems):
    at = orbitals((low, high), (low_held, high_held), sems)
    weights = margin[...].astype(BF16)
    i = lax.broadcasted_iota(jnp.int32, (1, N), 1)
    band = i // BANDS * BANDS + band_of(i % BANDS, where[0])
    to_place = lax.broadcasted_iota(jnp.int32, (N, 1), 0) == band
    weights = dot(weights, jnp.where(to_place, 1.0, 0.0).astype(BF16))
    plain = jnp.zeros((STK, 2 * N), F32)
    turned = jnp.zeros((STK, 2 * N), F32)
    for w in range(BANDS):
        orbital = at(w)
        plain = plain + weights[:, w : w + 1] * orbital
        turned = turned + weights[:, BANDS + w : BANDS + w + 1] * orbital
    removed = plain + jnp.concatenate([-turned[:, N:], turned[:, :N]], axis=1)
    rest_out[...] = scalars[0] * resp[...] + applied[...] - removed - scalars[1] * prev[...]


def finish(recv, resp, rest, next_out, coef_out):
    rows = [jnp.concatenate([recv[i][:, j * N : (j + 1) * N] for i in range(BANDS)], axis=0) for j in range(2)]
    norms, alongs, slopes, removed_resp, lefts = (rows[1][:, i : i + 1] for i in range(5))
    add = lambda v: jnp.sum(v, axis=0, keepdims=True)
    real, imag, same, cross = (rows[0][:, i * BANDS : (i + 1) * BANDS] for i in range(4))
    times = lambda a, b: lax.dot_general(
        a, b, (((1,), (1,)), ((), ())), precision=lax.Precision.HIGHEST, preferred_element_type=F32
    )
    square = total_sum(real * (times(real, same) + 2.0 * times(imag, cross)) + imag * times(imag, same))
    alpha = add(alongs) / add(norms)
    gap = slopes - alpha
    resid_sq = add(lefts + gap * (gap * norms - 2.0 * removed_resp)) + square
    beta = jnp.sqrt(jnp.maximum(resid_sq, 0.0) / float(2 * BANDS * STICKS * N) + 1e-06)
    next_out[...] = (rest[...] - alpha * resp[...]) / beta
    coef_out[0] = alpha[0, 0]
    coef_out[1] = beta[0, 0]


def swap(value, axis):
    return lax.all_to_all(value, axis, 0, 0, tiled=True)


def across(blocks, bit):
    return lax.ppermute(blocks, "band", [(i, i ^ bit) for i in range(BANDS)])


def after(value, other):
    return lax.optimization_barrier((value, other))


def per_device(
    response, previous, earlier_beta, band_gap, occupied, occupied_real, xc_kernel, stick_map
):
    t = {name: jnp.asarray(value) for name, value in TABLES.items()}
    where = jnp.stack([lax.axis_index("band"), lax.axis_index("slab")]).astype(jnp.int32)
    resp = response.reshape(STK, 2 * N)
    prev = previous.reshape(STK, 2 * N)

    occ_planes = occupied_real.reshape(2, PL, N, N)
    field = call(sticks_to_z, shape(SLABS, 2 * PL, STK), resp, t["z_inverse"], in_hbm=(0, 1), vmem=60)
    stick_map, _ = after(stick_map, field)
    gx = stick_map // N % HALF
    cells = (gx // 4 * 256 + gx % 4 * HALF + stick_map % HALF).reshape(1, STICKS)
    own, cells = after(occupied.reshape(1, STK, 2 * N), cells)
    x1, x3 = across(own, 2), across(own, 6)
    field = swap(field, "slab")
    bf_scratch = lambda *dims: pltpu.VMEM(dims, BF16)
    partial = call(
        planes_to_modes,
        shape(N * PL, N),
        field, cells, t["y_inverse"], t["x_inverse"], occ_planes, t["modes_left"], t["modes_t_right"],
        in_hbm=(2, 3, 4, 5, 6),
        late=(x1, x3),
        scratch=[bf_scratch(2 * N, PL * N), bf_scratch(2 * N, PL * N)],
    )
    partial = swap(partial.reshape(BANDS, AX * PL, N), "band")
    x2 = across(own, 4)
    own_modes, total = call(
        sum_bands,
        [shape(AX * PL, N), shape(SLABS, AX * PL + 8, N, dtype=jnp.int16)],
        partial,
        late=(x2,),
    )
    row = jnp.concatenate([own, x1, x2, x3], axis=0)
    y1, y3 = across(row, 8), across(row, 24)
    columns = swap(total, "slab")
    hartree = call(
        solve_z, shape(BANDS, 2 * AX * PL + 8, N, dtype=jnp.int16), where, columns, own_modes, t["modes_left"], t["modes_t32"],
        in_smem=(0,),
        late=(y1, y3),
    )
    (row, y1, y2, y3), _ = after((row, y1, across(y1, 24), y3), hartree)
    xc_planes, _ = after(xc_kernel, hartree)
    xc_planes = xc_planes.reshape(PL, N, N)
    hartree = swap(hartree, "band")
    chosen = call(
        planes_to_sticks,
        shape(SLABS, 2 * PL, STK),
        hartree, cells, t["modes_right"], t["modes_t_left"],
        xc_planes, occ_planes, t["x_forward"], t["y_forward"],
        in_hbm=(2, 3, 4, 5, 6, 7),
        vmem=59.8,
        scratch=[pltpu.VMEM((2 * N * PL, N), F32), bf_scratch(8 * N, 2 * N), pltpu.VMEM((2, 2 * N, N), F32)],
    )
    low = jnp.concatenate([row, y1, y2, y3], axis=0)
    high = across(low, 1)
    gathered = swap(chosen, "slab")
    fixed = call(
        fixed_overlaps,
        shape(8, N),
        where, low, high, resp, prev, occupied.reshape(STK, 2 * N),
        in_smem=(0,),
        in_hbm=(1, 2),
        scratch=[pltpu.VMEM((3, N, N), F32)],
    )
    scalars = jnp.stack([band_gap[0], earlier_beta[0]])
    applied, parts = call(
        apply_and_overlap,
        [shape(STK, 2 * N), shape(SLABS, 1, 3 * N)],
        gathered, t["z_forward"], where, scalars, resp, prev, fixed, low, high,
        in_smem=(2, 3),
        in_hbm=(7, 8),
        scratch=[pltpu.VMEM((2, N, N), F32)],
    )
    margin, parts = call(
        join_slabs, [shape(1, N), shape(BANDS, 1, 2 * N)], swap(parts, "slab")
    )
    rest = call(
        remove,
        shape(STK, 2 * N),
        margin, where, scalars, resp, prev, applied, low, high,
        in_smem=(1, 2),
        in_hbm=(6, 7),
    )
    next_vector, coefficients = call(
        finish,
        [shape(STK, 2 * N), shape(2)],
        swap(parts, "band"), resp, rest,
        out_smem=(1,),
    )
    return (
        next_vector.reshape(1, STK, 2 * N),
        margin[0, : 2 * BANDS].reshape(2, BANDS, 1),
        coefficients,
    )


def solution(mesh):
    placed = (
        P("band", "slab", None),
        P("band", "slab", None),
        P(),
        P("band"),
        P("band", "slab", None),
        P("band", None, "slab", None),
        P("slab", None),
        P(),
    )
    return jax.shard_map(
        per_device,
        mesh=mesh,
        in_specs=placed,
        out_specs=(P("band", "slab", None), P(None, None, "band"), P()),
        check_vma=False,
    )
```

```python
import math

import jax
import jax.numpy as jnp
import ml_dtypes
import numpy as np
from jax import lax
from jax.experimental import pallas as pl
from jax.experimental.pallas import tpu as pltpu
from jax.sharding import PartitionSpec as P

F32 = jnp.float32
BF16 = jnp.bfloat16
MIB = 1024 * 1024

N = 128
SLABS = 16
PL = N // SLABS
BANDS = 32
AX = N // BANDS
STK = 128
STICKS = SLABS * STK
HALF = 64
NORM = float(N) ** -1.5


def pieces(table):
    high = table.astype(np.float32).astype(ml_dtypes.bfloat16)
    low = (table - high.astype(np.float64)).astype(np.float32).astype(ml_dtypes.bfloat16)
    return np.stack([high, low])


def left(table):
    high, low = pieces(table)
    return np.concatenate([np.concatenate([high, high], 1), np.concatenate([low, np.zeros_like(low)], 1)], 0)


def right(table):
    return left(table.T).T.copy()


def angle(a, b):
    return 2.0 * np.pi * ((np.asarray(a)[:, None] * np.asarray(b)[None, :]) % N) / N


def tables():
    every = np.arange(N)
    short = np.arange(HALF)
    signed = np.where(short < HALF // 2, short, short - HALF)
    signed_x = signed.reshape(16, 4).T.reshape(-1)

    c, s = np.cos(angle(every, every)), np.sin(angle(every, every))
    by_slab = lambda m: m.reshape(SLABS, 1, PL, -1)
    z_inverse = np.concatenate(
        [
            np.concatenate([by_slab(c), by_slab(-s)], axis=3),
            np.concatenate([by_slab(s), by_slab(c)], axis=3),
        ],
        axis=1,
    ).reshape(2 * N, 2 * N)
    z_forward = np.concatenate(
        [
            np.concatenate([by_slab(c), by_slab(-s)], axis=3),
            np.concatenate([by_slab(s), by_slab(c)], axis=3),
        ],
        axis=1,
    ).reshape(2 * N, 2 * N)

    cy, sy = np.cos(angle(signed, every)), np.sin(angle(signed, every))
    high, low = pieces(np.concatenate([cy, sy], axis=1))
    y_inverse = np.concatenate([high, high, low, np.zeros_like(low)], axis=0)
    y_forward = np.concatenate(pieces(np.block([[cy.T, -sy.T], [sy.T, cy.T]])), axis=1)

    cx, sx = np.cos(angle(every, signed_x)), np.sin(angle(every, signed_x))
    x_inverse = 2.0 * NORM * np.block([[cx, -sx], [sx, cx]])
    x_forward = NORM * np.concatenate([cx.T, sx.T], axis=0)

    modes = np.zeros((N, N))
    modes[0] = 1.0 / math.sqrt(N)
    modes[1:64] = math.sqrt(2.0 / N) * np.cos(angle(np.arange(1, 64), every))
    modes[64] = np.cos(np.pi * every) / math.sqrt(N)
    modes[65:] = math.sqrt(2.0 / N) * np.sin(angle(np.arange(1, 64), every))
    return {
        "z_inverse": pieces(z_inverse),
        "z_forward": pieces(z_forward),
        "y_inverse": y_inverse,
        "y_forward": y_forward,
        "x_inverse": left(x_inverse),
        "x_forward": left(x_forward),
        "modes_left": left(modes),
        "modes_right": right(modes),
        "modes_t_left": left(modes.T),
        "modes_t_right": right(modes.T),
        "modes_t32": modes.T.astype(np.float32),
    }


TABLES = tables()


def split(value):
    high = value.astype(BF16)
    return high, (value - high.astype(F32)).astype(BF16)


def dot(a, b, contract=((1,), (0,))):
    return lax.dot_general(a, b, (contract, ((), ())), preferred_element_type=F32)


def dot3(a, b, contract=((1,), (0,))):
    return dot(a[0], b[0], contract) + (dot(a[1], b[0], contract) + dot(a[0], b[1], contract))


def both(value, axis):
    return jnp.concatenate(split(value), axis=axis)


def times_left(table, value):
    out = dot(table[...], both(value, 0) if value.dtype == F32 else value)
    half = out.shape[0] // 2
    return out[:half] + out[half:]


def times_right(value, table):
    out = dot(both(value, 1), table[...])
    return out[:, :N] + out[:, N:]


def call(body, out, *args, scratch=(), in_smem=(), in_hbm=(), out_smem=(), vmem=16, late=()):
    space = lambda i: pltpu.SMEM if i in in_smem else pltpu.HBM if i in in_hbm else pltpu.VMEM
    many = isinstance(out, (list, tuple))
    n = len(args)
    inner = (lambda *refs: body(*refs[:n], *refs[n + len(late) :])) if late else body
    return pl.pallas_call(
        inner,
        out_shape=out,
        in_specs=[
            *(pl.BlockSpec(memory_space=space(i)) for i in range(len(args))),
            *(pl.BlockSpec(memory_space=pltpu.HBM) for _ in late),
        ],
        out_specs=[
            pl.BlockSpec(memory_space=pltpu.SMEM if i in out_smem else pltpu.VMEM) for i in range(len(out))
        ]
        if many
        else pl.BlockSpec(memory_space=pltpu.VMEM),
        scratch_shapes=[
            *(pltpu.VMEM(args[i].shape, args[i].dtype) for i in in_hbm),
            *([pltpu.SemaphoreType.DMA((16,))] if in_hbm else []),
            *scratch,
        ],
        compiler_params=pltpu.CompilerParams(vmem_limit_bytes=int(vmem * MIB)),
    )(*args, *late)


def fetch(sources, targets, sems):
    copies = [pltpu.make_async_copy(s, t, sems.at[i]) for i, (s, t) in enumerate(zip(sources, targets))]
    for copy in copies:
        copy.start()
    return copies


def shape(*dims, dtype=F32):
    return jax.ShapeDtypeStruct(dims, dtype)


def sticks_to_z(resp_hbm, table_hbm, out, resp, table, sems):
    for copy in fetch((resp_hbm, table_hbm), (resp, table), sems):
        copy.wait()
    out[...] = dot3((table[0], table[1]), split(resp[...]), ((1,), (1,))).reshape(SLABS, 2 * PL, STK)


def q_mask_of(cells, lanes):
    q = lax.broadcasted_iota(jnp.int32, (16, 1), 0)
    return (cells[:, lanes] // 256 == q).astype(F32)


def pick_of(cells, lanes):
    column = lax.broadcasted_iota(jnp.int32, (256, 1), 0)
    return jnp.where(cells[:, lanes] % 256 == column, 1.0, 0.0).astype(BF16)


def planes_to_modes(
    recv, cells, y_hbm, x_hbm, occ_hbm, modes_hbm, modes_t_hbm,
    out, y_table, x_table, occ, modes, modes_t, sems, field, spectrum
):
    copies = fetch(
        (y_hbm, x_hbm, occ_hbm, modes_hbm, modes_t_hbm), (y_table, x_table, occ, modes, modes_t), sems
    )
    grid = jnp.zeros((512, 256), F32)
    for pair in range(SLABS // 2):
        rows = []
        for src in (2 * pair, 2 * pair + 1):
            mask = q_mask_of(cells, slice(src * STK, (src + 1) * STK))
            rows.append(
                jnp.concatenate(
                    [
                        (part.astype(F32)[:, None, :] * mask[None]).reshape(256, STK).astype(BF16)
                        for part in split(recv[src])
                    ],
                    axis=0,
                )
            )
        chosen = pick_of(cells, slice(2 * pair * STK, 2 * (pair + 1) * STK))
        grid += dot(jnp.concatenate(rows, axis=1), chosen, ((1,), (1,)))
    high, low = split(grid[:256] + grid[256:])
    first = lax.broadcasted_iota(jnp.int32, (1, N), 1) < HALF
    swap_halves = lambda v: jnp.concatenate([v[:, HALF:], v[:, :HALF]], axis=1)
    rows = []
    for j in range(4):
        h, l = (v[:, j // 2 * N : (j // 2 + 1) * N] for v in (high, low))
        if j % 2 == 0:
            l = swap_halves(l)
        else:
            h = swap_halves(h)
        rows.append(jnp.concatenate([jnp.where(first, h, l), h], axis=1))
    for copy in copies:
        copy.wait()
    mixed = dot(jnp.concatenate(rows, axis=0), y_table[...])
    for j in range(4):
        block = mixed[j * 256 : (j + 1) * 256]
        real = block[:N, :N] - block[N:, N:]
        imag = block[:N, N:] + block[N:, :N]
        for c, part in enumerate((real, imag)):
            for k, piece in enumerate(split(part)):
                at = slice(k * N + c * HALF + j * 16, k * N + c * HALF + (j + 1) * 16)
                for p in range(PL):
                    field[at, p * N : (p + 1) * N] = piece[p * 16 : (p + 1) * 16]
    for pair in range(PL // 2):
        lanes = slice(pair * 2 * N, (pair + 1) * 2 * N)
        values = times_left(x_table, field[:, lanes])
        for i in range(2):
            p = 2 * pair + i
            at = slice(i * N, (i + 1) * N)
            density = occ[0, p].astype(F32) * values[:N, at] + occ[1, p].astype(F32) * values[N:, at]
            spectrum[:, p * N : (p + 1) * N] = both(times_right(density, modes_t), 0)
    for pair in range(PL // 2):
        values = times_left(modes, spectrum[:, pair * 2 * N : (pair + 1) * 2 * N])
        for i in range(2):
            out[pl.ds(2 * pair + i, N, stride=PL), :] = values[:, i * N : (i + 1) * N]


TOP = 32767.0


def code(value):
    top = jnp.maximum(jnp.max(jnp.abs(value), axis=0, keepdims=True), 1e-30)
    log = jnp.ceil(jnp.log(top) * (4.0 / math.log(2.0)) + 0.01)
    codes = jnp.round(value * (TOP / jnp.exp2(log * 0.25)))
    return jnp.clip(codes, -TOP, TOP), log


def scale_of(log):
    return jnp.exp2(log * 0.25) * (1.0 / TOP)


def narrow(value):
    return value.astype(jnp.int32).astype(jnp.int16)


def widen(value):
    return value.astype(jnp.int32).astype(F32)


def sum_bands(recv, total_out, to_slabs):
    total = recv[0]
    for b in range(1, BANDS):
        total = total + recv[b]
    total_out[...] = total
    codes, log = code(total)
    tile = narrow(jnp.concatenate([codes, jnp.broadcast_to(log, (8, N))], axis=0))
    for i in range(SLABS):
        to_slabs[i] = tile


def solve_z(where, recv, density, modes, modes_t32, out):
    slabs = []
    for i in range(SLABS):
        tile = widen(recv[i])
        slabs.append(tile[: AX * PL] * scale_of(tile[AX * PL : AX * PL + 1]))
    columns = [
        jnp.concatenate([tile[a * PL : (a + 1) * PL] for tile in slabs], axis=0) for a in range(AX)
    ]
    spectrum = times_left(modes, jnp.concatenate(columns, axis=1))
    freq = lambda i: jnp.where(i <= N // 2, i, i - N // 2)
    fz = freq(lax.broadcasted_iota(jnp.int32, (N, N), 0))
    fy = freq(lax.broadcasted_iota(jnp.int32, (N, N), 1))
    plane_sq = fz * fz + fy * fy
    weighted = []
    for a in range(AX):
        fx = freq(where[0] * AX + a)
        square = (plane_sq + fx * fx).astype(F32)
        kernel = jnp.where(
            square > 0.0, (0.2 * N) ** 2 / (math.pi * jnp.maximum(square, 1.0)), 0.0
        )
        weighted.append(spectrum[:, a * N : (a + 1) * N] * kernel)
    own = modes_t32[pl.ds(pl.multiple_of(where[1] * PL, PL), PL), :]
    result = dot3(split(own), split(jnp.concatenate(weighted, axis=1)))
    result = jnp.concatenate([result[:, a * N : (a + 1) * N] for a in range(AX)], axis=0)
    values, logs = zip(code(result), code(density[...]))
    tile = []
    for a in range(AX):
        tile += [value[a * PL : (a + 1) * PL] for value in values]
    tile += [jnp.broadcast_to(log, (4, N)) for log in logs]
    tile = narrow(jnp.concatenate(tile, axis=0))
    for i in range(BANDS):
        out[i] = tile


def planes_to_sticks(
    recv, cells, modes_hbm, modes_t_hbm, xc_hbm, occ_hbm, x_hbm, y_hbm,
    out, modes, modes_t, xc, occ, x_table, y_table, sems, half, rows, grid
):
    copies = fetch(
        (modes_hbm, modes_t_hbm, xc_hbm, occ_hbm, x_hbm, y_hbm),
        (modes, modes_t, xc, occ, x_table, y_table),
        sems,
    )
    copies[0].wait()
    size = 2 * AX * PL
    for i in range(0, BANDS, 4):
        tiles = []
        for b in range(i, i + 4):
            tile = widen(recv[b])
            scales = [
                jnp.broadcast_to(scale_of(tile[size + 4 * k : size + 4 * k + 1]), (PL, N)) for k in range(2)
            ]
            tiles.append(tile[:size] * jnp.concatenate(scales * AX, axis=0))
        half[i * size : (i + 4) * size, :] = times_right(jnp.concatenate(tiles, axis=0), modes)
    for copy in copies[1:]:
        copy.wait()
    for p in range(PL):
        value = jnp.concatenate(
            [half[pl.ds(i * PL + p, N, stride=2 * PL), :] for i in range(2)], axis=1
        )
        value = times_left(modes_t, value)
        potential = value[:, :N] + xc[p] * value[:, N:]
        product = jnp.concatenate(
            [potential * occ[0, p].astype(F32), potential * occ[1, p].astype(F32)], axis=1
        )
        mixed = times_left(x_table, product)
        real = mixed[:HALF, :N] + mixed[HALF:, N:]
        imag = mixed[:HALF, N:] - mixed[HALF:, :N]
        for c, part in enumerate((real, imag)):
            for k, piece in enumerate(split(part)):
                for j in range(4):
                    at = slice(k * 512 + j * N + p * 16, k * 512 + j * N + (p + 1) * 16)
                    rows[at, c * N : (c + 1) * N] = piece[j * 16 : (j + 1) * 16]
    mixed = dot(rows[:512], y_table[...])
    mixed = mixed[:, :N] + mixed[:, N:] + dot(rows[512:], y_table[:, :N])
    by_j = [mixed[j * N : (j + 1) * N] for j in range(4)]
    first = lax.broadcasted_iota(jnp.int32, (1, N), 1) < HALF
    for h in range(2):
        even, odd = by_j[2 * h], by_j[2 * h + 1]
        grid[h, :N, :] = jnp.where(first, even, pltpu.roll(odd, HALF, 1))
        grid[h, N:, :] = jnp.where(first, pltpu.roll(even, HALF, 1), odd)
    values = both(
        jnp.concatenate(
            [
                jnp.concatenate([grid[h, pl.ds(q, 16, stride=16), :] for h in range(2)], axis=1)
                for q in range(16)
            ],
            axis=0,
        ),
        0,
    )
    for pair in range(SLABS // 2):
        lanes = slice(2 * pair * STK, 2 * (pair + 1) * STK)
        mask = q_mask_of(cells, lanes)
        chosen = dot(values, pick_of(cells, lanes))
        total = jnp.zeros((2 * PL, 2 * STK), F32)
        for q in range(16):
            at = slice(q * 16, (q + 1) * 16)
            total = total + (chosen[:256][at] + chosen[256:][at]) * mask[q : q + 1]
        out[2 * pair] = total[:, :STK]
        out[2 * pair + 1] = total[:, STK:]


CHUNK = 8


def orbitals(hbm, held, sems):
    parts = BANDS // 2 // CHUNK
    copies = [
        pltpu.make_async_copy(
            ref.at[pl.ds(i * CHUNK, CHUNK)], to.at[pl.ds(i * CHUNK, CHUNK)], sems.at[h * parts + i]
        )
        for h, (ref, to) in enumerate(zip(hbm, held))
        for i in range(parts)
    ]
    for copy in copies:
        copy.start()

    def at(k):
        if k % CHUNK == 0:
            copies[k // CHUNK].wait()
        return held[k * 2 // BANDS][k % (BANDS // 2)].astype(F32)

    return at


def band_of(place, me):
    return (place % 4 * 2 + place // 4 % 4 * 8 + place // 16) ^ me


def overlap_rows(at, where, probes, sums):
    pairs = [
        (x, jnp.concatenate([x[:, N:], -x[:, :N]], axis=1)) for x in probes
    ]
    for place in range(BANDS):
        orbital = at(place)
        w = band_of(place, where[0])
        for i, pair in enumerate(pairs):
            for c, probe in enumerate(pair):
                line = jnp.sum(orbital * probe, axis=0, keepdims=True)
                sums[i, pl.ds(c * BANDS + w, 1), :] = line[:, :N] + line[:, N:]
    rows = []
    for i in range(len(probes)):
        sums[i, 2 * BANDS :, :] = jnp.zeros((N - 2 * BANDS, N), F32)
        rows.append(jnp.sum(sums[i].T, axis=0, keepdims=True))
    return rows


def total_sum(value):
    return jnp.sum(jnp.sum(value, axis=0, keepdims=True), axis=1, keepdims=True)


def lane():
    return lax.broadcasted_iota(jnp.int32, (1, N), 1)


def with_lanes(row, first, values):
    for i, value in enumerate(values):
        row = jnp.where(lane() == first + i, value, row)
    return row


def lower(row):
    return jnp.where(lane() < 2 * BANDS, row, 0.0)


def fixed_overlaps(where, low, high, resp, prev, occ, out, low_held, high_held, sems, sums):
    at = orbitals((low, high), (low_held, high_held), sems)
    rows = overlap_rows(at, where, [resp[...], prev[...], occ[...].astype(F32)], sums)
    for i, row in enumerate(rows):
        out[i : i + 1, :] = row
    out[3:, :] = jnp.zeros((5, N), F32)


def apply_and_overlap(
    recv, table, where, scalars, resp, prev, fixed, low, high,
    applied_out, part_out, low_held, high_held, sems, sums
):
    at = orbitals((low, high), (low_held, high_held), sems)
    values = recv[...].reshape(2 * N, STK).T
    applied = dot3(split(values), (table[0], table[1]))
    applied_out[...] = applied
    margin, along = overlap_rows(at, where, [applied.astype(BF16).astype(F32), applied], sums)
    response = resp[...]
    first = scalars[0] * response + applied
    rest = first - scalars[1] * prev[...]
    norm = total_sum(response * response)
    slope = total_sum(response * rest) / jnp.where(norm > 0.0, norm, 1.0)
    left = rest - slope * response
    with_resp, with_prev, with_occ = fixed[0:1, :], fixed[1:2, :], fixed[2:3, :]
    along = along + (scalars[0] - slope) * with_resp - scalars[1] * with_prev
    row = jnp.concatenate(
        [
            margin + pltpu.roll(with_occ, 2 * BANDS, 1),
            along,
            with_lanes(
                with_resp,
                2 * BANDS,
                [norm, total_sum(response * first), slope, total_sum(left * left)],
            ),
        ],
        axis=1,
    )
    for i in range(SLABS):
        part_out[i] = row


def join_slabs(recv, margin_out, part_out):
    rows = [jnp.concatenate([recv[i][:, j * N : (j + 1) * N] for i in range(SLABS)], axis=0) for j in range(3)]
    add = lambda v: jnp.sum(v, axis=0, keepdims=True)
    norms, firsts, slopes, lefts = (rows[2][:, 2 * BANDS + i : 2 * BANDS + i + 1] for i in range(4))
    norm = add(norms)
    slope = add(norms * slopes) / jnp.where(norm > 0.0, norm, 1.0)
    spread_ = slopes - slope
    left = add(lefts + norms * spread_ * spread_)
    head = add(rows[0])
    weights = lower(head.astype(BF16).astype(F32))
    with_left = add(rows[1] + spread_ * rows[2])
    with_resp = add(rows[2])
    inner = lambda x: jnp.sum(weights * lower(x), axis=1, keepdims=True)
    removed_resp = inner(with_resp)
    margin_out[...] = head
    row = jnp.concatenate(
        [
            jnp.where(lane() < 2 * BANDS, weights, head),
            with_lanes(
                jnp.zeros((1, N), F32),
                0,
                [norm, add(firsts) - removed_resp, slope, removed_resp, left - 2.0 * inner(with_left)],
            ),
        ],
        axis=1,
    )
    for i in range(BANDS):
        part_out[i] = row


def remove(margin, where, scalars, resp, prev, applied, low, high, rest_out, low_held, high_held, sems):
    at = orbitals((low, high), (low_held, high_held), sems)
    weights = margin[...].astype(BF16)
    i = lax.broadcasted_iota(jnp.int32, (1, N), 1)
    band = i // BANDS * BANDS + band_of(i % BANDS, where[0])
    to_place = lax.broadcasted_iota(jnp.int32, (N, 1), 0) == band
    weights = dot(weights, jnp.where(to_place, 1.0, 0.0).astype(BF16))
    plain = jnp.zeros((STK, 2 * N), F32)
    turned = jnp.zeros((STK, 2 * N), F32)
    for w in range(BANDS):
        orbital = at(w)
        plain = plain + weights[:, w : w + 1] * orbital
        turned = turned + weights[:, BANDS + w : BANDS + w + 1] * orbital
    removed = plain + jnp.concatenate([-turned[:, N:], turned[:, :N]], axis=1)
    rest_out[...] = scalars[0] * resp[...] + applied[...] - removed - scalars[1] * prev[...]


def finish(recv, resp, rest, next_out, coef_out):
    rows = [jnp.concatenate([recv[i][:, j * N : (j + 1) * N] for i in range(BANDS)], axis=0) for j in range(2)]
    norms, alongs, slopes, removed_resp, lefts = (rows[1][:, i : i + 1] for i in range(5))
    add = lambda v: jnp.sum(v, axis=0, keepdims=True)
    real, imag, same, cross = (rows[0][:, i * BANDS : (i + 1) * BANDS] for i in range(4))
    times = lambda a, b: lax.dot_general(
        a, b, (((1,), (1,)), ((), ())), precision=lax.Precision.HIGHEST, preferred_element_type=F32
    )
    square = total_sum(real * (times(real, same) + 2.0 * times(imag, cross)) + imag * times(imag, same))
    alpha = add(alongs) / add(norms)
    gap = slopes - alpha
    resid_sq = add(lefts + gap * (gap * norms - 2.0 * removed_resp)) + square
    beta = jnp.sqrt(jnp.maximum(resid_sq, 0.0) / float(2 * BANDS * STICKS * N) + 1e-06)
    next_out[...] = (rest[...] - alpha * resp[...]) / beta
    coef_out[0] = alpha[0, 0]
    coef_out[1] = beta[0, 0]


def swap(value, axis):
    return lax.all_to_all(value, axis, 0, 0, tiled=True)


def across(blocks, bit):
    return lax.ppermute(blocks, "band", [(i, i ^ bit) for i in range(BANDS)])


def after(value, other):
    return lax.optimization_barrier((value, other))


def per_device(
    response, previous, earlier_beta, band_gap, occupied, occupied_real, xc_kernel, stick_map
):
    t = {name: jnp.asarray(value) for name, value in TABLES.items()}
    where = jnp.stack([lax.axis_index("band"), lax.axis_index("slab")]).astype(jnp.int32)
    resp = response.reshape(STK, 2 * N)
    prev = previous.reshape(STK, 2 * N)

    occ_planes = occupied_real.reshape(2, PL, N, N)
    field = call(sticks_to_z, shape(SLABS, 2 * PL, STK), resp, t["z_inverse"], in_hbm=(0, 1), vmem=60)
    stick_map, _ = after(stick_map, field)
    gx = stick_map // N % HALF
    cells = (gx // 4 * 256 + gx % 4 * HALF + stick_map % HALF).reshape(1, STICKS)
    own, cells = after(occupied.reshape(1, STK, 2 * N), cells)
    x1, x3 = across(own, 2), across(own, 6)
    field = swap(field, "slab")
    bf_scratch = lambda *dims: pltpu.VMEM(dims, BF16)
    partial = call(
        planes_to_modes,
        shape(N * PL, N),
        field, cells, t["y_inverse"], t["x_inverse"], occ_planes, t["modes_left"], t["modes_t_right"],
        in_hbm=(2, 3, 4, 5, 6),
        late=(x1, x3),
        scratch=[bf_scratch(2 * N, PL * N), bf_scratch(2 * N, PL * N)],
    )
    partial = swap(partial.reshape(BANDS, AX * PL, N), "band")
    x2 = across(own, 4)
    own_modes, total = call(
        sum_bands,
        [shape(AX * PL, N), shape(SLABS, AX * PL + 8, N, dtype=jnp.int16)],
        partial,
        late=(x2,),
    )
    row = jnp.concatenate([own, x1, x2, x3], axis=0)
    y1, y2, y3 = across(row, 8), across(row, 16), across(row, 24)
    columns = swap(total, "slab")
    hartree = call(
        solve_z, shape(BANDS, 2 * AX * PL + 8, N, dtype=jnp.int16), where, columns, own_modes, t["modes_left"], t["modes_t32"],
        in_smem=(0,),
    )
    (row, y1, y2, y3), _ = after((row, y1, y2, y3), hartree)
    xc_planes, _ = after(xc_kernel, hartree)
    xc_planes = xc_planes.reshape(PL, N, N)
    hartree = swap(hartree, "band")
    chosen = call(
        planes_to_sticks,
        shape(SLABS, 2 * PL, STK),
        hartree, cells, t["modes_right"], t["modes_t_left"],
        xc_planes, occ_planes, t["x_forward"], t["y_forward"],
        in_hbm=(2, 3, 4, 5, 6, 7),
        vmem=59.8,
        scratch=[pltpu.VMEM((2 * N * PL, N), F32), bf_scratch(8 * N, 2 * N), pltpu.VMEM((2, 2 * N, N), F32)],
    )
    low = jnp.concatenate([row, y1, y2, y3], axis=0)
    high = across(low, 1)
    gathered = swap(chosen, "slab")
    fixed = call(
        fixed_overlaps,
        shape(8, N),
        where, low, high, resp, prev, occupied.reshape(STK, 2 * N),
        in_smem=(0,),
        in_hbm=(1, 2),
        scratch=[pltpu.VMEM((3, N, N), F32)],
    )
    scalars = jnp.stack([band_gap[0], earlier_beta[0]])
    applied, parts = call(
        apply_and_overlap,
        [shape(STK, 2 * N), shape(SLABS, 1, 3 * N)],
        gathered, t["z_forward"], where, scalars, resp, prev, fixed, low, high,
        in_smem=(2, 3),
        in_hbm=(7, 8),
        scratch=[pltpu.VMEM((2, N, N), F32)],
    )
    margin, parts = call(
        join_slabs, [shape(1, N), shape(BANDS, 1, 2 * N)], swap(parts, "slab")
    )
    rest = call(
        remove,
        shape(STK, 2 * N),
        margin, where, scalars, resp, prev, applied, low, high,
        in_smem=(1, 2),
        in_hbm=(6, 7),
    )
    next_vector, coefficients = call(
        finish,
        [shape(STK, 2 * N), shape(2)],
        swap(parts, "band"), resp, rest,
        out_smem=(1,),
    )
    return (
        next_vector.reshape(1, STK, 2 * N),
        margin[0, : 2 * BANDS].reshape(2, BANDS, 1),
        coefficients,
    )


def solution(mesh):
    placed = (
        P("band", "slab", None),
        P("band", "slab", None),
        P(),
        P("band"),
        P("band", "slab", None),
        P("band", None, "slab", None),
        P("slab", None),
        P(),
    )
    return jax.shard_map(
        per_device,
        mesh=mesh,
        in_specs=placed,
        out_specs=(P("band", "slab", None), P(None, None, "band"), P()),
        check_vma=False,
    )
```

```python
import math

import jax
import jax.numpy as jnp
import ml_dtypes
import numpy as np
from jax import lax
from jax.experimental import pallas as pl
from jax.experimental.pallas import tpu as pltpu
from jax.sharding import PartitionSpec as P

F32 = jnp.float32
BF16 = jnp.bfloat16
MIB = 1024 * 1024

N = 128
SLABS = 16
PL = N // SLABS
BANDS = 32
AX = N // BANDS
STK = 128
STICKS = SLABS * STK
HALF = 64
NORM = float(N) ** -1.5


def pieces(table):
    high = table.astype(np.float32).astype(ml_dtypes.bfloat16)
    low = (table - high.astype(np.float64)).astype(np.float32).astype(ml_dtypes.bfloat16)
    return np.stack([high, low])


def left(table):
    high, low = pieces(table)
    return np.concatenate([np.concatenate([high, high], 1), np.concatenate([low, np.zeros_like(low)], 1)], 0)


def right(table):
    return left(table.T).T.copy()


def angle(a, b):
    return 2.0 * np.pi * ((np.asarray(a)[:, None] * np.asarray(b)[None, :]) % N) / N


def tables():
    every = np.arange(N)
    short = np.arange(HALF)
    signed = np.where(short < HALF // 2, short, short - HALF)
    signed_x = signed.reshape(16, 4).T.reshape(-1)

    c, s = np.cos(angle(every, every)), np.sin(angle(every, every))
    by_slab = lambda m: m.reshape(SLABS, 1, PL, -1)
    z_inverse = np.concatenate(
        [
            np.concatenate([by_slab(c), by_slab(-s)], axis=3),
            np.concatenate([by_slab(s), by_slab(c)], axis=3),
        ],
        axis=1,
    ).reshape(2 * N, 2 * N)
    z_forward = np.concatenate(
        [
            np.concatenate([by_slab(c), by_slab(-s)], axis=3),
            np.concatenate([by_slab(s), by_slab(c)], axis=3),
        ],
        axis=1,
    ).reshape(2 * N, 2 * N)

    cy, sy = np.cos(angle(signed, every)), np.sin(angle(signed, every))
    high, low = pieces(np.concatenate([cy, sy], axis=1))
    y_inverse = np.concatenate([high, high, low, np.zeros_like(low)], axis=0)
    y_forward = np.concatenate(pieces(np.block([[cy.T, -sy.T], [sy.T, cy.T]])), axis=1)

    cx, sx = np.cos(angle(every, signed_x)), np.sin(angle(every, signed_x))
    x_inverse = 2.0 * NORM * np.block([[cx, -sx], [sx, cx]])
    x_forward = NORM * np.concatenate([cx.T, sx.T], axis=0)

    modes = np.zeros((N, N))
    modes[0] = 1.0 / math.sqrt(N)
    modes[1:64] = math.sqrt(2.0 / N) * np.cos(angle(np.arange(1, 64), every))
    modes[64] = np.cos(np.pi * every) / math.sqrt(N)
    modes[65:] = math.sqrt(2.0 / N) * np.sin(angle(np.arange(1, 64), every))
    return {
        "z_inverse": pieces(z_inverse),
        "z_forward": pieces(z_forward),
        "y_inverse": y_inverse,
        "y_forward": y_forward,
        "x_inverse": left(x_inverse),
        "x_forward": left(x_forward),
        "modes_left": left(modes),
        "modes_right": right(modes),
        "modes_t_left": left(modes.T),
        "modes_t_right": right(modes.T),
        "modes_t32": modes.T.astype(np.float32),
    }


TABLES = tables()


def split(value):
    high = value.astype(BF16)
    return high, (value - high.astype(F32)).astype(BF16)


def dot(a, b, contract=((1,), (0,))):
    return lax.dot_general(a, b, (contract, ((), ())), preferred_element_type=F32)


def dot3(a, b, contract=((1,), (0,))):
    return dot(a[0], b[0], contract) + (dot(a[1], b[0], contract) + dot(a[0], b[1], contract))


def both(value, axis):
    return jnp.concatenate(split(value), axis=axis)


def times_left(table, value):
    out = dot(table[...], both(value, 0) if value.dtype == F32 else value)
    half = out.shape[0] // 2
    return out[:half] + out[half:]


def times_right(value, table):
    out = dot(both(value, 1), table[...])
    return out[:, :N] + out[:, N:]


def call(body, out, *args, scratch=(), in_smem=(), in_hbm=(), out_smem=(), vmem=16, late=()):
    space = lambda i: pltpu.SMEM if i in in_smem else pltpu.HBM if i in in_hbm else pltpu.VMEM
    many = isinstance(out, (list, tuple))
    n = len(args)
    inner = (lambda *refs: body(*refs[:n], *refs[n + len(late) :])) if late else body
    return pl.pallas_call(
        inner,
        out_shape=out,
        in_specs=[
            *(pl.BlockSpec(memory_space=space(i)) for i in range(len(args))),
            *(pl.BlockSpec(memory_space=pltpu.HBM) for _ in late),
        ],
        out_specs=[
            pl.BlockSpec(memory_space=pltpu.SMEM if i in out_smem else pltpu.VMEM) for i in range(len(out))
        ]
        if many
        else pl.BlockSpec(memory_space=pltpu.VMEM),
        scratch_shapes=[
            *(pltpu.VMEM(args[i].shape, args[i].dtype) for i in in_hbm),
            *([pltpu.SemaphoreType.DMA((16,))] if in_hbm else []),
            *scratch,
        ],
        compiler_params=pltpu.CompilerParams(vmem_limit_bytes=int(vmem * MIB)),
    )(*args, *late)


def fetch(sources, targets, sems):
    copies = [pltpu.make_async_copy(s, t, sems.at[i]) for i, (s, t) in enumerate(zip(sources, targets))]
    for copy in copies:
        copy.start()
    return copies


def shape(*dims, dtype=F32):
    return jax.ShapeDtypeStruct(dims, dtype)


def sticks_to_z(resp_hbm, table_hbm, out, resp, table, sems):
    for copy in fetch((resp_hbm, table_hbm), (resp, table), sems):
        copy.wait()
    out[...] = dot3((table[0], table[1]), split(resp[...]), ((1,), (1,))).reshape(SLABS, 2 * PL, STK)


def q_mask_of(cells, lanes):
    q = lax.broadcasted_iota(jnp.int32, (16, 1), 0)
    return (cells[:, lanes] // 256 == q).astype(F32)


def pick_of(cells, lanes):
    column = lax.broadcasted_iota(jnp.int32, (256, 1), 0)
    return jnp.where(cells[:, lanes] % 256 == column, 1.0, 0.0).astype(BF16)


def planes_to_modes(
    recv, cells, y_hbm, x_hbm, occ_hbm, modes_hbm, modes_t_hbm,
    out, y_table, x_table, occ, modes, modes_t, sems, field, spectrum
):
    copies = fetch(
        (y_hbm, x_hbm, occ_hbm, modes_hbm, modes_t_hbm), (y_table, x_table, occ, modes, modes_t), sems
    )
    grid = jnp.zeros((512, 256), F32)
    for pair in range(SLABS // 2):
        rows = []
        for src in (2 * pair, 2 * pair + 1):
            mask = q_mask_of(cells, slice(src * STK, (src + 1) * STK))
            rows.append(
                jnp.concatenate(
                    [
                        (part.astype(F32)[:, None, :] * mask[None]).reshape(256, STK).astype(BF16)
                        for part in split(recv[src])
                    ],
                    axis=0,
                )
            )
        chosen = pick_of(cells, slice(2 * pair * STK, 2 * (pair + 1) * STK))
        grid += dot(jnp.concatenate(rows, axis=1), chosen, ((1,), (1,)))
    high, low = split(grid[:256] + grid[256:])
    first = lax.broadcasted_iota(jnp.int32, (1, N), 1) < HALF
    swap_halves = lambda v: jnp.concatenate([v[:, HALF:], v[:, :HALF]], axis=1)
    rows = []
    for j in range(4):
        h, l = (v[:, j // 2 * N : (j // 2 + 1) * N] for v in (high, low))
        if j % 2 == 0:
            l = swap_halves(l)
        else:
            h = swap_halves(h)
        rows.append(jnp.concatenate([jnp.where(first, h, l), h], axis=1))
    for copy in copies:
        copy.wait()
    mixed = dot(jnp.concatenate(rows, axis=0), y_table[...])
    for j in range(4):
        block = mixed[j * 256 : (j + 1) * 256]
        real = block[:N, :N] - block[N:, N:]
        imag = block[:N, N:] + block[N:, :N]
        for c, part in enumerate((real, imag)):
            for k, piece in enumerate(split(part)):
                at = slice(k * N + c * HALF + j * 16, k * N + c * HALF + (j + 1) * 16)
                for p in range(PL):
                    field[at, p * N : (p + 1) * N] = piece[p * 16 : (p + 1) * 16]
    for pair in range(PL // 2):
        lanes = slice(pair * 2 * N, (pair + 1) * 2 * N)
        values = times_left(x_table, field[:, lanes])
        for i in range(2):
            p = 2 * pair + i
            at = slice(i * N, (i + 1) * N)
            density = occ[0, p].astype(F32) * values[:N, at] + occ[1, p].astype(F32) * values[N:, at]
            spectrum[:, p * N : (p + 1) * N] = both(times_right(density, modes_t), 0)
    for pair in range(PL // 2):
        values = times_left(modes, spectrum[:, pair * 2 * N : (pair + 1) * 2 * N])
        for i in range(2):
            out[pl.ds(2 * pair + i, N, stride=PL), :] = values[:, i * N : (i + 1) * N]


TOP = 32767.0


def code(value):
    top = jnp.maximum(jnp.max(jnp.abs(value), axis=0, keepdims=True), 1e-30)
    log = jnp.ceil(jnp.log(top) * (4.0 / math.log(2.0)) + 0.01)
    codes = jnp.round(value * (TOP / jnp.exp2(log * 0.25)))
    return jnp.clip(codes, -TOP, TOP), log


def scale_of(log):
    return jnp.exp2(log * 0.25) * (1.0 / TOP)


def narrow(value):
    return value.astype(jnp.int32).astype(jnp.int16)


def widen(value):
    return value.astype(jnp.int32).astype(F32)


def sum_bands(recv, total_out, to_slabs):
    total = recv[0]
    for b in range(1, BANDS):
        total = total + recv[b]
    total_out[...] = total
    codes, log = code(total)
    tile = narrow(jnp.concatenate([codes, jnp.broadcast_to(log, (8, N))], axis=0))
    for i in range(SLABS):
        to_slabs[i] = tile


def solve_z(where, recv, density, modes, modes_t32, out):
    slabs = []
    for i in range(SLABS):
        tile = widen(recv[i])
        slabs.append(tile[: AX * PL] * scale_of(tile[AX * PL : AX * PL + 1]))
    columns = [
        jnp.concatenate([tile[a * PL : (a + 1) * PL] for tile in slabs], axis=0) for a in range(AX)
    ]
    spectrum = times_left(modes, jnp.concatenate(columns, axis=1))
    freq = lambda i: jnp.where(i <= N // 2, i, i - N // 2)
    fz = freq(lax.broadcasted_iota(jnp.int32, (N, N), 0))
    fy = freq(lax.broadcasted_iota(jnp.int32, (N, N), 1))
    plane_sq = fz * fz + fy * fy
    weighted = []
    for a in range(AX):
        fx = freq(where[0] * AX + a)
        square = (plane_sq + fx * fx).astype(F32)
        kernel = jnp.where(
            square > 0.0, (0.2 * N) ** 2 / (math.pi * jnp.maximum(square, 1.0)), 0.0
        )
        weighted.append(spectrum[:, a * N : (a + 1) * N] * kernel)
    own = modes_t32[pl.ds(pl.multiple_of(where[1] * PL, PL), PL), :]
    result = dot3(split(own), split(jnp.concatenate(weighted, axis=1)))
    result = jnp.concatenate([result[:, a * N : (a + 1) * N] for a in range(AX)], axis=0)
    values, logs = zip(code(result), code(density[...]))
    tile = []
    for a in range(AX):
        tile += [value[a * PL : (a + 1) * PL] for value in values]
    tile += [jnp.broadcast_to(log, (4, N)) for log in logs]
    tile = narrow(jnp.concatenate(tile, axis=0))
    for i in range(BANDS):
        out[i] = tile


def planes_to_sticks(
    recv, cells, modes_hbm, modes_t_hbm, xc_hbm, occ_hbm, x_hbm, y_hbm,
    out, modes, modes_t, xc, occ, x_table, y_table, sems, half, rows, grid
):
    copies = fetch(
        (modes_hbm, modes_t_hbm, xc_hbm, occ_hbm, x_hbm, y_hbm),
        (modes, modes_t, xc, occ, x_table, y_table),
        sems,
    )
    copies[0].wait()
    size = 2 * AX * PL
    for i in range(0, BANDS, 4):
        tiles = []
        for b in range(i, i + 4):
            tile = widen(recv[b])
            scales = [
                jnp.broadcast_to(scale_of(tile[size + 4 * k : size + 4 * k + 1]), (PL, N)) for k in range(2)
            ]
            tiles.append(tile[:size] * jnp.concatenate(scales * AX, axis=0))
        half[i * size : (i + 4) * size, :] = times_right(jnp.concatenate(tiles, axis=0), modes)
    for copy in copies[1:]:
        copy.wait()
    for p in range(PL):
        value = jnp.concatenate(
            [half[pl.ds(i * PL + p, N, stride=2 * PL), :] for i in range(2)], axis=1
        )
        value = times_left(modes_t, value)
        potential = value[:, :N] + xc[p] * value[:, N:]
        product = jnp.concatenate(
            [potential * occ[0, p].astype(F32), potential * occ[1, p].astype(F32)], axis=1
        )
        mixed = times_left(x_table, product)
        real = mixed[:HALF, :N] + mixed[HALF:, N:]
        imag = mixed[:HALF, N:] - mixed[HALF:, :N]
        for c, part in enumerate((real, imag)):
            for k, piece in enumerate(split(part)):
                for j in range(4):
                    at = slice(k * 512 + j * N + p * 16, k * 512 + j * N + (p + 1) * 16)
                    rows[at, c * N : (c + 1) * N] = piece[j * 16 : (j + 1) * 16]
    mixed = dot(rows[:512], y_table[...])
    mixed = mixed[:, :N] + mixed[:, N:] + dot(rows[512:], y_table[:, :N])
    by_j = [mixed[j * N : (j + 1) * N] for j in range(4)]
    first = lax.broadcasted_iota(jnp.int32, (1, N), 1) < HALF
    for h in range(2):
        even, odd = by_j[2 * h], by_j[2 * h + 1]
        grid[h, :N, :] = jnp.where(first, even, pltpu.roll(odd, HALF, 1))
        grid[h, N:, :] = jnp.where(first, pltpu.roll(even, HALF, 1), odd)
    values = both(
        jnp.concatenate(
            [
                jnp.concatenate([grid[h, pl.ds(q, 16, stride=16), :] for h in range(2)], axis=1)
                for q in range(16)
            ],
            axis=0,
        ),
        0,
    )
    for pair in range(SLABS // 2):
        lanes = slice(2 * pair * STK, 2 * (pair + 1) * STK)
        mask = q_mask_of(cells, lanes)
        chosen = dot(values, pick_of(cells, lanes))
        total = jnp.zeros((2 * PL, 2 * STK), F32)
        for q in range(16):
            at = slice(q * 16, (q + 1) * 16)
            total = total + (chosen[:256][at] + chosen[256:][at]) * mask[q : q + 1]
        out[2 * pair] = total[:, :STK]
        out[2 * pair + 1] = total[:, STK:]


CHUNK = 8


def orbitals(hbm, held, sems):
    parts = BANDS // 2 // CHUNK
    copies = [
        pltpu.make_async_copy(
            ref.at[pl.ds(i * CHUNK, CHUNK)], to.at[pl.ds(i * CHUNK, CHUNK)], sems.at[h * parts + i]
        )
        for h, (ref, to) in enumerate(zip(hbm, held))
        for i in range(parts)
    ]
    for copy in copies:
        copy.start()

    def at(k):
        if k % CHUNK == 0:
            copies[k // CHUNK].wait()
        return held[k * 2 // BANDS][k % (BANDS // 2)].astype(F32)

    return at


def band_of(place, me):
    return (place % 4 * 2 + place // 4 % 4 * 8 + place // 16) ^ me


def overlap_rows(at, where, probes, sums):
    pairs = [
        (x, jnp.concatenate([x[:, N:], -x[:, :N]], axis=1)) for x in probes
    ]
    for place in range(BANDS):
        orbital = at(place)
        w = band_of(place, where[0])
        for i, pair in enumerate(pairs):
            for c, probe in enumerate(pair):
                line = jnp.sum(orbital * probe, axis=0, keepdims=True)
                sums[i, pl.ds(c * BANDS + w, 1), :] = line[:, :N] + line[:, N:]
    rows = []
    for i in range(len(probes)):
        sums[i, 2 * BANDS :, :] = jnp.zeros((N - 2 * BANDS, N), F32)
        rows.append(jnp.sum(sums[i].T, axis=0, keepdims=True))
    return rows


def total_sum(value):
    return jnp.sum(jnp.sum(value, axis=0, keepdims=True), axis=1, keepdims=True)


def lane():
    return lax.broadcasted_iota(jnp.int32, (1, N), 1)


def with_lanes(row, first, values):
    for i, value in enumerate(values):
        row = jnp.where(lane() == first + i, value, row)
    return row


def lower(row):
    return jnp.where(lane() < 2 * BANDS, row, 0.0)


def fixed_overlaps(where, low, high, resp, prev, occ, out, low_held, high_held, sems, sums):
    at = orbitals((low, high), (low_held, high_held), sems)
    rows = overlap_rows(at, where, [resp[...], prev[...], occ[...].astype(F32)], sums)
    for i, row in enumerate(rows):
        out[i : i + 1, :] = row
    out[3:, :] = jnp.zeros((5, N), F32)


def apply_and_overlap(
    recv, table, where, scalars, resp, prev, fixed, low, high,
    applied_out, part_out, low_held, high_held, sems, sums
):
    at = orbitals((low, high), (low_held, high_held), sems)
    values = recv[...].reshape(2 * N, STK).T
    applied = dot3(split(values), (table[0], table[1]))
    applied_out[...] = applied
    margin, along = overlap_rows(at, where, [applied.astype(BF16).astype(F32), applied], sums)
    response = resp[...]
    first = scalars[0] * response + applied
    rest = first - scalars[1] * prev[...]
    norm = total_sum(response * response)
    slope = total_sum(response * rest) / jnp.where(norm > 0.0, norm, 1.0)
    left = rest - slope * response
    with_resp, with_prev, with_occ = fixed[0:1, :], fixed[1:2, :], fixed[2:3, :]
    along = along + (scalars[0] - slope) * with_resp - scalars[1] * with_prev
    row = jnp.concatenate(
        [
            margin + pltpu.roll(with_occ, 2 * BANDS, 1),
            along,
            with_lanes(
                with_resp,
                2 * BANDS,
                [norm, total_sum(response * first), slope, total_sum(left * left)],
            ),
        ],
        axis=1,
    )
    for i in range(SLABS):
        part_out[i] = row


def join_slabs(recv, margin_out, part_out):
    rows = [jnp.concatenate([recv[i][:, j * N : (j + 1) * N] for i in range(SLABS)], axis=0) for j in range(3)]
    add = lambda v: jnp.sum(v, axis=0, keepdims=True)
    norms, firsts, slopes, lefts = (rows[2][:, 2 * BANDS + i : 2 * BANDS + i + 1] for i in range(4))
    norm = add(norms)
    slope = add(norms * slopes) / jnp.where(norm > 0.0, norm, 1.0)
    spread_ = slopes - slope
    left = add(lefts + norms * spread_ * spread_)
    head = add(rows[0])
    weights = lower(head.astype(BF16).astype(F32))
    with_left = add(rows[1] + spread_ * rows[2])
    with_resp = add(rows[2])
    inner = lambda x: jnp.sum(weights * lower(x), axis=1, keepdims=True)
    removed_resp = inner(with_resp)
    margin_out[...] = head
    row = jnp.concatenate(
        [
            jnp.where(lane() < 2 * BANDS, weights, head),
            with_lanes(
                jnp.zeros((1, N), F32),
                0,
                [norm, add(firsts) - removed_resp, slope, removed_resp, left - 2.0 * inner(with_left)],
            ),
        ],
        axis=1,
    )
    for i in range(BANDS):
        part_out[i] = row


def remove(margin, where, scalars, resp, prev, applied, low, high, rest_out, low_held, high_held, sems):
    at = orbitals((low, high), (low_held, high_held), sems)
    weights = margin[...].astype(BF16)
    i = lax.broadcasted_iota(jnp.int32, (1, N), 1)
    band = i // BANDS * BANDS + band_of(i % BANDS, where[0])
    to_place = lax.broadcasted_iota(jnp.int32, (N, 1), 0) == band
    weights = dot(weights, jnp.where(to_place, 1.0, 0.0).astype(BF16))
    plain = jnp.zeros((STK, 2 * N), F32)
    turned = jnp.zeros((STK, 2 * N), F32)
    for w in range(BANDS):
        orbital = at(w)
        plain = plain + weights[:, w : w + 1] * orbital
        turned = turned + weights[:, BANDS + w : BANDS + w + 1] * orbital
    removed = plain + jnp.concatenate([-turned[:, N:], turned[:, :N]], axis=1)
    rest_out[...] = scalars[0] * resp[...] + applied[...] - removed - scalars[1] * prev[...]


def finish(recv, resp, rest, next_out, coef_out):
    rows = [jnp.concatenate([recv[i][:, j * N : (j + 1) * N] for i in range(BANDS)], axis=0) for j in range(2)]
    norms, alongs, slopes, removed_resp, lefts = (rows[1][:, i : i + 1] for i in range(5))
    add = lambda v: jnp.sum(v, axis=0, keepdims=True)
    real, imag, same, cross = (rows[0][:, i * BANDS : (i + 1) * BANDS] for i in range(4))
    times = lambda a, b: lax.dot_general(
        a, b, (((1,), (1,)), ((), ())), precision=lax.Precision.HIGHEST, preferred_element_type=F32
    )
    square = total_sum(real * (times(real, same) + 2.0 * times(imag, cross)) + imag * times(imag, same))
    alpha = add(alongs) / add(norms)
    gap = slopes - alpha
    resid_sq = add(lefts + gap * (gap * norms - 2.0 * removed_resp)) + square
    beta = jnp.sqrt(jnp.maximum(resid_sq, 0.0) / float(2 * BANDS * STICKS * N) + 1e-06)
    next_out[...] = (rest[...] - alpha * resp[...]) / beta
    coef_out[0] = alpha[0, 0]
    coef_out[1] = beta[0, 0]


def swap(value, axis):
    return lax.all_to_all(value, axis, 0, 0, tiled=True)


def across(blocks, bit):
    return lax.ppermute(blocks, "band", [(i, i ^ bit) for i in range(BANDS)])


def after(value, other):
    return lax.optimization_barrier((value, other))


def per_device(
    response, previous, earlier_beta, band_gap, occupied, occupied_real, xc_kernel, stick_map
):
    t = {name: jnp.asarray(value) for name, value in TABLES.items()}
    where = jnp.stack([lax.axis_index("band"), lax.axis_index("slab")]).astype(jnp.int32)
    resp = response.reshape(STK, 2 * N)
    prev = previous.reshape(STK, 2 * N)

    occ_planes = occupied_real.reshape(2, PL, N, N)
    field = call(sticks_to_z, shape(SLABS, 2 * PL, STK), resp, t["z_inverse"], in_hbm=(0, 1), vmem=60)
    stick_map, _ = after(stick_map, field)
    gx = stick_map // N % HALF
    cells = (gx // 4 * 256 + gx % 4 * HALF + stick_map % HALF).reshape(1, STICKS)
    own, cells = after(occupied.reshape(1, STK, 2 * N), cells)
    x1, x3 = across(own, 2), across(own, 6)
    field = swap(field, "slab")
    bf_scratch = lambda *dims: pltpu.VMEM(dims, BF16)
    partial = call(
        planes_to_modes,
        shape(N * PL, N),
        field, cells, t["y_inverse"], t["x_inverse"], occ_planes, t["modes_left"], t["modes_t_right"],
        in_hbm=(2, 3, 4, 5, 6),
        scratch=[bf_scratch(2 * N, PL * N), bf_scratch(2 * N, PL * N)],
    )
    (x1, x3), partial = after((x1, x3), partial)
    partial = swap(partial.reshape(BANDS, AX * PL, N), "band")
    x2 = across(own, 4)
    own_modes, total = call(
        sum_bands,
        [shape(AX * PL, N), shape(SLABS, AX * PL + 8, N, dtype=jnp.int16)],
        partial,
        late=(x2,),
    )
    row = jnp.concatenate([own, x1, x2, x3], axis=0)
    y1, y2, y3 = across(row, 8), across(row, 16), across(row, 24)
    columns = swap(total, "slab")
    hartree = call(
        solve_z, shape(BANDS, 2 * AX * PL + 8, N, dtype=jnp.int16), where, columns, own_modes, t["modes_left"], t["modes_t32"],
        in_smem=(0,),
    )
    (row, y1, y2, y3), _ = after((row, y1, y2, y3), hartree)
    xc_planes, _ = after(xc_kernel, hartree)
    xc_planes = xc_planes.reshape(PL, N, N)
    hartree = swap(hartree, "band")
    chosen = call(
        planes_to_sticks,
        shape(SLABS, 2 * PL, STK),
        hartree, cells, t["modes_right"], t["modes_t_left"],
        xc_planes, occ_planes, t["x_forward"], t["y_forward"],
        in_hbm=(2, 3, 4, 5, 6, 7),
        vmem=59.8,
        scratch=[pltpu.VMEM((2 * N * PL, N), F32), bf_scratch(8 * N, 2 * N), pltpu.VMEM((2, 2 * N, N), F32)],
    )
    low = jnp.concatenate([row, y1, y2, y3], axis=0)
    high = across(low, 1)
    gathered = swap(chosen, "slab")
    fixed = call(
        fixed_overlaps,
        shape(8, N),
        where, low, high, resp, prev, occupied.reshape(STK, 2 * N),
        in_smem=(0,),
        in_hbm=(1, 2),
        scratch=[pltpu.VMEM((3, N, N), F32)],
    )
    scalars = jnp.stack([band_gap[0], earlier_beta[0]])
    applied, parts = call(
        apply_and_overlap,
        [shape(STK, 2 * N), shape(SLABS, 1, 3 * N)],
        gathered, t["z_forward"], where, scalars, resp, prev, fixed, low, high,
        in_smem=(2, 3),
        in_hbm=(7, 8),
        scratch=[pltpu.VMEM((2, N, N), F32)],
    )
    margin, parts = call(
        join_slabs, [shape(1, N), shape(BANDS, 1, 2 * N)], swap(parts, "slab")
    )
    rest = call(
        remove,
        shape(STK, 2 * N),
        margin, where, scalars, resp, prev, applied, low, high,
        in_smem=(1, 2),
        in_hbm=(6, 7),
    )
    next_vector, coefficients = call(
        finish,
        [shape(STK, 2 * N), shape(2)],
        swap(parts, "band"), resp, rest,
        out_smem=(1,),
    )
    return (
        next_vector.reshape(1, STK, 2 * N),
        margin[0, : 2 * BANDS].reshape(2, BANDS, 1),
        coefficients,
    )


def solution(mesh):
    placed = (
        P("band", "slab", None),
        P("band", "slab", None),
        P(),
        P("band"),
        P("band", "slab", None),
        P("band", None, "slab", None),
        P("slab", None),
        P(),
    )
    return jax.shard_map(
        per_device,
        mesh=mesh,
        in_specs=placed,
        out_specs=(P("band", "slab", None), P(None, None, "band"), P()),
        check_vma=False,
    )
```

```python
import math

import jax
import jax.numpy as jnp
import ml_dtypes
import numpy as np
from jax import lax
from jax.experimental import pallas as pl
from jax.experimental.pallas import tpu as pltpu
from jax.sharding import PartitionSpec as P

F32 = jnp.float32
BF16 = jnp.bfloat16
MIB = 1024 * 1024

N = 128
SLABS = 16
PL = N // SLABS
BANDS = 32
AX = N // BANDS
STK = 128
STICKS = SLABS * STK
HALF = 64
NORM = float(N) ** -1.5


def pieces(table):
    high = table.astype(np.float32).astype(ml_dtypes.bfloat16)
    low = (table - high.astype(np.float64)).astype(np.float32).astype(ml_dtypes.bfloat16)
    return np.stack([high, low])


def left(table):
    high, low = pieces(table)
    return np.concatenate([np.concatenate([high, high], 1), np.concatenate([low, np.zeros_like(low)], 1)], 0)


def right(table):
    return left(table.T).T.copy()


def angle(a, b):
    return 2.0 * np.pi * ((np.asarray(a)[:, None] * np.asarray(b)[None, :]) % N) / N


def tables():
    every = np.arange(N)
    short = np.arange(HALF)
    signed = np.where(short < HALF // 2, short, short - HALF)
    signed_x = signed.reshape(16, 4).T.reshape(-1)

    c, s = np.cos(angle(every, every)), np.sin(angle(every, every))
    by_slab = lambda m: m.reshape(SLABS, 1, PL, -1)
    z_inverse = np.concatenate(
        [
            np.concatenate([by_slab(c), by_slab(-s)], axis=3),
            np.concatenate([by_slab(s), by_slab(c)], axis=3),
        ],
        axis=1,
    ).reshape(2 * N, 2 * N)
    z_forward = np.concatenate(
        [
            np.concatenate([by_slab(c), by_slab(-s)], axis=3),
            np.concatenate([by_slab(s), by_slab(c)], axis=3),
        ],
        axis=1,
    ).reshape(2 * N, 2 * N)

    cy, sy = np.cos(angle(signed, every)), np.sin(angle(signed, every))
    high, low = pieces(np.concatenate([cy, sy], axis=1))
    y_inverse = np.concatenate([high, high, low, np.zeros_like(low)], axis=0)
    y_forward = np.concatenate(pieces(np.block([[cy.T, -sy.T], [sy.T, cy.T]])), axis=1)

    cx, sx = np.cos(angle(every, signed_x)), np.sin(angle(every, signed_x))
    x_inverse = 2.0 * NORM * np.block([[cx, -sx], [sx, cx]])
    x_forward = NORM * np.concatenate([cx.T, sx.T], axis=0)

    modes = np.zeros((N, N))
    modes[0] = 1.0 / math.sqrt(N)
    modes[1:64] = math.sqrt(2.0 / N) * np.cos(angle(np.arange(1, 64), every))
    modes[64] = np.cos(np.pi * every) / math.sqrt(N)
    modes[65:] = math.sqrt(2.0 / N) * np.sin(angle(np.arange(1, 64), every))
    return {
        "z_inverse": pieces(z_inverse),
        "z_forward": pieces(z_forward),
        "y_inverse": y_inverse,
        "y_forward": y_forward,
        "x_inverse": left(x_inverse),
        "x_forward": left(x_forward),
        "modes_left": left(modes),
        "modes_right": right(modes),
        "modes_t_left": left(modes.T),
        "modes_t_right": right(modes.T),
        "modes_t32": modes.T.astype(np.float32),
    }


TABLES = tables()


def split(value):
    high = value.astype(BF16)
    return high, (value - high.astype(F32)).astype(BF16)


def dot(a, b, contract=((1,), (0,))):
    return lax.dot_general(a, b, (contract, ((), ())), preferred_element_type=F32)


def dot3(a, b, contract=((1,), (0,))):
    return dot(a[0], b[0], contract) + (dot(a[1], b[0], contract) + dot(a[0], b[1], contract))


def both(value, axis):
    return jnp.concatenate(split(value), axis=axis)


def times_left(table, value):
    out = dot(table[...], both(value, 0) if value.dtype == F32 else value)
    half = out.shape[0] // 2
    return out[:half] + out[half:]


def times_right(value, table):
    out = dot(both(value, 1), table[...])
    return out[:, :N] + out[:, N:]


def call(body, out, *args, scratch=(), in_smem=(), in_hbm=(), out_smem=(), vmem=16, late=()):
    space = lambda i: pltpu.SMEM if i in in_smem else pltpu.HBM if i in in_hbm else pltpu.VMEM
    many = isinstance(out, (list, tuple))
    n = len(args)
    inner = (lambda *refs: body(*refs[:n], *refs[n + len(late) :])) if late else body
    return pl.pallas_call(
        inner,
        out_shape=out,
        in_specs=[
            *(pl.BlockSpec(memory_space=space(i)) for i in range(len(args))),
            *(pl.BlockSpec(memory_space=pltpu.HBM) for _ in late),
        ],
        out_specs=[
            pl.BlockSpec(memory_space=pltpu.SMEM if i in out_smem else pltpu.VMEM) for i in range(len(out))
        ]
        if many
        else pl.BlockSpec(memory_space=pltpu.VMEM),
        scratch_shapes=[
            *(pltpu.VMEM(args[i].shape, args[i].dtype) for i in in_hbm),
            *([pltpu.SemaphoreType.DMA((16,))] if in_hbm else []),
            *scratch,
        ],
        compiler_params=pltpu.CompilerParams(vmem_limit_bytes=int(vmem * MIB)),
    )(*args, *late)


def fetch(sources, targets, sems):
    copies = [pltpu.make_async_copy(s, t, sems.at[i]) for i, (s, t) in enumerate(zip(sources, targets))]
    for copy in copies:
        copy.start()
    return copies


def shape(*dims, dtype=F32):
    return jax.ShapeDtypeStruct(dims, dtype)


def sticks_to_z(resp_hbm, table_hbm, out, resp, table, sems):
    for copy in fetch((resp_hbm, table_hbm), (resp, table), sems):
        copy.wait()
    out[...] = dot3((table[0], table[1]), split(resp[...]), ((1,), (1,))).reshape(SLABS, 2 * PL, STK)


def q_mask_of(cells, lanes):
    q = lax.broadcasted_iota(jnp.int32, (16, 1), 0)
    return (cells[:, lanes] // 256 == q).astype(F32)


def pick_of(cells, lanes):
    column = lax.broadcasted_iota(jnp.int32, (256, 1), 0)
    return jnp.where(cells[:, lanes] % 256 == column, 1.0, 0.0).astype(BF16)


def planes_to_modes(
    recv, cells, y_hbm, x_hbm, occ_hbm, modes_hbm, modes_t_hbm,
    out, y_table, x_table, occ, modes, modes_t, sems, field, spectrum
):
    copies = fetch(
        (y_hbm, x_hbm, occ_hbm, modes_hbm, modes_t_hbm), (y_table, x_table, occ, modes, modes_t), sems
    )
    grid = jnp.zeros((512, 256), F32)
    for pair in range(SLABS // 2):
        rows = []
        for src in (2 * pair, 2 * pair + 1):
            mask = q_mask_of(cells, slice(src * STK, (src + 1) * STK))
            rows.append(
                jnp.concatenate(
                    [
                        (part.astype(F32)[:, None, :] * mask[None]).reshape(256, STK).astype(BF16)
                        for part in split(recv[src])
                    ],
                    axis=0,
                )
            )
        chosen = pick_of(cells, slice(2 * pair * STK, 2 * (pair + 1) * STK))
        grid += dot(jnp.concatenate(rows, axis=1), chosen, ((1,), (1,)))
    high, low = split(grid[:256] + grid[256:])
    first = lax.broadcasted_iota(jnp.int32, (1, N), 1) < HALF
    swap_halves = lambda v: jnp.concatenate([v[:, HALF:], v[:, :HALF]], axis=1)
    rows = []
    for j in range(4):
        h, l = (v[:, j // 2 * N : (j // 2 + 1) * N] for v in (high, low))
        if j % 2 == 0:
            l = swap_halves(l)
        else:
            h = swap_halves(h)
        rows.append(jnp.concatenate([jnp.where(first, h, l), h], axis=1))
    for copy in copies:
        copy.wait()
    mixed = dot(jnp.concatenate(rows, axis=0), y_table[...])
    for j in range(4):
        block = mixed[j * 256 : (j + 1) * 256]
        real = block[:N, :N] - block[N:, N:]
        imag = block[:N, N:] + block[N:, :N]
        for c, part in enumerate((real, imag)):
            for k, piece in enumerate(split(part)):
                at = slice(k * N + c * HALF + j * 16, k * N + c * HALF + (j + 1) * 16)
                for p in range(PL):
                    field[at, p * N : (p + 1) * N] = piece[p * 16 : (p + 1) * 16]
    for pair in range(PL // 2):
        lanes = slice(pair * 2 * N, (pair + 1) * 2 * N)
        values = times_left(x_table, field[:, lanes])
        for i in range(2):
            p = 2 * pair + i
            at = slice(i * N, (i + 1) * N)
            density = occ[0, p].astype(F32) * values[:N, at] + occ[1, p].astype(F32) * values[N:, at]
            spectrum[:, p * N : (p + 1) * N] = both(times_right(density, modes_t), 0)
    for pair in range(PL // 2):
        values = times_left(modes, spectrum[:, pair * 2 * N : (pair + 1) * 2 * N])
        for i in range(2):
            out[pl.ds(2 * pair + i, N, stride=PL), :] = values[:, i * N : (i + 1) * N]


TOP = 32767.0


def code(value):
    top = jnp.maximum(jnp.max(jnp.abs(value), axis=0, keepdims=True), 1e-30)
    log = jnp.ceil(jnp.log(top) * (4.0 / math.log(2.0)) + 0.01)
    codes = jnp.round(value * (TOP / jnp.exp2(log * 0.25)))
    return jnp.clip(codes, -TOP, TOP), log


def scale_of(log):
    return jnp.exp2(log * 0.25) * (1.0 / TOP)


def narrow(value):
    return value.astype(jnp.int32).astype(jnp.int16)


def widen(value):
    return value.astype(jnp.int32).astype(F32)


def sum_bands(recv, total_out, to_slabs):
    total = recv[0]
    for b in range(1, BANDS):
        total = total + recv[b]
    total_out[...] = total
    codes, log = code(total)
    tile = narrow(jnp.concatenate([codes, jnp.broadcast_to(log, (8, N))], axis=0))
    for i in range(SLABS):
        to_slabs[i] = tile


def solve_z(where, recv, density, modes, modes_t32, out):
    slabs = []
    for i in range(SLABS):
        tile = widen(recv[i])
        slabs.append(tile[: AX * PL] * scale_of(tile[AX * PL : AX * PL + 1]))
    columns = [
        jnp.concatenate([tile[a * PL : (a + 1) * PL] for tile in slabs], axis=0) for a in range(AX)
    ]
    spectrum = times_left(modes, jnp.concatenate(columns, axis=1))
    freq = lambda i: jnp.where(i <= N // 2, i, i - N // 2)
    fz = freq(lax.broadcasted_iota(jnp.int32, (N, N), 0))
    fy = freq(lax.broadcasted_iota(jnp.int32, (N, N), 1))
    plane_sq = fz * fz + fy * fy
    weighted = []
    for a in range(AX):
        fx = freq(where[0] * AX + a)
        square = (plane_sq + fx * fx).astype(F32)
        kernel = jnp.where(
            square > 0.0, (0.2 * N) ** 2 / (math.pi * jnp.maximum(square, 1.0)), 0.0
        )
        weighted.append(spectrum[:, a * N : (a + 1) * N] * kernel)
    own = modes_t32[pl.ds(pl.multiple_of(where[1] * PL, PL), PL), :]
    result = dot3(split(own), split(jnp.concatenate(weighted, axis=1)))
    result = jnp.concatenate([result[:, a * N : (a + 1) * N] for a in range(AX)], axis=0)
    values, logs = zip(code(result), code(density[...]))
    tile = []
    for a in range(AX):
        tile += [value[a * PL : (a + 1) * PL] for value in values]
    tile += [jnp.broadcast_to(log, (4, N)) for log in logs]
    tile = narrow(jnp.concatenate(tile, axis=0))
    for i in range(BANDS):
        out[i] = tile


def planes_to_sticks(
    recv, cells, modes_hbm, modes_t_hbm, xc_hbm, occ_hbm, x_hbm, y_hbm,
    out, modes, modes_t, xc, occ, x_table, y_table, sems, half, rows, grid
):
    copies = fetch(
        (modes_hbm, modes_t_hbm, xc_hbm, occ_hbm, x_hbm, y_hbm),
        (modes, modes_t, xc, occ, x_table, y_table),
        sems,
    )
    copies[0].wait()
    size = 2 * AX * PL
    for i in range(0, BANDS, 4):
        tiles = []
        for b in range(i, i + 4):
            tile = widen(recv[b])
            scales = [
                jnp.broadcast_to(scale_of(tile[size + 4 * k : size + 4 * k + 1]), (PL, N)) for k in range(2)
            ]
            tiles.append(tile[:size] * jnp.concatenate(scales * AX, axis=0))
        half[i * size : (i + 4) * size, :] = times_right(jnp.concatenate(tiles, axis=0), modes)
    for copy in copies[1:]:
        copy.wait()
    for p in range(PL):
        value = jnp.concatenate(
            [half[pl.ds(i * PL + p, N, stride=2 * PL), :] for i in range(2)], axis=1
        )
        value = times_left(modes_t, value)
        potential = value[:, :N] + xc[p] * value[:, N:]
        product = jnp.concatenate(
            [potential * occ[0, p].astype(F32), potential * occ[1, p].astype(F32)], axis=1
        )
        mixed = times_left(x_table, product)
        real = mixed[:HALF, :N] + mixed[HALF:, N:]
        imag = mixed[:HALF, N:] - mixed[HALF:, :N]
        for c, part in enumerate((real, imag)):
            for k, piece in enumerate(split(part)):
                for j in range(4):
                    at = slice(k * 512 + j * N + p * 16, k * 512 + j * N + (p + 1) * 16)
                    rows[at, c * N : (c + 1) * N] = piece[j * 16 : (j + 1) * 16]
    mixed = dot(rows[:512], y_table[...])
    mixed = mixed[:, :N] + mixed[:, N:] + dot(rows[512:], y_table[:, :N])
    by_j = [mixed[j * N : (j + 1) * N] for j in range(4)]
    first = lax.broadcasted_iota(jnp.int32, (1, N), 1) < HALF
    for h in range(2):
        even, odd = by_j[2 * h], by_j[2 * h + 1]
        grid[h, :N, :] = jnp.where(first, even, pltpu.roll(odd, HALF, 1))
        grid[h, N:, :] = jnp.where(first, pltpu.roll(even, HALF, 1), odd)
    values = both(
        jnp.concatenate(
            [
                jnp.concatenate([grid[h, pl.ds(q, 16, stride=16), :] for h in range(2)], axis=1)
                for q in range(16)
            ],
            axis=0,
        ),
        0,
    )
    for pair in range(SLABS // 2):
        lanes = slice(2 * pair * STK, 2 * (pair + 1) * STK)
        mask = q_mask_of(cells, lanes)
        chosen = dot(values, pick_of(cells, lanes))
        total = jnp.zeros((2 * PL, 2 * STK), F32)
        for q in range(16):
            at = slice(q * 16, (q + 1) * 16)
            total = total + (chosen[:256][at] + chosen[256:][at]) * mask[q : q + 1]
        out[2 * pair] = total[:, :STK]
        out[2 * pair + 1] = total[:, STK:]


CHUNK = 8


def orbitals(hbm, held, sems):
    parts = BANDS // 2 // CHUNK
    copies = [
        pltpu.make_async_copy(
            ref.at[pl.ds(i * CHUNK, CHUNK)], to.at[pl.ds(i * CHUNK, CHUNK)], sems.at[h * parts + i]
        )
        for h, (ref, to) in enumerate(zip(hbm, held))
        for i in range(parts)
    ]
    for copy in copies:
        copy.start()

    def at(k):
        if k % CHUNK == 0:
            copies[k // CHUNK].wait()
        return held[k * 2 // BANDS][k % (BANDS // 2)].astype(F32)

    return at


def band_of(place, me):
    return (place % 4 * 2 + place // 4 % 4 * 8 + place // 16) ^ me


def overlap_rows(at, where, probes, sums):
    pairs = [
        (x, jnp.concatenate([x[:, N:], -x[:, :N]], axis=1)) for x in probes
    ]
    for place in range(BANDS):
        orbital = at(place)
        w = band_of(place, where[0])
        for i, pair in enumerate(pairs):
            for c, probe in enumerate(pair):
                line = jnp.sum(orbital * probe, axis=0, keepdims=True)
                sums[i, pl.ds(c * BANDS + w, 1), :] = line[:, :N] + line[:, N:]
    rows = []
    for i in range(len(probes)):
        sums[i, 2 * BANDS :, :] = jnp.zeros((N - 2 * BANDS, N), F32)
        rows.append(jnp.sum(sums[i].T, axis=0, keepdims=True))
    return rows


def total_sum(value):
    return jnp.sum(jnp.sum(value, axis=0, keepdims=True), axis=1, keepdims=True)


def lane():
    return lax.broadcasted_iota(jnp.int32, (1, N), 1)


def with_lanes(row, first, values):
    for i, value in enumerate(values):
        row = jnp.where(lane() == first + i, value, row)
    return row


def lower(row):
    return jnp.where(lane() < 2 * BANDS, row, 0.0)


def fixed_overlaps(where, low, high, resp, prev, occ, out, low_held, high_held, sems, sums):
    at = orbitals((low, high), (low_held, high_held), sems)
    rows = overlap_rows(at, where, [resp[...], prev[...], occ[...].astype(F32)], sums)
    for i, row in enumerate(rows):
        out[i : i + 1, :] = row
    out[3:, :] = jnp.zeros((5, N), F32)


def apply_and_overlap(
    recv, table, where, scalars, resp, prev, fixed, low, high,
    applied_out, part_out, low_held, high_held, sems, sums
):
    at = orbitals((low, high), (low_held, high_held), sems)
    values = recv[...].reshape(2 * N, STK).T
    applied = dot3(split(values), (table[0], table[1]))
    applied_out[...] = applied
    margin, along = overlap_rows(at, where, [applied.astype(BF16).astype(F32), applied], sums)
    response = resp[...]
    first = scalars[0] * response + applied
    rest = first - scalars[1] * prev[...]
    norm = total_sum(response * response)
    slope = total_sum(response * rest) / jnp.where(norm > 0.0, norm, 1.0)
    left = rest - slope * response
    with_resp, with_prev, with_occ = fixed[0:1, :], fixed[1:2, :], fixed[2:3, :]
    along = along + (scalars[0] - slope) * with_resp - scalars[1] * with_prev
    row = jnp.concatenate(
        [
            margin + pltpu.roll(with_occ, 2 * BANDS, 1),
            along,
            with_lanes(
                with_resp,
                2 * BANDS,
                [norm, total_sum(response * first), slope, total_sum(left * left)],
            ),
        ],
        axis=1,
    )
    for i in range(SLABS):
        part_out[i] = row


def join_slabs(recv, margin_out, part_out):
    rows = [jnp.concatenate([recv[i][:, j * N : (j + 1) * N] for i in range(SLABS)], axis=0) for j in range(3)]
    add = lambda v: jnp.sum(v, axis=0, keepdims=True)
    norms, firsts, slopes, lefts = (rows[2][:, 2 * BANDS + i : 2 * BANDS + i + 1] for i in range(4))
    norm = add(norms)
    slope = add(norms * slopes) / jnp.where(norm > 0.0, norm, 1.0)
    spread_ = slopes - slope
    left = add(lefts + norms * spread_ * spread_)
    head = add(rows[0])
    weights = lower(head.astype(BF16).astype(F32))
    with_left = add(rows[1] + spread_ * rows[2])
    with_resp = add(rows[2])
    inner = lambda x: jnp.sum(weights * lower(x), axis=1, keepdims=True)
    removed_resp = inner(with_resp)
    margin_out[...] = head
    row = jnp.concatenate(
        [
            jnp.where(lane() < 2 * BANDS, weights, head),
            with_lanes(
                jnp.zeros((1, N), F32),
                0,
                [norm, add(firsts) - removed_resp, slope, removed_resp, left - 2.0 * inner(with_left)],
            ),
        ],
        axis=1,
    )
    for i in range(BANDS):
        part_out[i] = row


def remove(margin, where, scalars, resp, prev, applied, low, high, rest_out, low_held, high_held, sems):
    at = orbitals((low, high), (low_held, high_held), sems)
    weights = margin[...].astype(BF16)
    i = lax.broadcasted_iota(jnp.int32, (1, N), 1)
    band = i // BANDS * BANDS + band_of(i % BANDS, where[0])
    to_place = lax.broadcasted_iota(jnp.int32, (N, 1), 0) == band
    weights = dot(weights, jnp.where(to_place, 1.0, 0.0).astype(BF16))
    plain = jnp.zeros((STK, 2 * N), F32)
    turned = jnp.zeros((STK, 2 * N), F32)
    for w in range(BANDS):
        orbital = at(w)
        plain = plain + weights[:, w : w + 1] * orbital
        turned = turned + weights[:, BANDS + w : BANDS + w + 1] * orbital
    removed = plain + jnp.concatenate([-turned[:, N:], turned[:, :N]], axis=1)
    rest_out[...] = scalars[0] * resp[...] + applied[...] - removed - scalars[1] * prev[...]


def finish(recv, resp, rest, next_out, coef_out):
    rows = [jnp.concatenate([recv[i][:, j * N : (j + 1) * N] for i in range(BANDS)], axis=0) for j in range(2)]
    norms, alongs, slopes, removed_resp, lefts = (rows[1][:, i : i + 1] for i in range(5))
    add = lambda v: jnp.sum(v, axis=0, keepdims=True)
    real, imag, same, cross = (rows[0][:, i * BANDS : (i + 1) * BANDS] for i in range(4))
    times = lambda a, b: lax.dot_general(
        a, b, (((1,), (1,)), ((), ())), precision=lax.Precision.HIGHEST, preferred_element_type=F32
    )
    square = total_sum(real * (times(real, same) + 2.0 * times(imag, cross)) + imag * times(imag, same))
    alpha = add(alongs) / add(norms)
    gap = slopes - alpha
    resid_sq = add(lefts + gap * (gap * norms - 2.0 * removed_resp)) + square
    beta = jnp.sqrt(jnp.maximum(resid_sq, 0.0) / float(2 * BANDS * STICKS * N) + 1e-06)
    next_out[...] = (rest[...] - alpha * resp[...]) / beta
    coef_out[0] = alpha[0, 0]
    coef_out[1] = beta[0, 0]


def swap(value, axis):
    return lax.all_to_all(value, axis, 0, 0, tiled=True)


def across(blocks, bit):
    return lax.ppermute(blocks, "band", [(i, i ^ bit) for i in range(BANDS)])


def after(value, other):
    return lax.optimization_barrier((value, other))


def per_device(
    response, previous, earlier_beta, band_gap, occupied, occupied_real, xc_kernel, stick_map
):
    t = {name: jnp.asarray(value) for name, value in TABLES.items()}
    where = jnp.stack([lax.axis_index("band"), lax.axis_index("slab")]).astype(jnp.int32)
    resp = response.reshape(STK, 2 * N)
    prev = previous.reshape(STK, 2 * N)

    occ_planes = occupied_real.reshape(2, PL, N, N)
    field = call(sticks_to_z, shape(SLABS, 2 * PL, STK), resp, t["z_inverse"], in_hbm=(0, 1), vmem=60)
    stick_map, _ = after(stick_map, field)
    gx = stick_map // N % HALF
    cells = (gx // 4 * 256 + gx % 4 * HALF + stick_map % HALF).reshape(1, STICKS)
    own, cells = after(occupied.reshape(1, STK, 2 * N), cells)
    x1, x3 = across(own, 2), across(own, 6)
    field = swap(field, "slab")
    bf_scratch = lambda *dims: pltpu.VMEM(dims, BF16)
    partial = call(
        planes_to_modes,
        shape(N * PL, N),
        field, cells, t["y_inverse"], t["x_inverse"], occ_planes, t["modes_left"], t["modes_t_right"],
        in_hbm=(2, 3, 4, 5, 6),
        scratch=[bf_scratch(2 * N, PL * N), bf_scratch(2 * N, PL * N)],
    )
    (x1, x3), partial = after((x1, x3), partial)
    partial = swap(partial.reshape(BANDS, AX * PL, N), "band")
    x2 = across(own, 4)
    own_modes, total = call(
        sum_bands,
        [shape(AX * PL, N), shape(SLABS, AX * PL + 8, N, dtype=jnp.int16)],
        partial,
    )
    x2, total = after(x2, total)
    row = jnp.concatenate([own, x1, x2, x3], axis=0)
    y1, y2, y3 = across(row, 8), across(row, 16), across(row, 24)
    columns = swap(total, "slab")
    hartree = call(
        solve_z, shape(BANDS, 2 * AX * PL + 8, N, dtype=jnp.int16), where, columns, own_modes, t["modes_left"], t["modes_t32"],
        in_smem=(0,),
    )
    (row, y1, y2, y3), _ = after((row, y1, y2, y3), hartree)
    xc_planes, _ = after(xc_kernel, hartree)
    xc_planes = xc_planes.reshape(PL, N, N)
    hartree = swap(hartree, "band")
    chosen = call(
        planes_to_sticks,
        shape(SLABS, 2 * PL, STK),
        hartree, cells, t["modes_right"], t["modes_t_left"],
        xc_planes, occ_planes, t["x_forward"], t["y_forward"],
        in_hbm=(2, 3, 4, 5, 6, 7),
        vmem=59.8,
        scratch=[pltpu.VMEM((2 * N * PL, N), F32), bf_scratch(8 * N, 2 * N), pltpu.VMEM((2, 2 * N, N), F32)],
    )
    low = jnp.concatenate([row, y1, y2, y3], axis=0)
    high = across(low, 1)
    gathered = swap(chosen, "slab")
    fixed = call(
        fixed_overlaps,
        shape(8, N),
        where, low, high, resp, prev, occupied.reshape(STK, 2 * N),
        in_smem=(0,),
        in_hbm=(1, 2),
        scratch=[pltpu.VMEM((3, N, N), F32)],
    )
    scalars = jnp.stack([band_gap[0], earlier_beta[0]])
    applied, parts = call(
        apply_and_overlap,
        [shape(STK, 2 * N), shape(SLABS, 1, 3 * N)],
        gathered, t["z_forward"], where, scalars, resp, prev, fixed, low, high,
        in_smem=(2, 3),
        in_hbm=(7, 8),
        scratch=[pltpu.VMEM((2, N, N), F32)],
    )
    margin, parts = call(
        join_slabs, [shape(1, N), shape(BANDS, 1, 2 * N)], swap(parts, "slab")
    )
    rest = call(
        remove,
        shape(STK, 2 * N),
        margin, where, scalars, resp, prev, applied, low, high,
        in_smem=(1, 2),
        in_hbm=(6, 7),
    )
    next_vector, coefficients = call(
        finish,
        [shape(STK, 2 * N), shape(2)],
        swap(parts, "band"), resp, rest,
        out_smem=(1,),
    )
    return (
        next_vector.reshape(1, STK, 2 * N),
        margin[0, : 2 * BANDS].reshape(2, BANDS, 1),
        coefficients,
    )


def solution(mesh):
    placed = (
        P("band", "slab", None),
        P("band", "slab", None),
        P(),
        P("band"),
        P("band", "slab", None),
        P("band", None, "slab", None),
        P("slab", None),
        P(),
    )
    return jax.shard_map(
        per_device,
        mesh=mesh,
        in_specs=placed,
        out_specs=(P("band", "slab", None), P(None, None, "band"), P()),
        check_vma=False,
    )
```
